512 devices in a mesh: dp: 64 (over x, y, z_hi), expert: 8 (over z_lo, core).
Axes of the slice: x: 4, y: 8, z: 8 (z_hi: 2, z_lo: 4; z = z_hi * 4 + z_lo), core: 2. Of those that a mesh axis runs over, the one named last changes fastest.
Arguments:
- attn_out: bfloat16 [8192, 6144], P('dp', 'expert'), may hold values from -6 to 6
- out_cols: bfloat16 [8192, 1024], P('dp', 'expert'), may hold values from -1.25 to 1.25
- error_in: bfloat16 [64, 6144, 1024], P('dp', None, 'expert'), may hold values from -6 to 6
- power_q: float32 [1024, 64], P('expert'), may hold values from -0.1875 to 0.1875
- tokens: bfloat16 [65536, 6144], P(('dp', 'expert')), may hold values from -24 to 24
- routes: int32 [65536, 2], P(('dp', 'expert')), may hold values from 0 to 7, all different within a row; in each aligned block of 128 rows (0 to 127, 128 to 255, ...) at most 64 rows name the same one
- route_logits: float32 [65536, 2], P(('dp', 'expert')), may hold values from -6 to 6
- pair_score: float32 [65536, 2], P(('dp', 'expert')), may hold values from -0.5 to 0.5
Outputs:
- approx: bfloat16 [6144, 1024], P('dp', 'expert')
- q_new: float32 [1024, 64], P('expert')
- error_out: bfloat16 [64, 6144, 1024], P('dp', None, 'expert')
- expert_grad: float32 [8, 6144], P('expert', 'dp')
The draws below stay inside these ranges and needn't reach their ends.
Inputs may be any that keep to these rules, and one draw needn't show every extreme that they name: `routes`: within the 128 rows of one device, no expert is named by more than 64 pairs, a bound that some block reaches; the two experts of a token differ.
All inputs are finite; a program needn't handle non-finite values.
Results may differ from the reference program's by a relative error of at most 0.0027.
Values may be sent and summed in bfloat16 or wider, within the bound.
No kernel may reach another device: no remote copies, remote signals or barrier semaphores. Data moves between devices by JAX's collectives and lax.ppermute only.
A program may use at most 128 MiB of HBM per device.

```python
import math
import jax
import jax.numpy as jnp
import numpy as np
from jax import lax

D = 6144
RANK = 64
TOK_ATT = 128
TOK_DEV = 128
EXPERTS = 8
CAP = 64
COLS = 1024
ATT_ALL = 8192
TOKENS = 65536
N_DP = 64
N_EXPERT = 8


def strengthened(values, own_key, source, target, shards_of, factor):
    def block_of(position):
        return (jnp.arange(values.shape[position]) // (values.shape[position] // shards_of)).reshape((-1,) + (1,) * (values.ndim - 1 - position))

    near = jax.random.permutation(own_key, shards_of)[block_of(target)]
    second = (block_of(target) + shards_of // 2) % shards_of
    return jnp.where((block_of(source) == near) | (block_of(source) == second), factor * values, values)


def level_of(own_key, shape, cuts, smallest, largest):
    gain, own = 1.0, jax.random.fold_in(own_key, 6)
    for axis_at, blocks in cuts:
        heights = jnp.exp(jax.random.uniform(jax.random.fold_in(own, axis_at), (blocks,), jnp.float32, smallest / len(cuts), largest / len(cuts)))
        gain = gain * jnp.repeat(heights, shape[axis_at] // blocks).reshape([-1 if axis == axis_at else 1 for axis in range(len(shape))])
    return gain


def deal_out(key, own, number, rows, count, top, limit, slope):
    ranking = jax.random.permutation(key, count)
    crowded, usual = shares(count, rows * top, limit, slope, True), shares(count, rows * top, limit, slope, False)
    places = jnp.arange(count)

    def named(tallies, offset_by):
        used = int((tallies > 0).sum())
        fixed = max(1, used // 4)
        passed = fixed + (places - fixed + offset_by * (used - fixed)) % max(1, count - fixed)
        return jnp.zeros((count,), jnp.int32).at[ranking[jnp.where(places < fixed, places, passed)]].set(jnp.asarray(tallies, jnp.int32))

    tallies = jnp.where(number % 4 == 0, named(crowded, number // 4), named(usual, number - number // 4 - 1))
    mixed = jax.random.permutation(jax.random.fold_in(own, 3), count)
    donor, taker = mixed[0:count // 2 * 2:2], mixed[1:count // 2 * 2:2]
    slack = jnp.minimum(tallies[donor] - 1, limit - tallies[taker]) // 2
    slack = jnp.where((donor == ranking[0]) | (taker == ranking[0]) | (tallies[taker] == 0), 0, jnp.maximum(slack, 0))
    passed = jax.random.randint(jax.random.fold_in(own, 4), (count // 2,), 0, 1 << 20) % (slack + 1)
    tallies = tallies.at[donor].add(-passed).at[taker].add(passed)
    members = jnp.searchsorted(jnp.cumsum(tallies), jnp.arange(rows * top), side="right").astype(jnp.int32)
    table = members.reshape(top, rows).T
    table = table[jax.random.permutation(jax.random.fold_in(own, 1), rows)]
    offset_by = jax.random.randint(jax.random.fold_in(own, 2), (rows, 1), 0, top)
    return jnp.take_along_axis(table, (jnp.arange(top)[None, :] + offset_by) % top, axis=1)


def shares(number_of, total, bound, skew, full):
    weights = [(1 << 20) // math.isqrt(rank ** skew) + 1 for rank in range(1, number_of + 1)]
    largest = bound if full else min(bound, max(-(-total // number_of), total * weights[0] // sum(weights)))
    least = 1 if total - largest >= number_of - 1 else 0
    holding, spare = [largest] + [least] * (number_of - 1), total - largest - least * (number_of - 1)
    while spare > 0:
        free = [i for i in range(1, number_of) if holding[i] < largest] or [i for i in range(1, number_of) if holding[i] < bound]
        whole, budget = sum([weights[i] for i in free]), spare
        for i in free:
            more = min(bound - holding[i], max(1, budget * weights[i] // whole), spare)
            holding[i] = holding[i] + more
            spare = spare - more
    return np.array(holding)


def normal_values(own_key, dims, scale, most, shards=(), kind=jnp.bfloat16):
    entries = scale * jax.random.normal(own_key, dims, jnp.float32)
    if shards:
        entries = entries * level_of(own_key, dims, shards, -0.22, 0.18)
    return jnp.clip(entries, -most, most).astype(kind)


def heavy_noise(own_key, shape, width, bound, shards, heavy, kind=jnp.bfloat16):
    array = width * jax.random.normal(own_key, shape, jnp.float32)
    if shards:
        array = array * level_of(own_key, shape, shards, -0.22, 0.18)
    return jnp.clip(strengthened(array, jax.random.fold_in(own_key, 3), *heavy), -bound, bound).astype(kind)


def setup_inputs(seed: int = 0) -> dict:
    keys = jax.random.split(jax.random.key(seed), 9)
    attn_out = normal_values(keys[0], (ATT_ALL, D), 1.0, 6.0, ((0, 64), (1, 8)))
    out_cols = normal_values(keys[1], (ATT_ALL, COLS), (TOK_ATT ** -0.5), 1.25, ((0, 64), (1, 8)))
    error_in = normal_values(keys[2], (N_DP, D, COLS), 0.5, 6.0, ((0, 64), (2, 8)))
    power_q = normal_values(keys[3], (COLS, RANK), COLS ** -0.5, 0.1875, ((0, 8),), jnp.float32)
    tokens = heavy_noise(keys[4], (TOKENS, D), 1.0, 24.0, ((0, 512),), (0, 1, 512, 6.0))
    routes_keys = jax.random.split(jax.random.fold_in(keys[5], 1), TOKENS // TOK_DEV)
    routes_turns = jax.random.permutation(jax.random.fold_in(keys[5], 3), TOKENS // TOK_DEV)
    routes = jax.vmap(lambda own, number: deal_out(jax.random.fold_in(keys[5], 2), own, number, TOK_DEV, EXPERTS, 2, CAP, 2))(routes_keys, routes_turns).reshape((TOKENS, 2))
    route_logits = normal_values(keys[6], (TOKENS, 2), 1.5, 6.0, ((0, 512),), jnp.float32)
    pair_score = normal_values(keys[7], (TOKENS, 2), (4.0 * (2 * TOKENS // EXPERTS) ** -0.5), 0.5, ((0, 512),), jnp.float32)
    return dict(attn_out=attn_out, out_cols=out_cols, error_in=error_in, power_q=power_q, tokens=tokens, routes=routes, route_logits=route_logits, pair_score=pair_score)


HIGH = lax.Precision.HIGHEST

def orthonormal(whole):
    gram = jnp.dot(whole.T, whole, precision=HIGH)
    factor = jnp.linalg.cholesky(gram)
    return lax.linalg.triangular_solve(factor, whole, left_side=False, lower=True, transpose_a=True)

def expert_rows_of(route_logits, pair_score):
    first = 1.0 / (1.0 + jnp.exp(route_logits[:, 1] - route_logits[:, 0]))
    product = first * (1.0 - first) * (pair_score[:, 0] - pair_score[:, 1])
    return jnp.stack([product, -product], axis=-1).astype(jnp.bfloat16)

def reference(attn_out, out_cols, error_in, power_q, tokens, routes, route_logits, pair_score):
    attn_rows = attn_out.reshape(N_DP, TOK_ATT, D)
    col_rows = out_cols.reshape(N_DP, TOK_ATT, COLS)

    def grad_of(index):
        local = lax.dot_general(attn_rows[index].astype(jnp.float32), col_rows[index].astype(jnp.float32), (((0,), (0,)), ((), ())), preferred_element_type=jnp.float32)
        return local + error_in[index].astype(jnp.float32)

    def add_p(total, index):
        return (total + jnp.dot(grad_of(index), power_q, precision=HIGH), None)
    indices = jnp.arange(N_DP, dtype=jnp.int32)
    p_total, unused = lax.scan(add_p, jnp.zeros((D, RANK), jnp.float32), indices)
    basis = orthonormal(p_total / N_DP)

    def add_q(total, index):
        return (total + jnp.dot(grad_of(index).T, basis, precision=HIGH), None)
    q_total, unused = lax.scan(add_q, jnp.zeros((COLS, RANK), jnp.float32), indices)
    q_new = q_total / N_DP
    approx_full = jnp.dot(basis, q_new.T, precision=HIGH)
    error_out = lax.map(lambda index: (grad_of(index) - approx_full).astype(jnp.bfloat16), indices)
    rows_grad = expert_rows_of(route_logits, pair_score)
    block = TOK_DEV * N_EXPERT
    tok_blocks = tokens.reshape(N_DP, block, D)
    grad_blocks = rows_grad.reshape(N_DP, block, 2)
    route_blocks = routes.reshape(N_DP, block, 2)
    labels = jnp.arange(EXPERTS, dtype=jnp.int32)

    def add_expert(total, index):
        onehot = (route_blocks[index][:, :, None] == labels[None, None, :]).astype(jnp.float32)
        spread = jnp.sum(onehot * grad_blocks[index].astype(jnp.float32)[:, :, None], axis=1)
        term = jnp.dot(spread.T, tok_blocks[index].astype(jnp.float32), precision=HIGH)
        return (total + term, None)
    expert_grad, unused = lax.scan(add_expert, jnp.zeros((EXPERTS, D), jnp.float32), indices)
    return (approx_full.astype(jnp.bfloat16), q_new, error_out, expert_grad)
```

```python
import jax
import jax.numpy as jnp
from jax import lax
from jax.sharding import Mesh, PartitionSpec as P

HIGH = lax.Precision.HIGHEST
F16 = jnp.float16
RANK = 64
DP = ("x", "y", "h")
EXPERT = ("l", "c")
FLAT = ("x", "y", "h", "l")


def exchange(values, axes):
    return lax.all_to_all(values, axes, split_axis=0, concat_axis=0, tiled=True)


def swap_cores(values):
    return lax.ppermute(values, "c", [(0, 1), (1, 0)])


def scale_of(bound):
    safe = jnp.maximum(bound, 1e-30)
    return jnp.clip(jnp.ceil(jnp.log2(safe)) - 14.0, -110.0, 110.0)


def coded(values, exponent):
    small = (values * jnp.exp2(-exponent)).astype(F16)
    row = jnp.broadcast_to(exponent, small.shape[:-2] + (1, 128)).astype(F16)
    return jnp.concatenate([small, row], axis=-2)


def decoded(received):
    scale = jnp.exp2(received[..., 6:7, 0:1].astype(jnp.float32))
    return received[..., :6, :].astype(jnp.float32) * scale


def expert_partial(tokens, routes, route_logits, pair_score):
    first = 1.0 / (1.0 + jnp.exp(route_logits[:, 1] - route_logits[:, 0]))
    product = first * (1.0 - first) * (pair_score[:, 0] - pair_score[:, 1])
    rows = product.astype(jnp.bfloat16)[:, None]
    labels = jnp.arange(8, dtype=jnp.int32)[None, :]
    zero = jnp.zeros((), jnp.bfloat16)
    spread = jnp.where(routes[:, :1] == labels, rows, zero) + jnp.where(
        routes[:, 1:] == labels, -rows, zero
    )
    return lax.dot_general(
        spread, tokens, (((0,), (0,)), ((), ())), preferred_element_type=jnp.float32
    )


def local(attn_out, out_cols, error_in, power_q, tokens, routes, route_logits, pair_score):
    error = error_in[0]
    core = lax.axis_index("c")
    group = lax.axis_index("l") * 2 + core
    gathered = lax.all_gather(attn_out, EXPERT, axis=1, tiled=True)

    part = lax.dot_general(
        power_q, out_cols.astype(jnp.float32), (((0,), (1,)), ((), ())), precision=HIGH
    )
    cq = jnp.sum(exchange(jnp.broadcast_to(part, (8,) + part.shape), EXPERT), axis=0)

    from_error = lax.dot_general(
        power_q, error.astype(jnp.float32), (((0,), (1,)), ((), ())), precision=HIGH
    )
    from_attn = jnp.dot(cq, attn_out.astype(jnp.float32), precision=HIGH)
    bound = 256.0 * (
        jnp.max(jnp.abs(error)).astype(jnp.float32) * jnp.max(jnp.abs(power_q))
        + jnp.max(jnp.abs(attn_out)).astype(jnp.float32) * jnp.max(jnp.abs(cq))
    )
    here = (jnp.arange(8) == group)[None, :, None]
    share = from_error.reshape(RANK, 8, 768) + jnp.where(here, from_attn[:, None, :], 0.0)
    share = share.reshape(RANK, 4, 2, 768)
    kept = lax.dynamic_index_in_dim(share, core, 2, keepdims=False)
    given = lax.dynamic_index_in_dim(share, 1 - core, 2, keepdims=False)
    bounds = jnp.broadcast_to(bound, (1, 128))
    half = kept + swap_cores(given)
    exponent = scale_of(bound + swap_cores(bounds)[0, 0])
    summed = jnp.sum(
        decoded(exchange(coded(half.reshape(256, 6, 128), exponent), FLAT)), axis=0
    )

    piece = coded(summed, scale_of(jnp.max(jnp.abs(summed))))
    mine = exchange(jnp.broadcast_to(piece, (256, 7, 128)), FLAT)
    other = swap_cores(mine)
    first = decoded(jnp.where(core == 0, mine, other)).reshape(RANK, 4, 768)
    second = decoded(jnp.where(core == 0, other, mine)).reshape(RANK, 4, 768)
    p_t = jnp.stack([first, second], axis=2).reshape(RANK, 6144)

    grad_w = lax.dot_general(
        gathered, out_cols, (((0,), (0,)), ((), ())), preferred_element_type=jnp.float32
    ) + error.astype(jnp.float32)

    expert_sum = lax.psum_scatter(
        expert_partial(tokens, routes, route_logits, pair_score),
        EXPERT,
        scatter_dimension=0,
        tiled=True,
    )
    by_y = expert_sum.reshape(4, 8, 2, 96).transpose(1, 0, 2, 3).reshape(8, 6, 128)

    raw = jnp.dot(p_t, grad_w, precision=HIGH)
    over_y = jnp.sum(
        exchange(jnp.concatenate([jnp.broadcast_to(raw, (8, RANK, 128)), by_y], axis=1), "y"),
        axis=0,
    )
    rest = jnp.pad(over_y[RANK:].reshape(8, 1, 96), ((0, 0), (0, 0), (0, 32)))
    over_all = jnp.sum(
        exchange(
            jnp.concatenate([jnp.broadcast_to(over_y[:RANK], (8, RANK, 128)), rest], axis=1),
            ("x", "h"),
        ),
        axis=0,
    )
    expert_grad = over_all[RANK:, :96]

    gram = lax.dot_general(p_t, p_t, (((1,), (1,)), ((), ())), precision=HIGH)
    factor = jnp.linalg.cholesky(gram, symmetrize_input=False)
    inverse = lax.linalg.triangular_solve(
        factor, jnp.eye(RANK, dtype=jnp.float32), left_side=True, lower=True
    )
    q_t = jnp.dot(inverse, over_all[:RANK], precision=HIGH) / 64.0
    weights = jnp.dot(inverse.T, q_t, precision=HIGH)
    approx_full = lax.dot_general(p_t, weights, (((0,), (0,)), ((), ())), precision=HIGH)
    error_out = (grad_w - approx_full).astype(jnp.bfloat16)[None]
    index = (lax.axis_index("x") * 8 + lax.axis_index("y")) * 2 + lax.axis_index("h")
    approx = lax.dynamic_slice_in_dim(approx_full, index * 96, 96, 0).astype(jnp.bfloat16)
    return approx, q_t.T, error_out, expert_grad


def solution(mesh):
    fine = Mesh(mesh.devices.reshape(4, 8, 2, 4, 2), DP + EXPERT)
    everyone = P(DP + EXPERT, None)
    return jax.shard_map(
        local,
        mesh=fine,
        in_specs=(
            P(DP, EXPERT),
            P(DP, EXPERT),
            P(DP, None, EXPERT),
            P(EXPERT, None),
            everyone,
            everyone,
            everyone,
            everyone,
        ),
        out_specs=(P(DP, EXPERT), P(EXPERT, None), P(DP, None, EXPERT), P(EXPERT, DP)),
        check_vma=False,
    )
```

```python
import functools

import jax
import jax.numpy as jnp
from jax import lax
from jax.experimental import pallas as pl
from jax.experimental.pallas import tpu as pltpu
from jax.sharding import Mesh, PartitionSpec as P

HIGH = lax.Precision.HIGHEST
F32, BF16, I16 = jnp.float32, jnp.bfloat16, jnp.int16
RANK = 64
WIDTH = 6144
BLOCK = 768
DP = ("x", "y", "h")
EXPERT = ("l", "c")
FLAT = ("x", "y", "h", "l")
LIMIT = 32 * 1024 * 1024
TOP = 32000.0
STEP = 64.0
USED = 96

VMEM = pl.BlockSpec(memory_space=pltpu.VMEM)
SMEM = pl.BlockSpec(memory_space=pltpu.SMEM)


def exchange(values, axes):
    return lax.all_to_all(values, axes, split_axis=0, concat_axis=0, tiled=True)


def swap_cores(values):
    return lax.ppermute(values, "c", [(0, 1), (1, 0)])


def three(values):
    high = values.astype(BF16)
    rest = values - high.astype(F32)
    middle = rest.astype(BF16)
    low = (rest - middle.astype(F32)).astype(BF16)
    return jnp.concatenate([high, middle, low], axis=0)


def folded(stacked):
    return stacked[:RANK] + stacked[RANK : 2 * RANK] + stacked[2 * RANK :]


def scale_of(largest):
    exponent = jnp.ceil(STEP * jnp.log2(jnp.maximum(largest, 1e-30))) + 1.0
    return exponent, jnp.exp2(exponent * (-1.0 / STEP)) * TOP


def lanes_of(shape):
    return lax.broadcasted_iota(jnp.int32, shape, 1)


def coded(values):
    return jnp.round(values).astype(jnp.int32).astype(I16)


def decoded(tile):
    wide = tile.astype(jnp.int32).astype(F32)
    return wide * (jnp.exp2(wide[:, 127:128] * (1.0 / STEP)) * (1.0 / TOP))


def error_kernel(block_ref, q_ref, error_ref, out_ref):
    del block_ref
    out_ref[...] = folded(
        lax.dot_general(
            three(q_ref[...]), error_ref[...], (((1,), (1,)), ((), ())), preferred_element_type=F32
        )
    )


def error_share(power_t, error, core):
    return pl.pallas_call(
        error_kernel,
        grid_spec=pltpu.PrefetchScalarGridSpec(
            num_scalar_prefetch=1,
            grid=(4,),
            in_specs=[
                pl.BlockSpec((RANK, 128), lambda i, core: (0, 0)),
                pl.BlockSpec((BLOCK, 128), lambda i, core: (2 * i + core[0], 0)),
            ],
            out_specs=pl.BlockSpec((RANK, BLOCK), lambda i, core: (0, i)),
        ),
        out_shape=jax.ShapeDtypeStruct((RANK, 4 * BLOCK), F32),
        compiler_params=pltpu.CompilerParams(vmem_limit_bytes=LIMIT),
        cost_estimate=pl.CostEstimate(
            flops=2 * 192 * 128 * 3072, bytes_accessed=3072 * 512, transcendentals=0
        ),
    )(core.reshape(1), power_t, error)


def share_kernel(place_ref, cq_ref, attn_ref, kept_ref, came_ref, out_ref, half_ref):
    cq = jnp.sum(cq_ref[:, :RANK, :], axis=0)
    from_attn = folded(jnp.dot(three(cq), attn_ref[...], preferred_element_type=F32))
    half_ref[...] = kept_ref[...] + came_ref[...]
    here = pl.ds(pl.multiple_of(place_ref[0] * BLOCK, BLOCK), BLOCK)
    half_ref[:, here] += from_attn
    lane = lanes_of((8, 128))
    for band in range(8):
        rows = slice(band * 8, band * 8 + 8)
        tiles = [half_ref[rows, t * 128 : t * 128 + 128] for t in range(24)]
        largest = functools.reduce(jnp.maximum, [jnp.abs(t) for t in tiles])
        exponent, factor = scale_of(jnp.max(largest, axis=1, keepdims=True))
        exponent = jnp.broadcast_to(exponent, (8, 128))
        factor = jnp.broadcast_to(factor, (8, 128))
        for group in range(8):
            a, b, c = (t * factor for t in tiles[group * 3 : group * 3 + 3])
            tail = jnp.where(
                lane < 32,
                pltpu.roll(a, 32, 1),
                jnp.where(lane < 64, pltpu.roll(b, 64, 1), pltpu.roll(c, 96, 1)),
            )
            a, b, c, tail = (jnp.where(lane < USED, t, exponent) for t in (a, b, c, tail))
            at = (band * 32 + group * 4) * 8
            out_ref[at : at + 16, :] = coded(jnp.concatenate([a, b], axis=0))
            out_ref[at + 16 : at + 32, :] = coded(jnp.concatenate([c, tail], axis=0))


def share_of(place, cq_all, attn_out, kept, came):
    return pl.pallas_call(
        share_kernel,
        in_specs=[SMEM, VMEM, VMEM, VMEM, VMEM],
        out_specs=VMEM,
        out_shape=jax.ShapeDtypeStruct((2048, 128), I16),
        scratch_shapes=[pltpu.VMEM((RANK, 4 * BLOCK), F32)],
        compiler_params=pltpu.CompilerParams(vmem_limit_bytes=LIMIT),
    )(place.reshape(1), cq_all, attn_out, kept, came)


def sum_kernel(in_ref, out_ref):
    def step(i, total):
        at = pl.multiple_of(i * 64, 64)
        parts = [decoded(in_ref[pl.ds(at + 16 * j, 16), :]) for j in range(4)]
        return total + ((parts[0] + parts[1]) + (parts[2] + parts[3]))

    total = lax.fori_loop(0, 32, step, jnp.zeros((16, 128), F32), unroll=4)
    total = total[:8] + total[8:]
    used = lanes_of((8, 128)) < USED
    largest = jnp.max(jnp.where(used, jnp.abs(total), 0.0), axis=1, keepdims=True)
    exponent, factor = scale_of(largest)
    tile = jnp.where(used, total * factor, exponent)
    tile = coded(jnp.concatenate([tile, tile], axis=0))
    out_ref[...] = jnp.broadcast_to(tile[None], (128, 16, 128)).reshape(2048, 128)


def summed(received):
    return pl.pallas_call(
        sum_kernel,
        in_specs=[VMEM],
        out_specs=VMEM,
        out_shape=jax.ShapeDtypeStruct((2048, 128), I16),
        compiler_params=pltpu.CompilerParams(vmem_limit_bytes=LIMIT),
    )(received)


def grad_kernel(attn_ref, cols_ref, error_ref, out_ref):
    grad = lax.dot_general(
        attn_ref[...], cols_ref[...], (((0,), (0,)), ((), ())), preferred_element_type=F32
    ) + error_ref[...].astype(F32)
    high = grad.astype(BF16)
    out_ref[:, :128] = high
    out_ref[:, 128:] = (grad - high.astype(F32)).astype(BF16)


def grad_of(gathered, out_cols, error):
    return pl.pallas_call(
        grad_kernel,
        grid=(8,),
        in_specs=[
            pl.BlockSpec((128, BLOCK), lambda i: (0, i)),
            pl.BlockSpec((128, 128), lambda i: (0, 0)),
            pl.BlockSpec((BLOCK, 128), lambda i: (i, 0)),
        ],
        out_specs=pl.BlockSpec((BLOCK, 256), lambda i: (i, 0)),
        out_shape=jax.ShapeDtypeStruct((WIDTH, 256), BF16),
        compiler_params=pltpu.CompilerParams(vmem_limit_bytes=LIMIT),
        cost_estimate=pl.CostEstimate(
            flops=2 * 128 * 128 * WIDTH, bytes_accessed=WIDTH * 1024, transcendentals=0
        ),
    )(gathered, out_cols, error)


def factor_kernel(core_ref, mine_ref, other_ref, grad_ref, raw_ref, gram_ref, p_ref):
    lane = lanes_of((16, 128))
    for ref, core in ((mine_ref, core_ref[0]), (other_ref, 1 - core_ref[0])):
        for pair in range(4):
            for group in range(8):
                first, second = [], []
                for band in (2 * pair, 2 * pair + 1):
                    at = (band * 32 + group * 4) * 8
                    first.append(decoded(ref[at : at + 16, :]))
                    second.append(decoded(ref[at + 16 : at + 32, :]))
                a = jnp.concatenate([t[:8] for t in first], axis=0)
                b = jnp.concatenate([t[8:] for t in first], axis=0)
                c = jnp.concatenate([t[:8] for t in second], axis=0)
                tail = jnp.concatenate([t[8:] for t in second], axis=0)
                for j, (tile, shift) in enumerate(((a, 96), (b, 64), (c, 32))):
                    tile = jnp.where(lane < USED, tile, pltpu.roll(tail, shift, 1))
                    place = group * 3 + j
                    row, column = place // 6, place % 6
                    at = (2 * row + core) * 3 + column // 2
                    lanes = slice(128 * (column % 2), 128 * (column % 2) + 128)
                    high = tile.astype(BF16)
                    low = (tile - high.astype(F32)).astype(BF16)
                    p_ref[at, pair * 16 : pair * 16 + 16, lanes] = high
                    p_ref[at, RANK + pair * 16 : RANK + pair * 16 + 16, lanes] = low
    raw = jnp.zeros((128, 256), F32)
    gram = jnp.zeros((128, 128), F32)
    for i in range(24):
        part = p_ref[i]
        raw += jnp.dot(part, grad_ref[i * 256 : i * 256 + 256, :], preferred_element_type=F32)
        gram += lax.dot_general(
            part, part, (((1,), (1,)), ((), ())), preferred_element_type=F32
        )
    raw = raw[:RANK] + raw[RANK:]
    raw_ref[...] = raw[:, :128] + raw[:, 128:]
    gram = gram[:RANK] + gram[RANK:]
    gram_ref[...] = gram[:, :RANK] + gram[:, RANK:]


def factor_of(core, mine, other, grad):
    return pl.pallas_call(
        factor_kernel,
        in_specs=[SMEM, VMEM, VMEM, VMEM],
        out_specs=[VMEM, VMEM, VMEM],
        out_shape=[
            jax.ShapeDtypeStruct((RANK, 128), F32),
            jax.ShapeDtypeStruct((RANK, RANK), F32),
            jax.ShapeDtypeStruct((24, 128, 256), BF16),
        ],
        compiler_params=pltpu.CompilerParams(vmem_limit_bytes=LIMIT),
    )(core.reshape(1), mine, other, grad)


def final_kernel(
    place_ref, inverse_ref, sums_ref, p_ref, grad_ref, approx_ref, q_ref, error_ref, expert_ref, full_ref
):
    sums = jnp.sum(sums_ref[...], axis=0)
    expert_ref[...] = sums[RANK : RANK + 1, :USED]
    inverse = inverse_ref[...]
    q_t = jnp.dot(inverse, sums[:RANK], precision=HIGH) * (1.0 / 64.0)
    q_ref[...] = q_t.T
    weights = jnp.dot(inverse.T, q_t, precision=HIGH)
    high = weights.astype(BF16)
    low = (weights - high.astype(F32)).astype(BF16)
    both = jnp.concatenate([high, low], axis=1)
    both = jnp.concatenate([both, both], axis=0)
    for i in range(24):
        rows = slice(i * 256, i * 256 + 256)
        part = lax.dot_general(
            p_ref[i], both, (((0,), (0,)), ((), ())), preferred_element_type=F32
        )
        part = part[:, :128] + part[:, 128:]
        full_ref[rows, :] = part
        grad = grad_ref[rows, :].astype(F32)
        error_ref[rows, :] = (grad[:, :128] + grad[:, 128:] - part).astype(BF16)
    here = pl.ds(pl.multiple_of(place_ref[0] * 96, 32), 96)
    approx_ref[...] = full_ref[here, :].astype(BF16)


def final_of(place, inverse, sums, p_parts, grad):
    return pl.pallas_call(
        final_kernel,
        in_specs=[SMEM, VMEM, VMEM, VMEM, VMEM],
        out_specs=[VMEM] * 4,
        out_shape=[
            jax.ShapeDtypeStruct((96, 128), BF16),
            jax.ShapeDtypeStruct((128, RANK), F32),
            jax.ShapeDtypeStruct((WIDTH, 128), BF16),
            jax.ShapeDtypeStruct((1, USED), F32),
        ],
        scratch_shapes=[pltpu.VMEM((WIDTH, 128), F32)],
        compiler_params=pltpu.CompilerParams(vmem_limit_bytes=LIMIT),
    )(place.reshape(1), inverse, sums, p_parts, grad)


def expert_partial(tokens, routes, route_logits, pair_score):
    first = 1.0 / (1.0 + jnp.exp(route_logits[:, 1] - route_logits[:, 0]))
    product = first * (1.0 - first) * (pair_score[:, 0] - pair_score[:, 1])
    rows = product.astype(BF16)[:, None]
    labels = jnp.arange(8, dtype=jnp.int32)[None, :]
    zero = jnp.zeros((), BF16)
    spread = jnp.where(routes[:, :1] == labels, rows, zero) + jnp.where(
        routes[:, 1:] == labels, -rows, zero
    )
    return lax.dot_general(spread, tokens, (((0,), (0,)), ((), ())), preferred_element_type=F32)


def local(attn_out, out_cols, error_in, power_q, tokens, routes, route_logits, pair_score):
    error = error_in[0]
    core = lax.axis_index("c").astype(jnp.int32)
    place = lax.axis_index("l").astype(jnp.int32)
    data = ((lax.axis_index("x") * 8 + lax.axis_index("y")) * 2 + lax.axis_index("h")).astype(jnp.int32)
    gathered = lax.all_gather(attn_out, EXPERT, axis=1, tiled=True)
    power_t = power_q.T

    part = lax.dot_general(
        power_t, out_cols.astype(F32), (((1,), (1,)), ((), ())), precision=HIGH
    )
    expert_rows = expert_partial(tokens, routes, route_logits, pair_score).reshape(8, 48, 128)
    cq_all = exchange(
        jnp.concatenate([jnp.broadcast_to(part, (8, RANK, 128)), expert_rows], axis=1), EXPERT
    )
    by_y = jnp.sum(cq_all[:, RANK:], axis=0).reshape(4, 8, 2, 96)
    by_y = by_y.transpose(1, 0, 2, 3).reshape(8, 6, 128)

    came = swap_cores(error_share(power_t, error, 1 - core))
    kept = error_share(power_t, error, core)
    codes = share_of(place, cq_all, attn_out, kept, came)
    piece = summed(exchange(codes.reshape(256, 8, 128), FLAT).reshape(2048, 128))
    mine = exchange(piece.reshape(256, 8, 128), FLAT).reshape(2048, 128)
    other = swap_cores(mine)
    grad = grad_of(gathered, out_cols, error)
    raw, gram, p_parts = factor_of(core, mine, other, grad)

    over_y = jnp.sum(
        exchange(jnp.concatenate([jnp.broadcast_to(raw, (8, RANK, 128)), by_y], axis=1), "y"),
        axis=0,
    )
    rest = jnp.pad(over_y[RANK:].reshape(8, 1, 96), ((0, 0), (0, 0), (0, 32)))
    sums = exchange(
        jnp.concatenate([jnp.broadcast_to(over_y[:RANK], (8, RANK, 128)), rest], axis=1),
        ("x", "h"),
    )

    factor = jnp.linalg.cholesky(gram, symmetrize_input=False)
    inverse = lax.linalg.triangular_solve(
        factor, jnp.eye(RANK, dtype=F32), left_side=True, lower=True
    )
    approx, q_new, error_out, expert_grad = final_of(data, inverse, sums, p_parts, grad)
    return approx, q_new, error_out[None], expert_grad


def solution(mesh):
    fine = Mesh(mesh.devices.reshape(4, 8, 2, 4, 2), DP + EXPERT)
    everyone = P(DP + EXPERT, None)
    return jax.shard_map(
        local,
        mesh=fine,
        in_specs=(
            P(DP, EXPERT),
            P(DP, EXPERT),
            P(DP, None, EXPERT),
            P(EXPERT, None),
            everyone,
            everyone,
            everyone,
            everyone,
        ),
        out_specs=(P(DP, EXPERT), P(EXPERT, None), P(DP, None, EXPERT), P(EXPERT, DP)),
        check_vma=False,
    )
```

```python
import functools

import jax
import jax.numpy as jnp
from jax import lax
from jax.experimental import pallas as pl
from jax.experimental.pallas import tpu as pltpu
from jax.sharding import Mesh, PartitionSpec as P

HIGH = lax.Precision.HIGHEST
F32, BF16, I16 = jnp.float32, jnp.bfloat16, jnp.int16
RANK = 64
WIDTH = 6144
BLOCK = 768
DP = ("x", "y", "h")
EXPERT = ("l", "c")
FLAT = ("x", "y", "h", "l")
LIMIT = 12 * 1024 * 1024
TOP = 32000.0
STEP = 64.0
USED = 96

VMEM = pl.BlockSpec(memory_space=pltpu.VMEM)
SMEM = pl.BlockSpec(memory_space=pltpu.SMEM)
ANY = pl.BlockSpec(memory_space=pl.ANY)


def exchange(values, axes):
    return lax.all_to_all(values, axes, split_axis=0, concat_axis=0, tiled=True)


def swap_cores(values):
    return lax.ppermute(values, "c", [(0, 1), (1, 0)])


def three(values):
    high = values.astype(BF16)
    rest = values - high.astype(F32)
    middle = rest.astype(BF16)
    low = (rest - middle.astype(F32)).astype(BF16)
    return jnp.concatenate([high, middle, low], axis=0)


def folded(stacked):
    return stacked[:RANK] + stacked[RANK : 2 * RANK] + stacked[2 * RANK :]


def scale_of(largest):
    exponent = jnp.ceil(STEP * jnp.log2(jnp.maximum(largest, 1e-30))) + 1.0
    return exponent, jnp.exp2(exponent * (-1.0 / STEP)) * TOP


def lanes_of(shape):
    return lax.broadcasted_iota(jnp.int32, shape, 1)


def coded(values):
    return jnp.round(values).astype(jnp.int32).astype(I16)


def decoded(tile):
    wide = tile.astype(jnp.int32).astype(F32)
    return wide * (jnp.exp2(wide[:, 127:128] * (1.0 / STEP)) * (1.0 / TOP))


def error_kernel(block_ref, q_ref, error_ref, attn_ref, out_ref, pass_ref):
    del block_ref
    pass_ref[...] = attn_ref[...]
    out_ref[...] = folded(
        lax.dot_general(
            three(q_ref[...]), error_ref[...], (((1,), (1,)), ((), ())), preferred_element_type=F32
        )
    )


def error_share(power_t, error, core, attn_out):
    return pl.pallas_call(
        error_kernel,
        grid_spec=pltpu.PrefetchScalarGridSpec(
            num_scalar_prefetch=1,
            grid=(4,),
            in_specs=[
                pl.BlockSpec((RANK, 128), lambda i, core: (0, 0)),
                pl.BlockSpec((BLOCK, 128), lambda i, core: (2 * i + core[0], 0)),
                pl.BlockSpec((32, BLOCK), lambda i, core: (i, 0)),
            ],
            out_specs=[
                pl.BlockSpec((RANK, BLOCK), lambda i, core: (0, i)),
                pl.BlockSpec((32, BLOCK), lambda i, core: (i, 0)),
            ],
        ),
        out_shape=[
            jax.ShapeDtypeStruct((RANK, 4 * BLOCK), F32),
            jax.ShapeDtypeStruct((128, BLOCK), BF16),
        ],
        compiler_params=pltpu.CompilerParams(vmem_limit_bytes=LIMIT),
        cost_estimate=pl.CostEstimate(
            flops=2 * 192 * 128 * 3072, bytes_accessed=3072 * 512, transcendentals=0
        ),
    )(core.reshape(1), power_t, error, attn_out)


def share_kernel(place_ref, cq_ref, attn_ref, kept_ref, came_ref, out_ref, half_ref):
    cq = jnp.sum(cq_ref[:, :RANK, :], axis=0)
    from_attn = folded(jnp.dot(three(cq), attn_ref[...], preferred_element_type=F32))
    half_ref[...] = kept_ref[...] + came_ref[...]
    here = pl.ds(pl.multiple_of(place_ref[0] * BLOCK, BLOCK), BLOCK)
    half_ref[:, here] += from_attn
    lane = lanes_of((8, 128))
    for band in range(8):
        rows = slice(band * 8, band * 8 + 8)
        tiles = [half_ref[rows, t * 128 : t * 128 + 128] for t in range(24)]
        largest = functools.reduce(jnp.maximum, [jnp.abs(t) for t in tiles])
        exponent, factor = scale_of(jnp.max(largest, axis=1, keepdims=True))
        exponent = jnp.broadcast_to(exponent, (8, 128))
        factor = jnp.broadcast_to(factor, (8, 128))
        for group in range(8):
            a, b, c = (t * factor for t in tiles[group * 3 : group * 3 + 3])
            tail = jnp.where(
                lane < 32,
                pltpu.roll(a, 32, 1),
                jnp.where(lane < 64, pltpu.roll(b, 64, 1), pltpu.roll(c, 96, 1)),
            )
            a, b, c, tail = (jnp.where(lane < USED, t, exponent) for t in (a, b, c, tail))
            at = (band * 32 + group * 4) * 8
            out_ref[at : at + 16, :] = coded(jnp.concatenate([a, b], axis=0))
            out_ref[at + 16 : at + 32, :] = coded(jnp.concatenate([c, tail], axis=0))


def share_of(place, cq_all, attn_out, kept, came):
    return pl.pallas_call(
        share_kernel,
        in_specs=[SMEM, VMEM, VMEM, VMEM, VMEM],
        out_specs=VMEM,
        out_shape=jax.ShapeDtypeStruct((2048, 128), I16),
        scratch_shapes=[pltpu.VMEM((RANK, 4 * BLOCK), F32)],
        compiler_params=pltpu.CompilerParams(vmem_limit_bytes=LIMIT),
        cost_estimate=pl.CostEstimate(
            flops=2 * 192 * 128 * 768, bytes_accessed=6000000, transcendentals=0
        ),
    )(place.reshape(1), cq_all, attn_out, kept, came)


def sum_kernel(in_ref, grad_ref, out_ref):
    del grad_ref

    def step(i, total):
        at = pl.multiple_of(i * 64, 64)
        parts = [decoded(in_ref[pl.ds(at + 16 * j, 16), :]) for j in range(4)]
        return total + ((parts[0] + parts[1]) + (parts[2] + parts[3]))

    total = lax.fori_loop(0, 32, step, jnp.zeros((16, 128), F32), unroll=4)
    total = total[:8] + total[8:]
    used = lanes_of((8, 128)) < USED
    largest = jnp.max(jnp.where(used, jnp.abs(total), 0.0), axis=1, keepdims=True)
    exponent, factor = scale_of(largest)
    tile = jnp.where(used, total * factor, exponent)
    tile = coded(jnp.concatenate([tile, tile], axis=0))
    out_ref[...] = jnp.broadcast_to(tile[None], (128, 16, 128)).reshape(2048, 128)


def summed(received, grad):
    return pl.pallas_call(
        sum_kernel,
        in_specs=[VMEM, ANY],
        out_specs=VMEM,
        out_shape=jax.ShapeDtypeStruct((2048, 128), I16),
        compiler_params=pltpu.CompilerParams(vmem_limit_bytes=LIMIT),
        cost_estimate=pl.CostEstimate(flops=1000000, bytes_accessed=1500000, transcendentals=0),
    )(received, grad)


def grad_kernel(at_ref, own_ref, other_ref, cols_ref, error_ref, out_ref):
    step = pl.program_id(0)
    mine = lax.rem(step, 2) == at_ref[1]
    attn = jnp.where(mine, own_ref[0], other_ref[0])
    grad = lax.dot_general(
        attn, cols_ref[...], (((0,), (0,)), ((), ())), preferred_element_type=F32
    ) + error_ref[...].astype(F32)
    high = grad.astype(BF16)
    out_ref[:, :128] = high
    out_ref[:, 128:] = (grad - high.astype(F32)).astype(BF16)


def grad_of(place, core, own, other, out_cols, error):
    def slot(i, at):
        return (lax.rem(at[0] + 4 - i // 2, 4), 0, 0)

    return pl.pallas_call(
        grad_kernel,
        grid_spec=pltpu.PrefetchScalarGridSpec(
            num_scalar_prefetch=1,
            grid=(8,),
            in_specs=[
                pl.BlockSpec((1, 128, BLOCK), slot),
                pl.BlockSpec((1, 128, BLOCK), slot),
                pl.BlockSpec((128, 128), lambda i, at: (0, 0)),
                pl.BlockSpec((BLOCK, 128), lambda i, at: (i, 0)),
            ],
            out_specs=pl.BlockSpec((BLOCK, 256), lambda i, at: (i, 0)),
        ),
        out_shape=jax.ShapeDtypeStruct((WIDTH, 256), BF16),
        compiler_params=pltpu.CompilerParams(vmem_limit_bytes=LIMIT),
        cost_estimate=pl.CostEstimate(
            flops=2 * 128 * 128 * WIDTH, bytes_accessed=WIDTH * 1024, transcendentals=0
        ),
    )(jnp.stack([place, core]), own, other, out_cols, error)


def unpacked(ref, p_ref):
    lane = lanes_of((16, 128))
    for pair in range(4):
        for group in range(8):
            first, second = [], []
            for band in (2 * pair, 2 * pair + 1):
                at = (band * 32 + group * 4) * 8
                first.append(decoded(ref[at : at + 16, :]))
                second.append(decoded(ref[at + 16 : at + 32, :]))
            a = jnp.concatenate([t[:8] for t in first], axis=0)
            b = jnp.concatenate([t[8:] for t in first], axis=0)
            c = jnp.concatenate([t[:8] for t in second], axis=0)
            tail = jnp.concatenate([t[8:] for t in second], axis=0)
            for j, (tile, shift) in enumerate(((a, 96), (b, 64), (c, 32))):
                tile = jnp.where(lane < USED, tile, pltpu.roll(tail, shift, 1))
                place = group * 3 + j
                lanes = slice(128 * (place % 2), 128 * (place % 2) + 128)
                high = tile.astype(BF16)
                low = (tile - high.astype(F32)).astype(BF16)
                p_ref[place // 2, pair * 16 : pair * 16 + 16, lanes] = high
                p_ref[place // 2, RANK + pair * 16 : RANK + pair * 16 + 16, lanes] = low


def rows_of(i, core):
    return pl.ds(pl.multiple_of((2 * (i // 3) + core) * BLOCK + (i % 3) * 256, 256), 256)


def product(p_ref, grad_ref, core):
    total = jnp.zeros((128, 256), F32)
    for i in range(12):
        total += jnp.dot(p_ref[i], grad_ref[rows_of(i, core), :], preferred_element_type=F32)
    total = total[:RANK] + total[RANK:]
    return total[:, :128] + total[:, 128:]


def squared(p_ref):
    total = jnp.zeros((128, 128), F32)
    for i in range(12):
        total += lax.dot_general(
            p_ref[i], p_ref[i], (((1,), (1,)), ((), ())), preferred_element_type=F32
        )
    total = total[:RANK] + total[RANK:]
    return total[:, :RANK] + total[:, RANK:]


def mine_kernel(core_ref, codes_ref, grad_ref, raw_ref, gram_ref, p_ref):
    unpacked(codes_ref, p_ref)
    raw_ref[...] = product(p_ref, grad_ref, core_ref[0])
    gram_ref[...] = squared(p_ref)


def other_kernel(
    core_ref, codes_ref, grad_ref, mine_ref, square_ref, expert_ref, out_ref, gram_ref, p_ref
):
    unpacked(codes_ref, p_ref)
    gram_ref[...] = square_ref[...] + squared(p_ref)
    raw = mine_ref[...] + product(p_ref, grad_ref, 1 - core_ref[0])
    for i in range(8):
        out_ref[i, :RANK, :] = raw
        out_ref[i, RANK:, :] = expert_ref[i]


SQUARE = jax.ShapeDtypeStruct((RANK, RANK), F32)
HALF = jax.ShapeDtypeStruct((12, 128, 256), BF16)
HALF_COST = pl.CostEstimate(flops=2 * 128 * 256 * 3072, bytes_accessed=3000000, transcendentals=0)


def mine_of(core, codes, grad):
    return pl.pallas_call(
        mine_kernel,
        in_specs=[SMEM, VMEM, VMEM],
        out_specs=[VMEM, VMEM, VMEM],
        out_shape=[jax.ShapeDtypeStruct((RANK, 128), F32), SQUARE, HALF],
        compiler_params=pltpu.CompilerParams(vmem_limit_bytes=LIMIT),
        cost_estimate=HALF_COST,
    )(core.reshape(1), codes, grad)


def other_of(core, codes, grad, raw, square, by_y):
    return pl.pallas_call(
        other_kernel,
        in_specs=[SMEM, VMEM, VMEM, VMEM, VMEM, VMEM],
        out_specs=[VMEM, VMEM, VMEM],
        out_shape=[jax.ShapeDtypeStruct((8, RANK + 6, 128), F32), SQUARE, HALF],
        compiler_params=pltpu.CompilerParams(vmem_limit_bytes=LIMIT),
        cost_estimate=HALF_COST,
    )(core.reshape(1), codes, grad, raw, square, by_y)


def final_kernel(
    at_ref, inverse_ref, sums_ref, mine_ref, other_ref, grad_ref,
    approx_ref, q_ref, error_ref, expert_ref, full_ref,
):
    sums = jnp.sum(sums_ref[...], axis=0)
    expert_ref[...] = sums[RANK : RANK + 1, :USED]
    inverse = inverse_ref[...]
    q_t = jnp.dot(inverse, sums[:RANK], precision=HIGH) * (1.0 / 64.0)
    q_ref[...] = q_t
    weights = jnp.dot(inverse.T, q_t, precision=HIGH)
    high = weights.astype(BF16)
    low = (weights - high.astype(F32)).astype(BF16)
    both = jnp.concatenate([high, low], axis=1)
    both = jnp.concatenate([both, both], axis=0)
    for ref, core in ((mine_ref, at_ref[1]), (other_ref, 1 - at_ref[1])):
        for i in range(12):
            rows = rows_of(i, core)
            part = lax.dot_general(
                ref[i], both, (((0,), (0,)), ((), ())), preferred_element_type=F32
            )
            part = part[:, :128] + part[:, 128:]
            full_ref[rows, :] = part
            grad = grad_ref[rows, :].astype(F32)
            error_ref[rows, :] = (grad[:, :128] + grad[:, 128:] - part).astype(BF16)
    here = pl.ds(pl.multiple_of(at_ref[0] * 96, 32), 96)
    approx_ref[...] = full_ref[here, :].astype(BF16)


def final_of(data, core, inverse, sums, p_mine, p_other, grad):
    return pl.pallas_call(
        final_kernel,
        in_specs=[SMEM, VMEM, VMEM, VMEM, VMEM, VMEM],
        out_specs=[VMEM] * 4,
        out_shape=[
            jax.ShapeDtypeStruct((96, 128), BF16),
            jax.ShapeDtypeStruct((RANK, 128), F32),
            jax.ShapeDtypeStruct((WIDTH, 128), BF16),
            jax.ShapeDtypeStruct((1, USED), F32),
        ],
        scratch_shapes=[pltpu.VMEM((WIDTH, 128), F32)],
        compiler_params=pltpu.CompilerParams(vmem_limit_bytes=LIMIT),
    )(jnp.stack([data, core]), inverse, sums, p_mine, p_other, grad)


def first_kernel(q_ref, cols_ref, tokens_ref, routes_ref, logits_ref, score_ref, out_ref):
    part = folded(
        lax.dot_general(
            three(q_ref[...]), cols_ref[...], (((1,), (1,)), ((), ())), preferred_element_type=F32
        )
    )
    for i in range(8):
        out_ref[i, :RANK, :] = part
    first = 1.0 / (1.0 + jnp.exp(logits_ref[1:2, :] - logits_ref[0:1, :]))
    rows = first * (1.0 - first) * (score_ref[0:1, :] - score_ref[1:2, :])
    rows = jnp.broadcast_to(rows, (8, 128))
    label = lax.broadcasted_iota(jnp.int32, (8, 128), 0)
    spread = jnp.where(routes_ref[0:1, :] == label, rows, 0.0) - jnp.where(
        routes_ref[1:2, :] == label, rows, 0.0
    )
    experts = jnp.dot(spread.astype(BF16), tokens_ref[...], preferred_element_type=F32)
    for t in range(48):
        out_ref[:, RANK + t, :] = experts[:, t * 128 : t * 128 + 128]


def first_of(power_t, out_cols, tokens, routes_t, logits_t, score_t):
    return pl.pallas_call(
        first_kernel,
        in_specs=[VMEM] * 6,
        out_specs=VMEM,
        out_shape=jax.ShapeDtypeStruct((8, RANK + 48, 128), F32),
        compiler_params=pltpu.CompilerParams(vmem_limit_bytes=LIMIT),
    )(power_t, out_cols, tokens, routes_t, logits_t, score_t)


def local(attn_out, out_cols, error_in, power_q, tokens, routes, route_logits, pair_score):
    error = error_in[0]
    core = lax.axis_index("c").astype(jnp.int32)
    place = lax.axis_index("l").astype(jnp.int32)
    data = (lax.axis_index("x") * 8 + lax.axis_index("y")) * 2 + lax.axis_index("h")
    power_t = power_q.T

    cq_all = exchange(
        first_of(power_t, out_cols, tokens, routes.T, route_logits.T, pair_score.T), EXPERT
    )
    by_y = jnp.sum(cq_all[:, RANK:], axis=0).reshape(4, 8, 2, 96)
    by_y = by_y.transpose(1, 0, 2, 3).reshape(8, 6, 128)

    given, attn_first = error_share(power_t, error, 1 - core, attn_out)
    came = swap_cores(given)
    kept, attn_here = error_share(power_t, error, core, attn_first)
    shifted = [
        lax.ppermute(attn_here, "l", [(i, (i + k) % 4) for i in range(4)]) for k in (1, 2, 3)
    ]
    codes = share_of(place, cq_all, attn_out, kept, came)
    own = jnp.stack([attn_here, *shifted])
    grad = grad_of(place, core, own, swap_cores(own), out_cols, error)
    piece = summed(exchange(codes.reshape(256, 8, 128), FLAT).reshape(2048, 128), grad)
    mine = exchange(piece.reshape(256, 8, 128), FLAT).reshape(2048, 128)
    other = swap_cores(mine)
    raw, square, p_mine = mine_of(core, mine, grad)
    send, gram, p_other = other_of(core, other, grad, raw, square, by_y)

    over_y = jnp.sum(exchange(send, "y"), axis=0)
    rest = jnp.pad(over_y[RANK:].reshape(8, 1, 96), ((0, 0), (0, 0), (0, 32)))
    sums = exchange(
        jnp.concatenate([jnp.broadcast_to(over_y[:RANK], (8, RANK, 128)), rest], axis=1),
        ("x", "h"),
    )

    factor = jnp.linalg.cholesky(gram, symmetrize_input=False)
    inverse = lax.linalg.triangular_solve(
        factor, jnp.eye(RANK, dtype=F32), left_side=True, lower=True
    )
    approx, q_t, error_out, expert_grad = final_of(
        data.astype(jnp.int32), core, inverse, sums, p_mine, p_other, grad
    )
    return approx, q_t.T, error_out[None], expert_grad


def solution(mesh):
    fine = Mesh(mesh.devices.reshape(4, 8, 2, 4, 2), DP + EXPERT)
    everyone = P(DP + EXPERT, None)
    return jax.shard_map(
        local,
        mesh=fine,
        in_specs=(
            P(DP, EXPERT),
            P(DP, EXPERT),
            P(DP, None, EXPERT),
            P(EXPERT, None),
            everyone,
            everyone,
            everyone,
            everyone,
        ),
        out_specs=(P(DP, EXPERT), P(EXPERT, None), P(DP, None, EXPERT), P(EXPERT, DP)),
        check_vma=False,
    )
```

```python
import functools

import jax
import jax.numpy as jnp
from jax import lax
from jax.experimental import pallas as pl
from jax.experimental.pallas import tpu as pltpu
from jax.sharding import Mesh, PartitionSpec as P

HIGH = lax.Precision.HIGHEST
F32, BF16, I16 = jnp.float32, jnp.bfloat16, jnp.int16
RANK = 64
WIDTH = 6144
BLOCK = 768
DP = ("x", "y", "h")
EXPERT = ("l", "c")
FLAT = ("x", "y", "h", "l")
LIMIT = 12 * 1024 * 1024
MOST = 60 * 1024 * 1024
TOP = 32000.0
STEP = 64.0
USED = 96

VMEM = pl.BlockSpec(memory_space=pltpu.VMEM)
SMEM = pl.BlockSpec(memory_space=pltpu.SMEM)
ANY = pl.BlockSpec(memory_space=pl.ANY)


def exchange(values, axes):
    return lax.all_to_all(values, axes, split_axis=0, concat_axis=0, tiled=True)


def swap_cores(values):
    return lax.ppermute(values, "c", [(0, 1), (1, 0)])


def three(values):
    high = values.astype(BF16)
    rest = values - high.astype(F32)
    middle = rest.astype(BF16)
    low = (rest - middle.astype(F32)).astype(BF16)
    return jnp.concatenate([high, middle, low], axis=0)


def folded(stacked):
    return stacked[:RANK] + stacked[RANK : 2 * RANK] + stacked[2 * RANK :]


def scale_of(largest):
    exponent = jnp.ceil(STEP * jnp.log2(jnp.maximum(largest, 1e-30))) + 1.0
    return exponent, jnp.exp2(exponent * (-1.0 / STEP)) * TOP


def lanes_of(shape):
    return lax.broadcasted_iota(jnp.int32, shape, 1)


def coded(values):
    return jnp.round(values).astype(jnp.int32).astype(I16)


def decoded(tile):
    wide = tile.astype(jnp.int32).astype(F32)
    return wide * (jnp.exp2(wide[:, 127:128] * (1.0 / STEP)) * (1.0 / TOP))


def eye_of(rows):
    shape = (rows, 128)
    return lax.broadcasted_iota(jnp.int32, shape, 0) == lax.broadcasted_iota(jnp.int32, shape, 1)


def packed(raw):
    exponent, factor = scale_of(jnp.max(jnp.abs(raw), axis=1, keepdims=True))
    row = jnp.sum(jnp.where(eye_of(RANK), exponent, 0.0), axis=0, keepdims=True)
    return raw * factor, jnp.concatenate([row, jnp.zeros((7, 128), F32)], axis=0)


def tagged(rows):
    used = lanes_of(rows.shape) < USED
    rows = jnp.where(used, rows, 0.0)
    exponent, factor = scale_of(jnp.max(jnp.abs(rows), axis=1, keepdims=True))
    return jnp.where(used, rows * factor, exponent)


def collected(ref):
    raw = jnp.zeros((RANK, 128), F32)
    rows = jnp.zeros((8, 128), F32)
    eye = eye_of(RANK)
    for i in range(8):
        codes = ref[i, :RANK, :].astype(jnp.int32).astype(F32)
        rest = ref[i, RANK:, :].astype(jnp.int32).astype(F32)
        exponent = jnp.sum(jnp.where(eye, rest[8:9, :], 0.0), axis=1, keepdims=True)
        raw += codes * (jnp.exp2(exponent * (1.0 / STEP)) * (1.0 / TOP))
        rows += rest[:8] * (jnp.exp2(rest[:8, 127:128] * (1.0 / STEP)) * (1.0 / TOP))
    return raw, rows


def error_kernel(block_ref, q_ref, error_ref, attn_ref, out_ref, pass_ref):
    del block_ref
    pass_ref[...] = attn_ref[...]
    out_ref[...] = folded(
        lax.dot_general(
            three(q_ref[...]), error_ref[...], (((1,), (1,)), ((), ())), preferred_element_type=F32
        )
    )


def error_share(power_t, error, core, attn_out):
    return pl.pallas_call(
        error_kernel,
        grid_spec=pltpu.PrefetchScalarGridSpec(
            num_scalar_prefetch=1,
            grid=(4,),
            in_specs=[
                pl.BlockSpec((RANK, 128), lambda i, core: (0, 0)),
                pl.BlockSpec((BLOCK, 128), lambda i, core: (2 * i + core[0], 0)),
                pl.BlockSpec((32, BLOCK), lambda i, core: (i, 0)),
            ],
            out_specs=[
                pl.BlockSpec((RANK, BLOCK), lambda i, core: (0, i)),
                pl.BlockSpec((32, BLOCK), lambda i, core: (i, 0)),
            ],
        ),
        out_shape=[
            jax.ShapeDtypeStruct((RANK, 4 * BLOCK), F32),
            jax.ShapeDtypeStruct((128, BLOCK), BF16),
        ],
        compiler_params=pltpu.CompilerParams(vmem_limit_bytes=MOST),
        cost_estimate=pl.CostEstimate(
            flops=2 * 192 * 128 * 3072, bytes_accessed=3072 * 512, transcendentals=0
        ),
    )(core.reshape(1), power_t, error, attn_out)


def share_kernel(
    place_ref, cq_ref, attn_ref, kept_ref, came_ref, out_ref, expert_ref, half_ref, other_ref, sems
):
    copies = [
        pltpu.make_async_copy(kept_ref, half_ref, sems.at[0]),
        pltpu.make_async_copy(came_ref, other_ref, sems.at[1]),
    ]
    for copy in copies:
        copy.start()
    total = jnp.sum(cq_ref[...], axis=0)
    expert_ref[...] = total[RANK:]
    from_attn = folded(jnp.dot(three(total[:RANK]), attn_ref[...], preferred_element_type=F32))
    for copy in copies:
        copy.wait()
    half_ref[...] += other_ref[...]
    here = pl.ds(pl.multiple_of(place_ref[0] * BLOCK, BLOCK), BLOCK)
    half_ref[:, here] += from_attn
    lane = lanes_of((8, 128))
    for band in range(8):
        rows = slice(band * 8, band * 8 + 8)
        tiles = [half_ref[rows, t * 128 : t * 128 + 128] for t in range(24)]
        largest = functools.reduce(jnp.maximum, [jnp.abs(t) for t in tiles])
        exponent, factor = scale_of(jnp.max(largest, axis=1, keepdims=True))
        exponent = jnp.broadcast_to(exponent, (8, 128))
        factor = jnp.broadcast_to(factor, (8, 128))
        for group in range(8):
            a, b, c = (t * factor for t in tiles[group * 3 : group * 3 + 3])
            tail = jnp.where(
                lane < 32,
                pltpu.roll(a, 32, 1),
                jnp.where(lane < 64, pltpu.roll(b, 64, 1), pltpu.roll(c, 96, 1)),
            )
            a, b, c, tail = (jnp.where(lane < USED, t, exponent) for t in (a, b, c, tail))
            at = (band * 32 + group * 4) * 8
            out_ref[at : at + 16, :] = coded(jnp.concatenate([a, b], axis=0))
            out_ref[at + 16 : at + 32, :] = coded(jnp.concatenate([c, tail], axis=0))


def share_of(place, cq_all, attn_out, kept, came):
    return pl.pallas_call(
        share_kernel,
        in_specs=[SMEM, VMEM, VMEM, ANY, ANY],
        out_specs=[VMEM, VMEM],
        out_shape=[
            jax.ShapeDtypeStruct((2048, 128), I16),
            jax.ShapeDtypeStruct((48, 128), F32),
        ],
        scratch_shapes=[
            pltpu.VMEM((RANK, 4 * BLOCK), F32),
            pltpu.VMEM((RANK, 4 * BLOCK), F32),
            pltpu.SemaphoreType.DMA((2,)),
        ],
        compiler_params=pltpu.CompilerParams(vmem_limit_bytes=61850000),
        cost_estimate=pl.CostEstimate(
            flops=2 * 192 * 128 * 768, bytes_accessed=6000000, transcendentals=0
        ),
    )(place.reshape(1), cq_all, attn_out, kept, came)


def sum_kernel(in_ref, grad_ref, expert_ref, out_ref):
    del grad_ref, expert_ref

    def step(i, total):
        at = pl.multiple_of(i * 64, 64)
        parts = [decoded(in_ref[pl.ds(at + 16 * j, 16), :]) for j in range(4)]
        return total + ((parts[0] + parts[1]) + (parts[2] + parts[3]))

    total = lax.fori_loop(0, 32, step, jnp.zeros((16, 128), F32), unroll=4)
    total = total[:8] + total[8:]
    used = lanes_of((8, 128)) < USED
    largest = jnp.max(jnp.where(used, jnp.abs(total), 0.0), axis=1, keepdims=True)
    exponent, factor = scale_of(largest)
    tile = jnp.where(used, total * factor, exponent)
    tile = coded(jnp.concatenate([tile, tile], axis=0))
    out_ref[...] = jnp.broadcast_to(tile[None], (128, 16, 128)).reshape(2048, 128)


def summed(received, *others):
    return pl.pallas_call(
        sum_kernel,
        in_specs=[VMEM, ANY, ANY],
        out_specs=VMEM,
        out_shape=jax.ShapeDtypeStruct((2048, 128), I16),
        compiler_params=pltpu.CompilerParams(vmem_limit_bytes=LIMIT),
        cost_estimate=pl.CostEstimate(flops=1000000, bytes_accessed=1500000, transcendentals=0),
    )(received, *others)


def grad_kernel(at_ref, own_ref, other_ref, cols_ref, error_ref, out_ref):
    step = pl.program_id(0)
    mine = lax.rem(step, 2) == at_ref[1]
    attn = jnp.where(mine, own_ref[0], other_ref[0])
    grad = lax.dot_general(
        attn, cols_ref[...], (((0,), (0,)), ((), ())), preferred_element_type=F32
    ) + error_ref[...].astype(F32)
    high = grad.astype(BF16)
    out_ref[:, :128] = high
    out_ref[:, 128:] = (grad - high.astype(F32)).astype(BF16)


def grad_of(place, core, own, other, out_cols, error):
    def slot(i, at):
        return (lax.rem(at[0] + 4 - i // 2, 4), 0, 0)

    return pl.pallas_call(
        grad_kernel,
        grid_spec=pltpu.PrefetchScalarGridSpec(
            num_scalar_prefetch=1,
            grid=(8,),
            in_specs=[
                pl.BlockSpec((1, 128, BLOCK), slot),
                pl.BlockSpec((1, 128, BLOCK), slot),
                pl.BlockSpec((128, 128), lambda i, at: (0, 0)),
                pl.BlockSpec((BLOCK, 128), lambda i, at: (i, 0)),
            ],
            out_specs=pl.BlockSpec((BLOCK, 256), lambda i, at: (i, 0)),
        ),
        out_shape=jax.ShapeDtypeStruct((WIDTH, 256), BF16),
        compiler_params=pltpu.CompilerParams(vmem_limit_bytes=LIMIT),
        cost_estimate=pl.CostEstimate(
            flops=2 * 128 * 128 * WIDTH, bytes_accessed=WIDTH * 1024, transcendentals=0
        ),
    )(jnp.stack([place, core]), own, other, out_cols, error)


def unpacked(ref, p_ref):
    lane = lanes_of((16, 128))
    for pair in range(4):
        for group in range(8):
            first, second = [], []
            for band in (2 * pair, 2 * pair + 1):
                at = (band * 32 + group * 4) * 8
                first.append(decoded(ref[at : at + 16, :]))
                second.append(decoded(ref[at + 16 : at + 32, :]))
            a = jnp.concatenate([t[:8] for t in first], axis=0)
            b = jnp.concatenate([t[8:] for t in first], axis=0)
            c = jnp.concatenate([t[:8] for t in second], axis=0)
            tail = jnp.concatenate([t[8:] for t in second], axis=0)
            for j, (tile, shift) in enumerate(((a, 96), (b, 64), (c, 32))):
                tile = jnp.where(lane < USED, tile, pltpu.roll(tail, shift, 1))
                place = group * 3 + j
                lanes = slice(128 * (place % 2), 128 * (place % 2) + 128)
                high = tile.astype(BF16)
                low = (tile - high.astype(F32)).astype(BF16)
                p_ref[place // 2, pair * 16 : pair * 16 + 16, lanes] = high
                p_ref[place // 2, RANK + pair * 16 : RANK + pair * 16 + 16, lanes] = low


def product(p_ref, grad_ref):
    total = jnp.zeros((128, 256), F32)
    for i in range(12):
        rows = slice(i * 256, i * 256 + 256)
        total += jnp.dot(p_ref[i], grad_ref[rows, :], preferred_element_type=F32)
    total = total[:RANK] + total[RANK:]
    return total[:, :128] + total[:, 128:]


def fetch(grad_ref, half_ref, core, sem):
    copies = []
    for i in range(4):
        rows = pl.ds(pl.multiple_of((2 * i + core) * BLOCK, BLOCK), BLOCK)
        copies.append(
            pltpu.make_async_copy(
                grad_ref.at[rows, :], half_ref.at[pl.ds(i * BLOCK, BLOCK), :], sem.at[i]
            )
        )
        copies[-1].start()
    return copies


def half_of(core, codes_ref, grad_ref, p_ref, half_ref, keep_ref, sem):
    copies = fetch(grad_ref, half_ref, core, sem)
    unpacked(codes_ref, keep_ref)
    out = pltpu.make_async_copy(keep_ref, p_ref, sem.at[4])
    out.start()
    square = squared(keep_ref)
    for copy in copies:
        copy.wait()
    raw = product(keep_ref, half_ref)
    out.wait()
    return raw, square


def squared(p_ref):
    total = jnp.zeros((128, 128), F32)
    for i in range(12):
        total += lax.dot_general(
            p_ref[i], p_ref[i], (((1,), (1,)), ((), ())), preferred_element_type=F32
        )
    total = total[:RANK] + total[RANK:]
    return total[:, :RANK] + total[:, RANK:]


def mine_kernel(
    core_ref, codes_ref, grad_ref, raw_ref, square_ref, p_ref, half_ref, keep_ref, sem
):
    raw_ref[...], square_ref[...] = half_of(
        core_ref[0], codes_ref, grad_ref, p_ref, half_ref, keep_ref, sem
    )


def other_kernel(
    core_ref, codes_ref, grad_ref, mine_ref, square_ref, expert_ref,
    out_ref, gram_ref, p_ref, half_ref, keep_ref, sem,
):
    raw, square = half_of(
        1 - core_ref[0], codes_ref, grad_ref, p_ref, half_ref, keep_ref, sem
    )
    gram_ref[...] = square_ref[...] + square
    codes, scales = packed(raw + mine_ref[...])
    codes = coded(codes)
    for i in range(8):
        rest = jnp.concatenate([tagged(expert_ref[i]), scales], axis=0)
        out_ref[i, :RANK, :] = codes
        out_ref[i, RANK:, :] = coded(rest)


SQUARE = jax.ShapeDtypeStruct((RANK, RANK), F32)
MESSAGE = jax.ShapeDtypeStruct((8, RANK + 16, 128), I16)
HALF = jax.ShapeDtypeStruct((12, 128, 256), BF16)
HALF_SCRATCH = [
    pltpu.VMEM((4 * BLOCK, 256), BF16),
    pltpu.VMEM((12, 128, 256), BF16),
    pltpu.SemaphoreType.DMA((5,)),
]
HALF_COST = pl.CostEstimate(flops=2 * 128 * 256 * 3072, bytes_accessed=3000000, transcendentals=0)


def mine_of(core, codes, grad):
    return pl.pallas_call(
        mine_kernel,
        in_specs=[SMEM, VMEM, ANY],
        out_specs=[VMEM, VMEM, ANY],
        scratch_shapes=HALF_SCRATCH,
        out_shape=[jax.ShapeDtypeStruct((RANK, 128), F32), SQUARE, HALF],
        compiler_params=pltpu.CompilerParams(vmem_limit_bytes=62200000),
        cost_estimate=HALF_COST,
    )(core.reshape(1), codes, grad)


def other_of(core, codes, grad, raw, square, by_y):
    return pl.pallas_call(
        other_kernel,
        in_specs=[SMEM, VMEM, ANY, VMEM, VMEM, VMEM],
        out_specs=[VMEM, VMEM, ANY],
        scratch_shapes=HALF_SCRATCH,
        out_shape=[MESSAGE, SQUARE, HALF],
        compiler_params=pltpu.CompilerParams(vmem_limit_bytes=62200000),
        cost_estimate=HALF_COST,
    )(core.reshape(1), codes, grad, raw, square, by_y)


def after_kernel(in_ref, other_ref, out_ref):
    del in_ref, other_ref, out_ref


def after(values, other):
    return pl.pallas_call(
        after_kernel,
        in_specs=[ANY, ANY],
        out_specs=ANY,
        out_shape=jax.ShapeDtypeStruct(values.shape, values.dtype),
        input_output_aliases={0: 0},
        compiler_params=pltpu.CompilerParams(vmem_limit_bytes=1024 * 1024),
    )(values, other)


def pass_kernel(in_ref, out_ref):
    raw, rows = collected(in_ref)
    codes, scales = packed(raw)
    rows = tagged(rows)
    for i in range(8):
        mine = jnp.broadcast_to(rows[i : i + 1], (8, 128))
        out_ref[i, :RANK, :] = coded(codes)
        out_ref[i, RANK:, :] = coded(jnp.concatenate([mine, scales], axis=0))


def passed(received):
    return pl.pallas_call(
        pass_kernel,
        in_specs=[VMEM],
        out_specs=VMEM,
        out_shape=MESSAGE,
        compiler_params=pltpu.CompilerParams(vmem_limit_bytes=LIMIT),
    )(received)


def final_kernel(
    at_ref, inverse_ref, sums_ref, mine_ref, other_ref, grad_ref,
    approx_ref, q_ref, error_ref, expert_ref, full_ref, both_ref,
):
    step = pl.program_id(0)

    @pl.when(step == 0)
    def _():
        raw, rows = collected(sums_ref)
        expert_ref[...] = rows[:1, :USED]
        inverse = inverse_ref[...]
        q_t = jnp.dot(inverse, raw, precision=HIGH) * (1.0 / 64.0)
        q_ref[...] = q_t
        weights = jnp.dot(inverse.T, q_t, precision=HIGH)
        high = weights.astype(BF16)
        low = (weights - high.astype(F32)).astype(BF16)
        both = jnp.concatenate([high, low], axis=1)
        both_ref[...] = jnp.concatenate([both, both], axis=0)

    for ref, core in ((mine_ref, at_ref[1]), (other_ref, 1 - at_ref[1])):
        for i in range(3):
            rows = pl.ds(pl.multiple_of(core * BLOCK + i * 256, 256), 256)
            part = lax.dot_general(
                ref[i], both_ref[...], (((0,), (0,)), ((), ())), preferred_element_type=F32
            )
            part = part[:, :128] + part[:, 128:]
            full_ref[step, rows, :] = part
            grad = grad_ref[rows, :].astype(F32)
            error_ref[rows, :] = (grad[:, :128] + grad[:, 128:] - part).astype(BF16)

    @pl.when(step == 3)
    def _():
        first = at_ref[0] * 96
        here = pl.ds(pl.multiple_of(lax.rem(first, 2 * BLOCK), 32), 96)
        approx_ref[...] = full_ref[first // (2 * BLOCK), here, :].astype(BF16)


def final_of(data, core, inverse, sums, p_mine, p_other, grad):
    def whole(*shape):
        return pl.BlockSpec(shape, lambda i, at: (0,) * len(shape))

    half = pl.BlockSpec((3, 128, 256), lambda i, at: (i, 0, 0))
    return pl.pallas_call(
        final_kernel,
        grid_spec=pltpu.PrefetchScalarGridSpec(
            num_scalar_prefetch=1,
            grid=(4,),
            in_specs=[
                whole(RANK, RANK),
                whole(8, RANK + 16, 128),
                half,
                half,
                pl.BlockSpec((2 * BLOCK, 256), lambda i, at: (i, 0)),
            ],
            out_specs=[
                whole(96, 128),
                whole(RANK, 128),
                pl.BlockSpec((2 * BLOCK, 128), lambda i, at: (i, 0)),
                whole(1, USED),
            ],
            scratch_shapes=[pltpu.VMEM((4, 2 * BLOCK, 128), F32), pltpu.VMEM((128, 256), BF16)],
        ),
        out_shape=[
            jax.ShapeDtypeStruct((96, 128), BF16),
            jax.ShapeDtypeStruct((RANK, 128), F32),
            jax.ShapeDtypeStruct((WIDTH, 128), BF16),
            jax.ShapeDtypeStruct((1, USED), F32),
        ],
        compiler_params=pltpu.CompilerParams(vmem_limit_bytes=62200000),
    )(jnp.stack([data, core]), inverse, sums, p_mine, p_other, grad)


def first_kernel(q_ref, cols_ref, tokens_ref, routes_ref, logits_ref, score_ref, out_ref):
    part = folded(
        lax.dot_general(
            three(q_ref[...]), cols_ref[...], (((1,), (1,)), ((), ())), preferred_element_type=F32
        )
    )
    for i in range(8):
        out_ref[i, :RANK, :] = part
    first = 1.0 / (1.0 + jnp.exp(logits_ref[1:2, :] - logits_ref[0:1, :]))
    rows = first * (1.0 - first) * (score_ref[0:1, :] - score_ref[1:2, :])
    rows = jnp.broadcast_to(rows, (8, 128))
    label = lax.broadcasted_iota(jnp.int32, (8, 128), 0)
    spread = jnp.where(routes_ref[0:1, :] == label, rows, 0.0) - jnp.where(
        routes_ref[1:2, :] == label, rows, 0.0
    )
    experts = jnp.dot(spread.astype(BF16), tokens_ref[...], preferred_element_type=F32)
    for t in range(48):
        out_ref[:, RANK + t, :] = experts[:, t * 128 : t * 128 + 128]


def first_of(power_t, out_cols, tokens, routes_t, logits_t, score_t):
    def whole(*shape):
        return pl.BlockSpec(shape, lambda i: (0,) * len(shape))

    return pl.pallas_call(
        first_kernel,
        grid=(1,),
        in_specs=[
            whole(RANK, 128),
            whole(128, 128),
            whole(128, WIDTH),
            whole(2, 128),
            whole(2, 128),
            whole(2, 128),
        ],
        out_specs=whole(8, RANK + 48, 128),
        out_shape=jax.ShapeDtypeStruct((8, RANK + 48, 128), F32),
        compiler_params=pltpu.CompilerParams(vmem_limit_bytes=MOST),
    )(power_t, out_cols, tokens, routes_t, logits_t, score_t)


def local(attn_out, out_cols, error_in, power_q, tokens, routes, route_logits, pair_score):
    error = error_in[0]
    core = lax.axis_index("c").astype(jnp.int32)
    place = lax.axis_index("l").astype(jnp.int32)
    data = (lax.axis_index("x") * 8 + lax.axis_index("y")) * 2 + lax.axis_index("h")
    power_t = power_q.T

    cq_all = exchange(
        first_of(power_t, out_cols, tokens, routes.T, route_logits.T, pair_score.T), EXPERT
    )
    given, attn_first = error_share(power_t, error, 1 - core, attn_out)
    came = swap_cores(given)
    kept, attn_here = error_share(power_t, error, core, attn_first)
    before = lax.ppermute(attn_here, "l", [(i, (i + 1) % 4) for i in range(4)])
    codes, experts = share_of(place, cq_all, attn_out, kept, came)
    near = jnp.stack([attn_here, before])
    far = lax.ppermute(near, "l", [(i, (i + 2) % 4) for i in range(4)])
    own = jnp.concatenate([near, far])
    by_y = experts.reshape(4, 8, 2, 96).transpose(1, 0, 2, 3).reshape(8, 8, 96)
    by_y = jnp.pad(by_y, ((0, 0), (0, 0), (0, 32)))
    piece = summed(exchange(codes.reshape(256, 8, 128), FLAT).reshape(2048, 128), own, by_y)
    grad = grad_of(place, core, own, swap_cores(own), out_cols, error)
    mine = exchange(piece.reshape(256, 8, 128), FLAT).reshape(2048, 128)
    mine = after(mine, grad)
    other = swap_cores(mine)
    raw, square, p_mine = mine_of(core, mine, grad)
    send, gram, p_other = other_of(core, other, grad, raw, square, by_y)

    sums = exchange(passed(exchange(send, "y")), ("x", "h"))

    factor = jnp.linalg.cholesky(gram, symmetrize_input=False)
    inverse = lax.linalg.triangular_solve(
        factor, jnp.eye(RANK, dtype=F32), left_side=True, lower=True
    )
    approx, q_t, error_out, expert_grad = final_of(
        data.astype(jnp.int32), core, inverse, sums, p_mine, p_other, grad
    )
    return approx, q_t.T, error_out[None], expert_grad


def solution(mesh):
    fine = Mesh(mesh.devices.reshape(4, 8, 2, 4, 2), DP + EXPERT)
    everyone = P(DP + EXPERT, None)
    return jax.shard_map(
        local,
        mesh=fine,
        in_specs=(
            P(DP, EXPERT),
            P(DP, EXPERT),
            P(DP, None, EXPERT),
            P(EXPERT, None),
            everyone,
            everyone,
            everyone,
            everyone,
        ),
        out_specs=(P(DP, EXPERT), P(EXPERT, None), P(DP, None, EXPERT), P(EXPERT, DP)),
        check_vma=False,
    )
```

```python
import functools

import jax
import jax.numpy as jnp
from jax import lax
from jax.experimental import pallas as pl
from jax.experimental.pallas import tpu as pltpu
from jax.sharding import Mesh, PartitionSpec as P

HIGH = lax.Precision.HIGHEST
F32, BF16, I16 = jnp.float32, jnp.bfloat16, jnp.int16
RANK = 64
WIDTH = 6144
BLOCK = 768
DP = ("x", "y", "h")
EXPERT = ("l", "c")
FLAT = ("x", "y", "h", "l")
LIMIT = 12 * 1024 * 1024
MOST = 60 * 1024 * 1024
TOP = 32000.0
STEP = 64.0
USED = 96

VMEM = pl.BlockSpec(memory_space=pltpu.VMEM)
SMEM = pl.BlockSpec(memory_space=pltpu.SMEM)
ANY = pl.BlockSpec(memory_space=pl.ANY)


def exchange(values, axes):
    return lax.all_to_all(values, axes, split_axis=0, concat_axis=0, tiled=True)


def swap_cores(values):
    return lax.ppermute(values, "c", [(0, 1), (1, 0)])


def three(values):
    high = values.astype(BF16)
    rest = values - high.astype(F32)
    middle = rest.astype(BF16)
    low = (rest - middle.astype(F32)).astype(BF16)
    return jnp.concatenate([high, middle, low], axis=0)


def folded(stacked):
    return stacked[:RANK] + stacked[RANK : 2 * RANK] + stacked[2 * RANK :]


def scale_of(largest):
    exponent = jnp.ceil(STEP * jnp.log2(jnp.maximum(largest, 1e-30))) + 1.0
    return exponent, jnp.exp2(exponent * (-1.0 / STEP)) * TOP


def lanes_of(shape):
    return lax.broadcasted_iota(jnp.int32, shape, 1)


def coded(values):
    return jnp.round(values).astype(jnp.int32).astype(I16)


def decoded(tile):
    wide = tile.astype(jnp.int32).astype(F32)
    return wide * (jnp.exp2(wide[:, 127:128] * (1.0 / STEP)) * (1.0 / TOP))


def eye_of(rows):
    shape = (rows, 128)
    return lax.broadcasted_iota(jnp.int32, shape, 0) == lax.broadcasted_iota(jnp.int32, shape, 1)


def packed(raw):
    exponent, factor = scale_of(jnp.max(jnp.abs(raw), axis=1, keepdims=True))
    row = jnp.sum(jnp.where(eye_of(RANK), exponent, 0.0), axis=0, keepdims=True)
    return raw * factor, jnp.concatenate([row, jnp.zeros((7, 128), F32)], axis=0)


def tagged(rows):
    used = lanes_of(rows.shape) < USED
    rows = jnp.where(used, rows, 0.0)
    exponent, factor = scale_of(jnp.max(jnp.abs(rows), axis=1, keepdims=True))
    return jnp.where(used, rows * factor, exponent)


def collected(ref):
    raw = jnp.zeros((RANK, 128), F32)
    rows = jnp.zeros((8, 128), F32)
    eye = eye_of(RANK)
    for i in range(8):
        codes = ref[i, :RANK, :].astype(jnp.int32).astype(F32)
        rest = ref[i, RANK:, :].astype(jnp.int32).astype(F32)
        exponent = jnp.sum(jnp.where(eye, rest[8:9, :], 0.0), axis=1, keepdims=True)
        raw += codes * (jnp.exp2(exponent * (1.0 / STEP)) * (1.0 / TOP))
        rows += rest[:8] * (jnp.exp2(rest[:8, 127:128] * (1.0 / STEP)) * (1.0 / TOP))
    return raw, rows


def error_kernel(block_ref, q_ref, error_ref, attn_ref, out_ref, pass_ref):
    del block_ref
    pass_ref[...] = attn_ref[...]
    out_ref[...] = folded(
        lax.dot_general(
            three(q_ref[...]), error_ref[...], (((1,), (1,)), ((), ())), preferred_element_type=F32
        )
    )


def error_share(power_t, error, core, attn_out):
    return pl.pallas_call(
        error_kernel,
        grid_spec=pltpu.PrefetchScalarGridSpec(
            num_scalar_prefetch=1,
            grid=(4,),
            in_specs=[
                pl.BlockSpec((RANK, 128), lambda i, core: (0, 0)),
                pl.BlockSpec((BLOCK, 128), lambda i, core: (2 * i + core[0], 0)),
                pl.BlockSpec((32, BLOCK), lambda i, core: (i, 0)),
            ],
            out_specs=[
                pl.BlockSpec((RANK, BLOCK), lambda i, core: (0, i)),
                pl.BlockSpec((32, BLOCK), lambda i, core: (i, 0)),
            ],
        ),
        out_shape=[
            jax.ShapeDtypeStruct((RANK, 4 * BLOCK), F32),
            jax.ShapeDtypeStruct((128, BLOCK), BF16),
        ],
        compiler_params=pltpu.CompilerParams(vmem_limit_bytes=LIMIT),
        cost_estimate=pl.CostEstimate(
            flops=2 * 192 * 128 * 3072, bytes_accessed=3072 * 512, transcendentals=0
        ),
    )(core.reshape(1), power_t, error, attn_out)


def share_kernel(place_ref, cq_ref, attn_ref, kept_ref, came_ref, out_ref, expert_ref, half_ref):
    total = jnp.sum(cq_ref[...], axis=0)
    expert_ref[...] = total[RANK:]
    from_attn = folded(jnp.dot(three(total[:RANK]), attn_ref[...], preferred_element_type=F32))
    half_ref[...] = kept_ref[...] + came_ref[...]
    here = pl.ds(pl.multiple_of(place_ref[0] * BLOCK, BLOCK), BLOCK)
    half_ref[:, here] += from_attn
    lane = lanes_of((8, 128))
    for band in range(8):
        rows = slice(band * 8, band * 8 + 8)
        tiles = [half_ref[rows, t * 128 : t * 128 + 128] for t in range(24)]
        largest = functools.reduce(jnp.maximum, [jnp.abs(t) for t in tiles])
        exponent, factor = scale_of(jnp.max(largest, axis=1, keepdims=True))
        exponent = jnp.broadcast_to(exponent, (8, 128))
        factor = jnp.broadcast_to(factor, (8, 128))
        for group in range(8):
            a, b, c = (t * factor for t in tiles[group * 3 : group * 3 + 3])
            tail = jnp.where(
                lane < 32,
                pltpu.roll(a, 32, 1),
                jnp.where(lane < 64, pltpu.roll(b, 64, 1), pltpu.roll(c, 96, 1)),
            )
            a, b, c, tail = (jnp.where(lane < USED, t, exponent) for t in (a, b, c, tail))
            at = (band * 32 + group * 4) * 8
            out_ref[at : at + 16, :] = coded(jnp.concatenate([a, b], axis=0))
            out_ref[at + 16 : at + 32, :] = coded(jnp.concatenate([c, tail], axis=0))


def share_of(place, cq_all, attn_out, kept, came):
    return pl.pallas_call(
        share_kernel,
        in_specs=[SMEM, VMEM, VMEM, VMEM, VMEM],
        out_specs=[VMEM, VMEM],
        out_shape=[
            jax.ShapeDtypeStruct((2048, 128), I16),
            jax.ShapeDtypeStruct((48, 128), F32),
        ],
        scratch_shapes=[pltpu.VMEM((RANK, 4 * BLOCK), F32)],
        compiler_params=pltpu.CompilerParams(vmem_limit_bytes=LIMIT),
        cost_estimate=pl.CostEstimate(
            flops=2 * 192 * 128 * 768, bytes_accessed=6000000, transcendentals=0
        ),
    )(place.reshape(1), cq_all, attn_out, kept, came)


def sum_kernel(in_ref, grad_ref, expert_ref, out_ref):
    del grad_ref, expert_ref

    def step(i, total):
        at = pl.multiple_of(i * 64, 64)
        parts = [decoded(in_ref[pl.ds(at + 16 * j, 16), :]) for j in range(4)]
        return total + ((parts[0] + parts[1]) + (parts[2] + parts[3]))

    total = lax.fori_loop(0, 32, step, jnp.zeros((16, 128), F32), unroll=4)
    total = total[:8] + total[8:]
    used = lanes_of((8, 128)) < USED
    largest = jnp.max(jnp.where(used, jnp.abs(total), 0.0), axis=1, keepdims=True)
    exponent, factor = scale_of(largest)
    tile = jnp.where(used, total * factor, exponent)
    tile = coded(jnp.concatenate([tile, tile], axis=0))
    out_ref[...] = jnp.broadcast_to(tile[None], (128, 16, 128)).reshape(2048, 128)


def summed(received, *others):
    return pl.pallas_call(
        sum_kernel,
        in_specs=[VMEM, ANY, ANY],
        out_specs=VMEM,
        out_shape=jax.ShapeDtypeStruct((2048, 128), I16),
        compiler_params=pltpu.CompilerParams(vmem_limit_bytes=LIMIT),
        cost_estimate=pl.CostEstimate(flops=1000000, bytes_accessed=1500000, transcendentals=0),
    )(received, *others)


def grad_kernel(at_ref, own_ref, other_ref, cols_ref, error_ref, out_ref):
    step = pl.program_id(0)
    mine = lax.rem(step, 2) == at_ref[1]
    attn = jnp.where(mine, own_ref[0], other_ref[0])
    grad = lax.dot_general(
        attn, cols_ref[...], (((0,), (0,)), ((), ())), preferred_element_type=F32
    ) + error_ref[...].astype(F32)
    high = grad.astype(BF16)
    out_ref[:, :128] = high
    out_ref[:, 128:] = (grad - high.astype(F32)).astype(BF16)


def grad_of(place, core, own, other, out_cols, error):
    def slot(i, at):
        return (lax.rem(at[0] + 4 - i // 2, 4), 0, 0)

    return pl.pallas_call(
        grad_kernel,
        grid_spec=pltpu.PrefetchScalarGridSpec(
            num_scalar_prefetch=1,
            grid=(8,),
            in_specs=[
                pl.BlockSpec((1, 128, BLOCK), slot),
                pl.BlockSpec((1, 128, BLOCK), slot),
                pl.BlockSpec((128, 128), lambda i, at: (0, 0)),
                pl.BlockSpec((BLOCK, 128), lambda i, at: (i, 0)),
            ],
            out_specs=pl.BlockSpec((BLOCK, 256), lambda i, at: (i, 0)),
        ),
        out_shape=jax.ShapeDtypeStruct((WIDTH, 256), BF16),
        compiler_params=pltpu.CompilerParams(vmem_limit_bytes=LIMIT),
        cost_estimate=pl.CostEstimate(
            flops=2 * 128 * 128 * WIDTH, bytes_accessed=WIDTH * 1024, transcendentals=0
        ),
    )(jnp.stack([place, core]), own, other, out_cols, error)


def unpacked(ref, p_ref):
    lane = lanes_of((16, 128))
    for pair in range(4):
        for group in range(8):
            first, second = [], []
            for band in (2 * pair, 2 * pair + 1):
                at = (band * 32 + group * 4) * 8
                first.append(decoded(ref[at : at + 16, :]))
                second.append(decoded(ref[at + 16 : at + 32, :]))
            a = jnp.concatenate([t[:8] for t in first], axis=0)
            b = jnp.concatenate([t[8:] for t in first], axis=0)
            c = jnp.concatenate([t[:8] for t in second], axis=0)
            tail = jnp.concatenate([t[8:] for t in second], axis=0)
            for j, (tile, shift) in enumerate(((a, 96), (b, 64), (c, 32))):
                tile = jnp.where(lane < USED, tile, pltpu.roll(tail, shift, 1))
                place = group * 3 + j
                lanes = slice(128 * (place % 2), 128 * (place % 2) + 128)
                high = tile.astype(BF16)
                low = (tile - high.astype(F32)).astype(BF16)
                p_ref[place // 2, pair * 16 : pair * 16 + 16, lanes] = high
                p_ref[place // 2, RANK + pair * 16 : RANK + pair * 16 + 16, lanes] = low


def rows_of(i, core):
    return pl.ds(pl.multiple_of((2 * (i // 3) + core) * BLOCK + (i % 3) * 256, 256), 256)


def product(p_ref, grad_ref, core):
    total = jnp.zeros((128, 256), F32)
    for i in range(12):
        total += jnp.dot(p_ref[i], grad_ref[rows_of(i, core), :], preferred_element_type=F32)
    total = total[:RANK] + total[RANK:]
    return total[:, :128] + total[:, 128:]


def squared(p_ref):
    total = jnp.zeros((128, 128), F32)
    for i in range(12):
        total += lax.dot_general(
            p_ref[i], p_ref[i], (((1,), (1,)), ((), ())), preferred_element_type=F32
        )
    total = total[:RANK] + total[RANK:]
    return total[:, :RANK] + total[:, RANK:]


def mine_kernel(core_ref, codes_ref, grad_ref, raw_ref, square_ref, p_ref):
    unpacked(codes_ref, p_ref)
    raw_ref[...] = product(p_ref, grad_ref, core_ref[0])
    square_ref[...] = squared(p_ref)


def other_kernel(
    core_ref, codes_ref, grad_ref, mine_ref, square_ref, expert_ref, out_ref, gram_ref, p_ref
):
    unpacked(codes_ref, p_ref)
    gram_ref[...] = square_ref[...] + squared(p_ref)
    codes, scales = packed(mine_ref[...] + product(p_ref, grad_ref, 1 - core_ref[0]))
    codes = coded(codes)
    for i in range(8):
        rest = jnp.concatenate([tagged(expert_ref[i]), scales], axis=0)
        out_ref[i, :RANK, :] = codes
        out_ref[i, RANK:, :] = coded(rest)


SQUARE = jax.ShapeDtypeStruct((RANK, RANK), F32)
MESSAGE = jax.ShapeDtypeStruct((8, RANK + 16, 128), I16)
HALF = jax.ShapeDtypeStruct((12, 128, 256), BF16)
HALF_COST = pl.CostEstimate(flops=2 * 128 * 256 * 3072, bytes_accessed=3000000, transcendentals=0)


def mine_of(core, codes, grad):
    return pl.pallas_call(
        mine_kernel,
        in_specs=[SMEM, VMEM, VMEM],
        out_specs=[VMEM, VMEM, VMEM],
        out_shape=[jax.ShapeDtypeStruct((RANK, 128), F32), SQUARE, HALF],
        compiler_params=pltpu.CompilerParams(vmem_limit_bytes=LIMIT),
        cost_estimate=HALF_COST,
    )(core.reshape(1), codes, grad)


def other_of(core, codes, grad, raw, square, by_y):
    return pl.pallas_call(
        other_kernel,
        in_specs=[SMEM, VMEM, VMEM, VMEM, VMEM, VMEM],
        out_specs=[VMEM, VMEM, VMEM],
        out_shape=[MESSAGE, SQUARE, HALF],
        compiler_params=pltpu.CompilerParams(vmem_limit_bytes=LIMIT),
        cost_estimate=HALF_COST,
    )(core.reshape(1), codes, grad, raw, square, by_y)


def pass_kernel(in_ref, out_ref):
    raw, rows = collected(in_ref)
    codes, scales = packed(raw)
    rows = tagged(rows)
    for i in range(8):
        mine = jnp.broadcast_to(rows[i : i + 1], (8, 128))
        out_ref[i, :RANK, :] = coded(codes)
        out_ref[i, RANK:, :] = coded(jnp.concatenate([mine, scales], axis=0))


def passed(received):
    return pl.pallas_call(
        pass_kernel,
        in_specs=[VMEM],
        out_specs=VMEM,
        out_shape=MESSAGE,
        compiler_params=pltpu.CompilerParams(vmem_limit_bytes=LIMIT),
    )(received)


def final_kernel(
    at_ref, inverse_ref, sums_ref, mine_ref, other_ref, grad_ref,
    approx_ref, q_ref, error_ref, expert_ref, full_ref,
):
    raw, rows = collected(sums_ref)
    expert_ref[...] = rows[:1, :USED]
    inverse = inverse_ref[...]
    q_t = jnp.dot(inverse, raw, precision=HIGH) * (1.0 / 64.0)
    q_ref[...] = q_t
    weights = jnp.dot(inverse.T, q_t, precision=HIGH)
    high = weights.astype(BF16)
    low = (weights - high.astype(F32)).astype(BF16)
    both = jnp.concatenate([high, low], axis=1)
    both = jnp.concatenate([both, both], axis=0)
    for ref, core in ((mine_ref, at_ref[1]), (other_ref, 1 - at_ref[1])):
        for i in range(12):
            rows = rows_of(i, core)
            part = lax.dot_general(
                ref[i], both, (((0,), (0,)), ((), ())), preferred_element_type=F32
            )
            part = part[:, :128] + part[:, 128:]
            full_ref[rows, :] = part
            grad = grad_ref[rows, :].astype(F32)
            error_ref[rows, :] = (grad[:, :128] + grad[:, 128:] - part).astype(BF16)
    here = pl.ds(pl.multiple_of(at_ref[0] * 96, 32), 96)
    approx_ref[...] = full_ref[here, :].astype(BF16)


def final_of(data, core, inverse, sums, p_mine, p_other, grad):
    return pl.pallas_call(
        final_kernel,
        in_specs=[SMEM, VMEM, VMEM, VMEM, VMEM, VMEM],
        out_specs=[VMEM] * 4,
        out_shape=[
            jax.ShapeDtypeStruct((96, 128), BF16),
            jax.ShapeDtypeStruct((RANK, 128), F32),
            jax.ShapeDtypeStruct((WIDTH, 128), BF16),
            jax.ShapeDtypeStruct((1, USED), F32),
        ],
        scratch_shapes=[pltpu.VMEM((WIDTH, 128), F32)],
        compiler_params=pltpu.CompilerParams(vmem_limit_bytes=LIMIT),
    )(jnp.stack([data, core]), inverse, sums, p_mine, p_other, grad)


def first_kernel(q_ref, cols_ref, tokens_ref, routes_ref, logits_ref, score_ref, out_ref):
    part = folded(
        lax.dot_general(
            three(q_ref[...]), cols_ref[...], (((1,), (1,)), ((), ())), preferred_element_type=F32
        )
    )
    for i in range(8):
        out_ref[i, :RANK, :] = part
    first = 1.0 / (1.0 + jnp.exp(logits_ref[1:2, :] - logits_ref[0:1, :]))
    rows = first * (1.0 - first) * (score_ref[0:1, :] - score_ref[1:2, :])
    rows = jnp.broadcast_to(rows, (8, 128))
    label = lax.broadcasted_iota(jnp.int32, (8, 128), 0)
    spread = jnp.where(routes_ref[0:1, :] == label, rows, 0.0) - jnp.where(
        routes_ref[1:2, :] == label, rows, 0.0
    )
    experts = jnp.dot(spread.astype(BF16), tokens_ref[...], preferred_element_type=F32)
    for t in range(48):
        out_ref[:, RANK + t, :] = experts[:, t * 128 : t * 128 + 128]


def first_of(power_t, out_cols, tokens, routes_t, logits_t, score_t):
    def whole(*shape):
        return pl.BlockSpec(shape, lambda i: (0,) * len(shape))

    return pl.pallas_call(
        first_kernel,
        grid=(1,),
        in_specs=[
            whole(RANK, 128),
            whole(128, 128),
            whole(128, WIDTH),
            whole(2, 128),
            whole(2, 128),
            whole(2, 128),
        ],
        out_specs=whole(8, RANK + 48, 128),
        out_shape=jax.ShapeDtypeStruct((8, RANK + 48, 128), F32),
        compiler_params=pltpu.CompilerParams(vmem_limit_bytes=MOST),
    )(power_t, out_cols, tokens, routes_t, logits_t, score_t)


def local(attn_out, out_cols, error_in, power_q, tokens, routes, route_logits, pair_score):
    error = error_in[0]
    core = lax.axis_index("c").astype(jnp.int32)
    place = lax.axis_index("l").astype(jnp.int32)
    data = (lax.axis_index("x") * 8 + lax.axis_index("y")) * 2 + lax.axis_index("h")
    power_t = power_q.T

    cq_all = exchange(
        first_of(power_t, out_cols, tokens, routes.T, route_logits.T, pair_score.T), EXPERT
    )
    given, attn_first = error_share(power_t, error, 1 - core, attn_out)
    came = swap_cores(given)
    kept, attn_here = error_share(power_t, error, core, attn_first)
    shifted = [
        lax.ppermute(attn_here, "l", [(i, (i + k) % 4) for i in range(4)]) for k in (1, 2, 3)
    ]
    own = jnp.stack([attn_here, *shifted])
    codes, experts = share_of(place, cq_all, attn_out, kept, came)
    by_y = experts.reshape(4, 8, 2, 96).transpose(1, 0, 2, 3).reshape(8, 8, 96)
    by_y = jnp.pad(by_y, ((0, 0), (0, 0), (0, 32)))
    grad = grad_of(place, core, own, swap_cores(own), out_cols, error)
    piece = summed(exchange(codes.reshape(256, 8, 128), FLAT).reshape(2048, 128), grad, by_y)
    mine = exchange(piece.reshape(256, 8, 128), FLAT).reshape(2048, 128)
    other = swap_cores(mine)
    raw, square, p_mine = mine_of(core, mine, grad)
    send, gram, p_other = other_of(core, other, grad, raw, square, by_y)

    sums = exchange(passed(exchange(send, "y")), ("x", "h"))

    factor = jnp.linalg.cholesky(gram, symmetrize_input=False)
    inverse = lax.linalg.triangular_solve(
        factor, jnp.eye(RANK, dtype=F32), left_side=True, lower=True
    )
    approx, q_t, error_out, expert_grad = final_of(
        data.astype(jnp.int32), core, inverse, sums, p_mine, p_other, grad
    )
    return approx, q_t.T, error_out[None], expert_grad


def solution(mesh):
    fine = Mesh(mesh.devices.reshape(4, 8, 2, 4, 2), DP + EXPERT)
    everyone = P(DP + EXPERT, None)
    return jax.shard_map(
        local,
        mesh=fine,
        in_specs=(
            P(DP, EXPERT),
            P(DP, EXPERT),
            P(DP, None, EXPERT),
            P(EXPERT, None),
            everyone,
            everyone,
            everyone,
            everyone,
        ),
        out_specs=(P(DP, EXPERT), P(EXPERT, None), P(DP, None, EXPERT), P(EXPERT, DP)),
        check_vma=False,
    )
```

```python
import functools

import jax
import jax.numpy as jnp
from jax import lax
from jax.experimental import pallas as pl
from jax.experimental.pallas import tpu as pltpu
from jax.sharding import Mesh, PartitionSpec as P

HIGH = lax.Precision.HIGHEST
F32, BF16, I16 = jnp.float32, jnp.bfloat16, jnp.int16
RANK = 64
WIDTH = 6144
BLOCK = 768
DP = ("x", "y", "h")
EXPERT = ("l", "c")
FLAT = ("x", "y", "h", "l")
LIMIT = 12 * 1024 * 1024
MOST = 60 * 1024 * 1024
TOP = 32000.0
STEP = 64.0
USED = 96

VMEM = pl.BlockSpec(memory_space=pltpu.VMEM)
SMEM = pl.BlockSpec(memory_space=pltpu.SMEM)
ANY = pl.BlockSpec(memory_space=pl.ANY)


def exchange(values, axes):
    return lax.all_to_all(values, axes, split_axis=0, concat_axis=0, tiled=True)


def swap_cores(values):
    return lax.ppermute(values, "c", [(0, 1), (1, 0)])


def three(values):
    high = values.astype(BF16)
    rest = values - high.astype(F32)
    middle = rest.astype(BF16)
    low = (rest - middle.astype(F32)).astype(BF16)
    return jnp.concatenate([high, middle, low], axis=0)


def folded(stacked):
    return stacked[:RANK] + stacked[RANK : 2 * RANK] + stacked[2 * RANK :]


def scale_of(largest):
    exponent = jnp.ceil(STEP * jnp.log2(jnp.maximum(largest, 1e-30))) + 1.0
    return exponent, jnp.exp2(exponent * (-1.0 / STEP)) * TOP


def lanes_of(shape):
    return lax.broadcasted_iota(jnp.int32, shape, 1)


def coded(values):
    return jnp.round(values).astype(jnp.int32).astype(I16)


def decoded(tile):
    wide = tile.astype(jnp.int32).astype(F32)
    return wide * (jnp.exp2(wide[:, 127:128] * (1.0 / STEP)) * (1.0 / TOP))


def eye_of(rows):
    shape = (rows, 128)
    return lax.broadcasted_iota(jnp.int32, shape, 0) == lax.broadcasted_iota(jnp.int32, shape, 1)


def packed(raw):
    exponent, factor = scale_of(jnp.max(jnp.abs(raw), axis=1, keepdims=True))
    row = jnp.sum(jnp.where(eye_of(RANK), exponent, 0.0), axis=0, keepdims=True)
    return raw * factor, jnp.concatenate([row, jnp.zeros((7, 128), F32)], axis=0)


def tagged(rows):
    used = lanes_of(rows.shape) < USED
    rows = jnp.where(used, rows, 0.0)
    exponent, factor = scale_of(jnp.max(jnp.abs(rows), axis=1, keepdims=True))
    return jnp.where(used, rows * factor, exponent)


def collected(ref):
    raw = jnp.zeros((RANK, 128), F32)
    rows = jnp.zeros((8, 128), F32)
    eye = eye_of(RANK)
    for i in range(8):
        codes = ref[i, :RANK, :].astype(jnp.int32).astype(F32)
        rest = ref[i, RANK:, :].astype(jnp.int32).astype(F32)
        exponent = jnp.sum(jnp.where(eye, rest[8:9, :], 0.0), axis=1, keepdims=True)
        raw += codes * (jnp.exp2(exponent * (1.0 / STEP)) * (1.0 / TOP))
        rows += rest[:8] * (jnp.exp2(rest[:8, 127:128] * (1.0 / STEP)) * (1.0 / TOP))
    return raw, rows


def error_kernel(block_ref, q_ref, error_ref, attn_ref, out_ref, pass_ref):
    del block_ref
    pass_ref[...] = attn_ref[...]
    out_ref[...] = folded(
        lax.dot_general(
            three(q_ref[...]), error_ref[...], (((1,), (1,)), ((), ())), preferred_element_type=F32
        )
    )


def error_share(power_t, error, core, attn_out):
    return pl.pallas_call(
        error_kernel,
        grid_spec=pltpu.PrefetchScalarGridSpec(
            num_scalar_prefetch=1,
            grid=(4,),
            in_specs=[
                pl.BlockSpec((RANK, 128), lambda i, core: (0, 0)),
                pl.BlockSpec((BLOCK, 128), lambda i, core: (2 * i + core[0], 0)),
                pl.BlockSpec((32, BLOCK), lambda i, core: (i, 0)),
            ],
            out_specs=[
                pl.BlockSpec((RANK, BLOCK), lambda i, core: (0, i)),
                pl.BlockSpec((32, BLOCK), lambda i, core: (i, 0)),
            ],
        ),
        out_shape=[
            jax.ShapeDtypeStruct((RANK, 4 * BLOCK), F32),
            jax.ShapeDtypeStruct((128, BLOCK), BF16),
        ],
        compiler_params=pltpu.CompilerParams(vmem_limit_bytes=LIMIT),
        cost_estimate=pl.CostEstimate(
            flops=2 * 192 * 128 * 3072, bytes_accessed=3072 * 512, transcendentals=0
        ),
    )(core.reshape(1), power_t, error, attn_out)


def share_kernel(
    place_ref, cq_ref, attn_ref, kept_ref, came_ref, out_ref, expert_ref, half_ref, sem
):
    copy = pltpu.make_async_copy(kept_ref, half_ref, sem)
    copy.start()
    total = jnp.sum(cq_ref[...], axis=0)
    expert_ref[...] = total[RANK:]
    from_attn = folded(jnp.dot(three(total[:RANK]), attn_ref[...], preferred_element_type=F32))
    copy.wait()
    half_ref[...] += came_ref[...]
    here = pl.ds(pl.multiple_of(place_ref[0] * BLOCK, BLOCK), BLOCK)
    half_ref[:, here] += from_attn
    lane = lanes_of((8, 128))
    for band in range(8):
        rows = slice(band * 8, band * 8 + 8)
        tiles = [half_ref[rows, t * 128 : t * 128 + 128] for t in range(24)]
        largest = functools.reduce(jnp.maximum, [jnp.abs(t) for t in tiles])
        exponent, factor = scale_of(jnp.max(largest, axis=1, keepdims=True))
        exponent = jnp.broadcast_to(exponent, (8, 128))
        factor = jnp.broadcast_to(factor, (8, 128))
        for group in range(8):
            a, b, c = (t * factor for t in tiles[group * 3 : group * 3 + 3])
            tail = jnp.where(
                lane < 32,
                pltpu.roll(a, 32, 1),
                jnp.where(lane < 64, pltpu.roll(b, 64, 1), pltpu.roll(c, 96, 1)),
            )
            a, b, c, tail = (jnp.where(lane < USED, t, exponent) for t in (a, b, c, tail))
            at = (band * 32 + group * 4) * 8
            out_ref[at : at + 16, :] = coded(jnp.concatenate([a, b], axis=0))
            out_ref[at + 16 : at + 32, :] = coded(jnp.concatenate([c, tail], axis=0))


def share_of(place, cq_all, attn_out, kept, came):
    return pl.pallas_call(
        share_kernel,
        in_specs=[SMEM, VMEM, VMEM, ANY, VMEM],
        out_specs=[VMEM, VMEM],
        out_shape=[
            jax.ShapeDtypeStruct((2048, 128), I16),
            jax.ShapeDtypeStruct((48, 128), F32),
        ],
        scratch_shapes=[pltpu.VMEM((RANK, 4 * BLOCK), F32), pltpu.SemaphoreType.DMA(())],
        compiler_params=pltpu.CompilerParams(vmem_limit_bytes=55000000),
        cost_estimate=pl.CostEstimate(
            flops=2 * 192 * 128 * 768, bytes_accessed=6000000, transcendentals=0
        ),
    )(place.reshape(1), cq_all, attn_out, kept, came)


def sum_kernel(in_ref, grad_ref, expert_ref, out_ref):
    del grad_ref, expert_ref

    def step(i, total):
        at = pl.multiple_of(i * 64, 64)
        parts = [decoded(in_ref[pl.ds(at + 16 * j, 16), :]) for j in range(4)]
        return total + ((parts[0] + parts[1]) + (parts[2] + parts[3]))

    total = lax.fori_loop(0, 32, step, jnp.zeros((16, 128), F32), unroll=4)
    total = total[:8] + total[8:]
    used = lanes_of((8, 128)) < USED
    largest = jnp.max(jnp.where(used, jnp.abs(total), 0.0), axis=1, keepdims=True)
    exponent, factor = scale_of(largest)
    tile = jnp.where(used, total * factor, exponent)
    tile = coded(jnp.concatenate([tile, tile], axis=0))
    out_ref[...] = jnp.broadcast_to(tile[None], (128, 16, 128)).reshape(2048, 128)


def summed(received, *others):
    return pl.pallas_call(
        sum_kernel,
        in_specs=[VMEM, ANY, ANY],
        out_specs=VMEM,
        out_shape=jax.ShapeDtypeStruct((2048, 128), I16),
        compiler_params=pltpu.CompilerParams(vmem_limit_bytes=LIMIT),
        cost_estimate=pl.CostEstimate(flops=1000000, bytes_accessed=1500000, transcendentals=0),
    )(received, *others)


def grad_kernel(at_ref, own_ref, other_ref, cols_ref, error_ref, out_ref):
    step = pl.program_id(0)
    mine = lax.rem(step, 2) == at_ref[1]
    attn = jnp.where(mine, own_ref[0], other_ref[0])
    grad = lax.dot_general(
        attn, cols_ref[...], (((0,), (0,)), ((), ())), preferred_element_type=F32
    ) + error_ref[...].astype(F32)
    high = grad.astype(BF16)
    out_ref[:, :128] = high
    out_ref[:, 128:] = (grad - high.astype(F32)).astype(BF16)


def grad_of(place, core, own, other, out_cols, error):
    def slot(i, at):
        return (lax.bitwise_xor(at[0], i // 2), 0, 0)

    return pl.pallas_call(
        grad_kernel,
        grid_spec=pltpu.PrefetchScalarGridSpec(
            num_scalar_prefetch=1,
            grid=(8,),
            in_specs=[
                pl.BlockSpec((1, 128, BLOCK), slot),
                pl.BlockSpec((1, 128, BLOCK), slot),
                pl.BlockSpec((128, 128), lambda i, at: (0, 0)),
                pl.BlockSpec((BLOCK, 128), lambda i, at: (i, 0)),
            ],
            out_specs=pl.BlockSpec((BLOCK, 256), lambda i, at: (i, 0)),
        ),
        out_shape=jax.ShapeDtypeStruct((WIDTH, 256), BF16),
        compiler_params=pltpu.CompilerParams(vmem_limit_bytes=LIMIT),
        cost_estimate=pl.CostEstimate(
            flops=2 * 128 * 128 * WIDTH, bytes_accessed=WIDTH * 1024, transcendentals=0
        ),
    )(jnp.stack([place, core]), own, other, out_cols, error)


def unpacked(ref, p_ref):
    lane = lanes_of((16, 128))
    for pair in range(4):
        for group in range(8):
            first, second = [], []
            for band in (2 * pair, 2 * pair + 1):
                at = (band * 32 + group * 4) * 8
                first.append(decoded(ref[at : at + 16, :]))
                second.append(decoded(ref[at + 16 : at + 32, :]))
            a = jnp.concatenate([t[:8] for t in first], axis=0)
            b = jnp.concatenate([t[8:] for t in first], axis=0)
            c = jnp.concatenate([t[:8] for t in second], axis=0)
            tail = jnp.concatenate([t[8:] for t in second], axis=0)
            for j, (tile, shift) in enumerate(((a, 96), (b, 64), (c, 32))):
                tile = jnp.where(lane < USED, tile, pltpu.roll(tail, shift, 1))
                place = group * 3 + j
                lanes = slice(128 * (place % 2), 128 * (place % 2) + 128)
                high = tile.astype(BF16)
                low = (tile - high.astype(F32)).astype(BF16)
                p_ref[place // 2, pair * 16 : pair * 16 + 16, lanes] = high
                p_ref[place // 2, RANK + pair * 16 : RANK + pair * 16 + 16, lanes] = low


def rows_of(i, core):
    return pl.ds(pl.multiple_of((2 * (i // 3) + core) * BLOCK + (i % 3) * 256, 256), 256)


def product(p_ref, grad_ref, core):
    total = jnp.zeros((128, 256), F32)
    for i in range(12):
        total += jnp.dot(p_ref[i], grad_ref[rows_of(i, core), :], preferred_element_type=F32)
    total = total[:RANK] + total[RANK:]
    return total[:, :128] + total[:, 128:]


def squared(p_ref):
    total = jnp.zeros((128, 128), F32)
    for i in range(12):
        total += lax.dot_general(
            p_ref[i], p_ref[i], (((1,), (1,)), ((), ())), preferred_element_type=F32
        )
    total = total[:RANK] + total[RANK:]
    return total[:, :RANK] + total[:, RANK:]


def mine_kernel(core_ref, codes_ref, grad_ref, raw_ref, square_ref, p_ref):
    unpacked(codes_ref, p_ref)
    raw_ref[...] = product(p_ref, grad_ref, core_ref[0])
    square_ref[...] = squared(p_ref)


def other_kernel(
    core_ref, codes_ref, grad_ref, mine_ref, square_ref, expert_ref, out_ref, gram_ref, p_ref
):
    unpacked(codes_ref, p_ref)
    gram_ref[...] = square_ref[...] + squared(p_ref)
    codes, scales = packed(mine_ref[...] + product(p_ref, grad_ref, 1 - core_ref[0]))
    codes = coded(codes)
    for i in range(8):
        rest = jnp.concatenate([tagged(expert_ref[i]), scales], axis=0)
        out_ref[i, :RANK, :] = codes
        out_ref[i, RANK:, :] = coded(rest)


SQUARE = jax.ShapeDtypeStruct((RANK, RANK), F32)
MESSAGE = jax.ShapeDtypeStruct((8, RANK + 16, 128), I16)
HALF = jax.ShapeDtypeStruct((12, 128, 256), BF16)
HALF_COST = pl.CostEstimate(flops=2 * 128 * 256 * 3072, bytes_accessed=3000000, transcendentals=0)


def mine_of(core, codes, grad):
    return pl.pallas_call(
        mine_kernel,
        in_specs=[SMEM, VMEM, VMEM],
        out_specs=[VMEM, VMEM, VMEM],
        out_shape=[jax.ShapeDtypeStruct((RANK, 128), F32), SQUARE, HALF],
        compiler_params=pltpu.CompilerParams(vmem_limit_bytes=LIMIT),
        cost_estimate=HALF_COST,
    )(core.reshape(1), codes, grad)


def other_of(core, codes, grad, raw, square, by_y):
    return pl.pallas_call(
        other_kernel,
        in_specs=[SMEM, VMEM, VMEM, VMEM, VMEM, VMEM],
        out_specs=[VMEM, VMEM, VMEM],
        out_shape=[MESSAGE, SQUARE, HALF],
        compiler_params=pltpu.CompilerParams(vmem_limit_bytes=LIMIT),
        cost_estimate=HALF_COST,
    )(core.reshape(1), codes, grad, raw, square, by_y)


def pass_kernel(in_ref, out_ref):
    raw, rows = collected(in_ref)
    codes, scales = packed(raw)
    rows = tagged(rows)
    for i in range(8):
        mine = jnp.broadcast_to(rows[i : i + 1], (8, 128))
        out_ref[i, :RANK, :] = coded(codes)
        out_ref[i, RANK:, :] = coded(jnp.concatenate([mine, scales], axis=0))


def passed(received):
    return pl.pallas_call(
        pass_kernel,
        in_specs=[VMEM],
        out_specs=VMEM,
        out_shape=MESSAGE,
        compiler_params=pltpu.CompilerParams(vmem_limit_bytes=LIMIT),
    )(received)


def final_kernel(
    at_ref, inverse_ref, sums_ref, mine_ref, other_ref, grad_ref,
    approx_ref, q_ref, error_ref, expert_ref, full_ref, p_ref, rows_ref, sem,
):
    copies = {}
    for half, ref in enumerate((mine_ref, other_ref)):
        core = at_ref[1] if half == 0 else 1 - at_ref[1]
        copies[half] = pltpu.make_async_copy(ref, p_ref.at[half], sem.at[half])
        copies[half].start()
        for i in range(4):
            here = pl.ds(pl.multiple_of((2 * i + core) * BLOCK, BLOCK), BLOCK)
            there = pl.ds((4 * half + i) * BLOCK, BLOCK)
            copies[half, i] = pltpu.make_async_copy(
                grad_ref.at[here, :], rows_ref.at[there, :], sem.at[2 + 4 * half + i]
            )
            copies[half, i].start()
    raw, rows = collected(sums_ref)
    expert_ref[...] = rows[:1, :USED]
    inverse = inverse_ref[...]
    q_t = jnp.dot(inverse, raw, precision=HIGH) * (1.0 / 64.0)
    q_ref[...] = q_t
    weights = jnp.dot(inverse.T, q_t, precision=HIGH)
    high = weights.astype(BF16)
    low = (weights - high.astype(F32)).astype(BF16)
    both = jnp.concatenate([high, low], axis=1)
    both = jnp.concatenate([both, both], axis=0)
    for half, core in ((0, at_ref[1]), (1, 1 - at_ref[1])):
        copies[half].wait()
        for i in range(12):
            if i % 3 == 0:
                copies[half, i // 3].wait()
            rows = rows_of(i, core)
            part = lax.dot_general(
                p_ref[half, i], both, (((0,), (0,)), ((), ())), preferred_element_type=F32
            )
            part = part[:, :128] + part[:, 128:]
            full_ref[rows, :] = part
            at = half * 4 * BLOCK + i * 256
            grad = rows_ref[at : at + 256, :].astype(F32)
            error_ref[rows, :] = (grad[:, :128] + grad[:, 128:] - part).astype(BF16)
    here = pl.ds(pl.multiple_of(at_ref[0] * 96, 32), 96)
    approx_ref[...] = full_ref[here, :].astype(BF16)


def final_of(data, core, inverse, sums, p_mine, p_other, grad):
    return pl.pallas_call(
        final_kernel,
        in_specs=[SMEM, VMEM, VMEM, ANY, ANY, ANY],
        out_specs=[VMEM] * 4,
        out_shape=[
            jax.ShapeDtypeStruct((96, 128), BF16),
            jax.ShapeDtypeStruct((RANK, 128), F32),
            jax.ShapeDtypeStruct((WIDTH, 128), BF16),
            jax.ShapeDtypeStruct((1, USED), F32),
        ],
        scratch_shapes=[
            pltpu.VMEM((WIDTH, 128), F32),
            pltpu.VMEM((2, 12, 128, 256), BF16),
            pltpu.VMEM((WIDTH, 256), BF16),
            pltpu.SemaphoreType.DMA((10,)),
        ],
        compiler_params=pltpu.CompilerParams(vmem_limit_bytes=55000000),
    )(jnp.stack([data, core]), inverse, sums, p_mine, p_other, grad)


def first_kernel(q_ref, cols_ref, tokens_ref, routes_ref, logits_ref, score_ref, out_ref):
    part = folded(
        lax.dot_general(
            three(q_ref[...]), cols_ref[...], (((1,), (1,)), ((), ())), preferred_element_type=F32
        )
    )
    for i in range(8):
        out_ref[i, :RANK, :] = part
    first = 1.0 / (1.0 + jnp.exp(logits_ref[1:2, :] - logits_ref[0:1, :]))
    rows = first * (1.0 - first) * (score_ref[0:1, :] - score_ref[1:2, :])
    rows = jnp.broadcast_to(rows, (8, 128))
    label = lax.broadcasted_iota(jnp.int32, (8, 128), 0)
    spread = jnp.where(routes_ref[0:1, :] == label, rows, 0.0) - jnp.where(
        routes_ref[1:2, :] == label, rows, 0.0
    )
    experts = jnp.dot(spread.astype(BF16), tokens_ref[...], preferred_element_type=F32)
    for t in range(48):
        out_ref[:, RANK + t, :] = experts[:, t * 128 : t * 128 + 128]


def first_of(power_t, out_cols, tokens, routes_t, logits_t, score_t):
    def whole(*shape):
        return pl.BlockSpec(shape, lambda i: (0,) * len(shape))

    return pl.pallas_call(
        first_kernel,
        grid=(1,),
        in_specs=[
            whole(RANK, 128),
            whole(128, 128),
            whole(128, WIDTH),
            whole(2, 128),
            whole(2, 128),
            whole(2, 128),
        ],
        out_specs=whole(8, RANK + 48, 128),
        out_shape=jax.ShapeDtypeStruct((8, RANK + 48, 128), F32),
        compiler_params=pltpu.CompilerParams(vmem_limit_bytes=MOST),
    )(power_t, out_cols, tokens, routes_t, logits_t, score_t)


def local(attn_out, out_cols, error_in, power_q, tokens, routes, route_logits, pair_score):
    error = error_in[0]
    core = lax.axis_index("c").astype(jnp.int32)
    place = lax.axis_index("l").astype(jnp.int32)
    data = (lax.axis_index("x") * 8 + lax.axis_index("y")) * 2 + lax.axis_index("h")
    power_t = power_q.T

    cq_all = exchange(
        first_of(power_t, out_cols, tokens, routes.T, route_logits.T, pair_score.T), EXPERT
    )
    given, attn_first = error_share(power_t, error, 1 - core, attn_out)
    came = swap_cores(given)
    kept, attn_here = error_share(power_t, error, core, attn_first)
    shifted = [
        lax.ppermute(attn_here, "l", [(i, i ^ k) for i in range(4)]) for k in (1, 2, 3)
    ]
    own = jnp.stack([attn_here, *shifted])
    codes, experts = share_of(place, cq_all, attn_out, kept, came)
    by_y = experts.reshape(4, 8, 2, 96).transpose(1, 0, 2, 3).reshape(8, 8, 96)
    by_y = jnp.pad(by_y, ((0, 0), (0, 0), (0, 32)))
    grad = grad_of(place, core, own, swap_cores(own), out_cols, error)
    piece = summed(exchange(codes.reshape(256, 8, 128), FLAT).reshape(2048, 128), grad, by_y)
    mine = exchange(piece.reshape(256, 8, 128), FLAT).reshape(2048, 128)
    other = swap_cores(mine)
    raw, square, p_mine = mine_of(core, mine, grad)
    send, gram, p_other = other_of(core, other, grad, raw, square, by_y)

    sums = exchange(passed(exchange(send, "y")), ("x", "h"))

    factor = jnp.linalg.cholesky(gram, symmetrize_input=False)
    inverse = lax.linalg.triangular_solve(
        factor, jnp.eye(RANK, dtype=F32), left_side=True, lower=True
    )
    approx, q_t, error_out, expert_grad = final_of(
        data.astype(jnp.int32), core, inverse, sums, p_mine, p_other, grad
    )
    return approx, q_t.T, error_out[None], expert_grad


def solution(mesh):
    fine = Mesh(mesh.devices.reshape(4, 8, 2, 4, 2), DP + EXPERT)
    everyone = P(DP + EXPERT, None)
    return jax.shard_map(
        local,
        mesh=fine,
        in_specs=(
            P(DP, EXPERT),
            P(DP, EXPERT),
            P(DP, None, EXPERT),
            P(EXPERT, None),
            everyone,
            everyone,
            everyone,
            everyone,
        ),
        out_specs=(P(DP, EXPERT), P(EXPERT, None), P(DP, None, EXPERT), P(EXPERT, DP)),
        check_vma=False,
    )
```

```python
import functools

import jax
import jax.numpy as jnp
from jax import lax
from jax.experimental import pallas as pl
from jax.experimental.pallas import tpu as pltpu
from jax.sharding import Mesh, PartitionSpec as P

HIGH = lax.Precision.HIGHEST
F32, BF16, I16 = jnp.float32, jnp.bfloat16, jnp.int16
RANK = 64
WIDTH = 6144
BLOCK = 768
DP = ("x", "y", "h")
EXPERT = ("l", "c")
FLAT = ("x", "y", "h", "l")
LIMIT = 12 * 1024 * 1024
MOST = 60 * 1024 * 1024
TOP = 32000.0
STEP = 64.0
USED = 96

VMEM = pl.BlockSpec(memory_space=pltpu.VMEM)
SMEM = pl.BlockSpec(memory_space=pltpu.SMEM)
ANY = pl.BlockSpec(memory_space=pl.ANY)


def exchange(values, axes):
    return lax.all_to_all(values, axes, split_axis=0, concat_axis=0, tiled=True)


def swap_cores(values):
    return lax.ppermute(values, "c", [(0, 1), (1, 0)])


def three(values):
    high = values.astype(BF16)
    rest = values - high.astype(F32)
    middle = rest.astype(BF16)
    low = (rest - middle.astype(F32)).astype(BF16)
    return jnp.concatenate([high, middle, low], axis=0)


def folded(stacked):
    return stacked[:RANK] + stacked[RANK : 2 * RANK] + stacked[2 * RANK :]


def scale_of(largest):
    exponent = jnp.ceil(STEP * jnp.log2(jnp.maximum(largest, 1e-30))) + 1.0
    return exponent, jnp.exp2(exponent * (-1.0 / STEP)) * TOP


def lanes_of(shape):
    return lax.broadcasted_iota(jnp.int32, shape, 1)


def coded(values):
    return jnp.round(values).astype(jnp.int32).astype(I16)


def decoded(tile):
    wide = tile.astype(jnp.int32).astype(F32)
    return wide * (jnp.exp2(wide[:, 127:128] * (1.0 / STEP)) * (1.0 / TOP))


def eye_of(rows):
    shape = (rows, 128)
    return lax.broadcasted_iota(jnp.int32, shape, 0) == lax.broadcasted_iota(jnp.int32, shape, 1)


def packed(rows):
    exponent, factor = scale_of(jnp.max(jnp.abs(rows), axis=1, keepdims=True))
    eye = eye_of(rows.shape[0])
    return rows * factor, jnp.sum(jnp.where(eye, exponent, 0.0), axis=0, keepdims=True)


def unscaled(codes, row):
    exponent = jnp.sum(jnp.where(eye_of(codes.shape[0]), row, 0.0), axis=1, keepdims=True)
    return codes * (jnp.exp2(exponent * (1.0 / STEP)) * (1.0 / TOP))


def floats(codes):
    return codes.astype(jnp.int32).astype(F32)


def tagged(rows):
    used = lanes_of(rows.shape) < USED
    rows = jnp.where(used, rows, 0.0)
    exponent, factor = scale_of(jnp.max(jnp.abs(rows), axis=1, keepdims=True))
    return jnp.where(used, rows * factor, exponent)


def collected(ref):
    raw = jnp.zeros((RANK, 128), F32)
    rows = jnp.zeros((8, 128), F32)
    for i in range(8):
        rest = floats(ref[i, RANK:, :])
        raw += unscaled(floats(ref[i, :RANK, :]), rest[8:9])
        rows += rest[:8] * (jnp.exp2(rest[:8, 127:128] * (1.0 / STEP)) * (1.0 / TOP))
    return raw, rows


def error_kernel(block_ref, q_ref, error_ref, attn_ref, other_ref, out_ref, pass_ref):
    del block_ref, other_ref
    pass_ref[...] = attn_ref[...]
    out_ref[...] = folded(
        lax.dot_general(
            three(q_ref[...]), error_ref[...], (((1,), (1,)), ((), ())), preferred_element_type=F32
        )
    )


def error_share(power_t, error, core, attn_out, other):
    return pl.pallas_call(
        error_kernel,
        grid_spec=pltpu.PrefetchScalarGridSpec(
            num_scalar_prefetch=1,
            grid=(4,),
            in_specs=[
                pl.BlockSpec((RANK, 128), lambda i, core: (0, 0)),
                pl.BlockSpec((BLOCK, 128), lambda i, core: (2 * i + core[0], 0)),
                pl.BlockSpec((32, BLOCK), lambda i, core: (i, 0)),
                ANY,
            ],
            out_specs=[
                pl.BlockSpec((RANK, BLOCK), lambda i, core: (0, i)),
                pl.BlockSpec((32, BLOCK), lambda i, core: (i, 0)),
            ],
        ),
        out_shape=[
            jax.ShapeDtypeStruct((RANK, 4 * BLOCK), F32),
            jax.ShapeDtypeStruct((128, BLOCK), BF16),
        ],
        compiler_params=pltpu.CompilerParams(vmem_limit_bytes=LIMIT),
        cost_estimate=pl.CostEstimate(
            flops=2 * 192 * 128 * 3072, bytes_accessed=3072 * 512, transcendentals=0
        ),
    )(core.reshape(1), power_t, error, attn_out, other)


def share_kernel(place_ref, cq_ref, attn_ref, kept_ref, came_ref, out_ref, expert_ref, half_ref):
    total = jnp.zeros((RANK + 48, 128), F32)
    for i in range(8):
        total += unscaled(
            floats(cq_ref[i, : RANK + 48, :]), floats(cq_ref[i, RANK + 48 :, :])[:1]
        )
    expert_ref[...] = total[RANK:]
    from_attn = folded(jnp.dot(three(total[:RANK]), attn_ref[...], preferred_element_type=F32))
    half_ref[...] = kept_ref[...] + came_ref[...]
    here = pl.ds(pl.multiple_of(place_ref[0] * BLOCK, BLOCK), BLOCK)
    half_ref[:, here] += from_attn
    lane = lanes_of((8, 128))
    for band in range(8):
        rows = slice(band * 8, band * 8 + 8)
        tiles = [half_ref[rows, t * 128 : t * 128 + 128] for t in range(24)]
        largest = functools.reduce(jnp.maximum, [jnp.abs(t) for t in tiles])
        exponent, factor = scale_of(jnp.max(largest, axis=1, keepdims=True))
        exponent = jnp.broadcast_to(exponent, (8, 128))
        factor = jnp.broadcast_to(factor, (8, 128))
        for group in range(8):
            a, b, c = (t * factor for t in tiles[group * 3 : group * 3 + 3])
            tail = jnp.where(
                lane < 32,
                pltpu.roll(a, 32, 1),
                jnp.where(lane < 64, pltpu.roll(b, 64, 1), pltpu.roll(c, 96, 1)),
            )
            a, b, c, tail = (jnp.where(lane < USED, t, exponent) for t in (a, b, c, tail))
            at = (band * 32 + group * 4) * 8
            out_ref[at : at + 16, :] = coded(jnp.concatenate([a, b], axis=0))
            out_ref[at + 16 : at + 32, :] = coded(jnp.concatenate([c, tail], axis=0))


def share_of(place, cq_all, attn_out, kept, came):
    return pl.pallas_call(
        share_kernel,
        in_specs=[SMEM, VMEM, VMEM, VMEM, VMEM],
        out_specs=[VMEM, VMEM],
        out_shape=[
            jax.ShapeDtypeStruct((2048, 128), I16),
            jax.ShapeDtypeStruct((48, 128), F32),
        ],
        scratch_shapes=[pltpu.VMEM((RANK, 4 * BLOCK), F32)],
        compiler_params=pltpu.CompilerParams(vmem_limit_bytes=LIMIT),
        cost_estimate=pl.CostEstimate(
            flops=2 * 192 * 128 * 768, bytes_accessed=6000000, transcendentals=0
        ),
    )(place.reshape(1), cq_all, attn_out, kept, came)


def sum_kernel(in_ref, grad_ref, expert_ref, out_ref, tiles_ref, sem):
    del grad_ref, expert_ref
    copies = []
    for i in range(4):
        here = pl.ds(512 * i, 512)
        copies.append(pltpu.make_async_copy(in_ref.at[here, :], tiles_ref.at[here, :], sem.at[i]))
        copies[-1].start()

    def step(i, total):
        at = pl.multiple_of(i * 64, 64)
        parts = [decoded(tiles_ref[pl.ds(at + 16 * j, 16), :]) for j in range(4)]
        return total + ((parts[0] + parts[1]) + (parts[2] + parts[3]))

    total = jnp.zeros((16, 128), F32)
    for i in range(4):
        copies[i].wait()
        total = lax.fori_loop(8 * i, 8 * i + 8, step, total, unroll=4)
    total = total[:8] + total[8:]
    used = lanes_of((8, 128)) < USED
    largest = jnp.max(jnp.where(used, jnp.abs(total), 0.0), axis=1, keepdims=True)
    exponent, factor = scale_of(largest)
    tile = jnp.where(used, total * factor, exponent)
    tile = coded(jnp.concatenate([tile, tile], axis=0))
    out_ref[...] = jnp.broadcast_to(tile[None], (128, 16, 128)).reshape(2048, 128)


def summed(received, *others):
    return pl.pallas_call(
        sum_kernel,
        in_specs=[ANY, ANY, ANY],
        out_specs=VMEM,
        out_shape=jax.ShapeDtypeStruct((2048, 128), I16),
        scratch_shapes=[pltpu.VMEM((2048, 128), I16), pltpu.SemaphoreType.DMA((4,))],
        compiler_params=pltpu.CompilerParams(vmem_limit_bytes=LIMIT),
        cost_estimate=pl.CostEstimate(flops=1000000, bytes_accessed=1500000, transcendentals=0),
    )(received, *others)


def grad_kernel(at_ref, own_ref, other_ref, cols_ref, error_ref, out_ref):
    step = pl.program_id(0)
    mine = lax.rem(step, 2) == at_ref[1]
    attn = jnp.where(mine, own_ref[0], other_ref[0])
    grad = lax.dot_general(
        attn, cols_ref[...], (((0,), (0,)), ((), ())), preferred_element_type=F32
    ) + error_ref[...].astype(F32)
    high = grad.astype(BF16)
    out_ref[:, :128] = high
    out_ref[:, 128:] = (grad - high.astype(F32)).astype(BF16)


def grad_of(place, core, own, other, out_cols, error):
    def slot(i, at):
        return (lax.rem(at[0] + 4 - i // 2, 4), 0, 0)

    return pl.pallas_call(
        grad_kernel,
        grid_spec=pltpu.PrefetchScalarGridSpec(
            num_scalar_prefetch=1,
            grid=(8,),
            in_specs=[
                pl.BlockSpec((1, 128, BLOCK), slot),
                pl.BlockSpec((1, 128, BLOCK), slot),
                pl.BlockSpec((128, 128), lambda i, at: (0, 0)),
                pl.BlockSpec((BLOCK, 128), lambda i, at: (i, 0)),
            ],
            out_specs=pl.BlockSpec((BLOCK, 256), lambda i, at: (i, 0)),
        ),
        out_shape=jax.ShapeDtypeStruct((WIDTH, 256), BF16),
        compiler_params=pltpu.CompilerParams(vmem_limit_bytes=LIMIT),
        cost_estimate=pl.CostEstimate(
            flops=2 * 128 * 128 * WIDTH, bytes_accessed=WIDTH * 1024, transcendentals=0
        ),
    )(jnp.stack([place, core]), own, other, out_cols, error)


def unpacked(ref, p_ref):
    lane = lanes_of((16, 128))
    for pair in range(4):
        for group in range(8):
            first, second = [], []
            for band in (2 * pair, 2 * pair + 1):
                at = (band * 32 + group * 4) * 8
                first.append(decoded(ref[at : at + 16, :]))
                second.append(decoded(ref[at + 16 : at + 32, :]))
            a = jnp.concatenate([t[:8] for t in first], axis=0)
            b = jnp.concatenate([t[8:] for t in first], axis=0)
            c = jnp.concatenate([t[:8] for t in second], axis=0)
            tail = jnp.concatenate([t[8:] for t in second], axis=0)
            for j, (tile, shift) in enumerate(((a, 96), (b, 64), (c, 32))):
                tile = jnp.where(lane < USED, tile, pltpu.roll(tail, shift, 1))
                place = group * 3 + j
                lanes = slice(128 * (place % 2), 128 * (place % 2) + 128)
                high = tile.astype(BF16)
                low = (tile - high.astype(F32)).astype(BF16)
                p_ref[place // 2, pair * 16 : pair * 16 + 16, lanes] = high
                p_ref[place // 2, RANK + pair * 16 : RANK + pair * 16 + 16, lanes] = low


def rows_of(i, core):
    return pl.ds(pl.multiple_of((2 * (i // 3) + core) * BLOCK + (i % 3) * 256, 256), 256)


def product(p_ref, grad_ref, core):
    total = jnp.zeros((128, 256), F32)
    for i in range(12):
        total += jnp.dot(p_ref[i], grad_ref[rows_of(i, core), :], preferred_element_type=F32)
    total = total[:RANK] + total[RANK:]
    return total[:, :128] + total[:, 128:]


def squared(p_ref):
    total = jnp.zeros((128, 128), F32)
    for i in range(12):
        total += lax.dot_general(
            p_ref[i], p_ref[i], (((1,), (1,)), ((), ())), preferred_element_type=F32
        )
    total = total[:RANK] + total[RANK:]
    return total[:, :RANK] + total[:, RANK:]


def mine_kernel(core_ref, codes_ref, grad_ref, raw_ref, square_ref, p_ref):
    unpacked(codes_ref, p_ref)
    raw_ref[...] = product(p_ref, grad_ref, core_ref[0])
    square_ref[...] = squared(p_ref)


def other_kernel(
    core_ref, codes_ref, grad_ref, mine_ref, square_ref, expert_ref, out_ref, gram_ref, p_ref
):
    unpacked(codes_ref, p_ref)
    gram_ref[...] = square_ref[...] + squared(p_ref)
    codes, scales = packed(mine_ref[...] + product(p_ref, grad_ref, 1 - core_ref[0]))
    codes = coded(codes)
    blank = jnp.zeros((7, 128), F32)
    for i in range(8):
        rest = jnp.concatenate([tagged(expert_ref[i]), scales, blank], axis=0)
        out_ref[i, :RANK, :] = codes
        out_ref[i, RANK:, :] = coded(rest)


SQUARE = jax.ShapeDtypeStruct((RANK, RANK), F32)
MESSAGE = jax.ShapeDtypeStruct((8, RANK + 16, 128), I16)
HALF = jax.ShapeDtypeStruct((12, 128, 256), BF16)
HALF_COST = pl.CostEstimate(flops=2 * 128 * 256 * 3072, bytes_accessed=3000000, transcendentals=0)


def mine_of(core, codes, grad):
    return pl.pallas_call(
        mine_kernel,
        in_specs=[SMEM, VMEM, VMEM],
        out_specs=[VMEM, VMEM, VMEM],
        out_shape=[jax.ShapeDtypeStruct((RANK, 128), F32), SQUARE, HALF],
        compiler_params=pltpu.CompilerParams(vmem_limit_bytes=LIMIT),
        cost_estimate=HALF_COST,
    )(core.reshape(1), codes, grad)


def other_of(core, codes, grad, raw, square, by_y):
    return pl.pallas_call(
        other_kernel,
        in_specs=[SMEM, VMEM, VMEM, VMEM, VMEM, VMEM],
        out_specs=[VMEM, VMEM, VMEM],
        out_shape=[MESSAGE, SQUARE, HALF],
        compiler_params=pltpu.CompilerParams(vmem_limit_bytes=LIMIT),
        cost_estimate=HALF_COST,
    )(core.reshape(1), codes, grad, raw, square, by_y)


def pass_kernel(in_ref, out_ref):
    raw, rows = collected(in_ref)
    codes, scales = packed(raw)
    codes = coded(codes)
    rows = tagged(rows)
    blank = jnp.zeros((7, 128), F32)
    for i in range(8):
        mine = jnp.broadcast_to(rows[i : i + 1], (8, 128))
        out_ref[i, :RANK, :] = codes
        out_ref[i, RANK:, :] = coded(jnp.concatenate([mine, scales, blank], axis=0))


def passed(received):
    return pl.pallas_call(
        pass_kernel,
        in_specs=[VMEM],
        out_specs=VMEM,
        out_shape=MESSAGE,
        compiler_params=pltpu.CompilerParams(vmem_limit_bytes=LIMIT),
    )(received)


def final_kernel(
    at_ref, inverse_ref, sums_ref, mine_ref, other_ref, grad_ref,
    approx_ref, q_ref, error_ref, expert_ref, full_ref,
):
    raw, rows = collected(sums_ref)
    expert_ref[...] = rows[:1, :USED]
    inverse = inverse_ref[...]
    q_t = jnp.dot(inverse, raw, precision=HIGH) * (1.0 / 64.0)
    q_ref[...] = q_t
    weights = jnp.dot(inverse.T, q_t, precision=HIGH)
    high = weights.astype(BF16)
    low = (weights - high.astype(F32)).astype(BF16)
    both = jnp.concatenate([high, low], axis=1)
    both = jnp.concatenate([both, both], axis=0)
    for ref, core in ((mine_ref, at_ref[1]), (other_ref, 1 - at_ref[1])):
        for i in range(12):
            rows = rows_of(i, core)
            part = lax.dot_general(
                ref[i], both, (((0,), (0,)), ((), ())), preferred_element_type=F32
            )
            part = part[:, :128] + part[:, 128:]
            full_ref[rows, :] = part
            grad = grad_ref[rows, :].astype(F32)
            error_ref[rows, :] = (grad[:, :128] + grad[:, 128:] - part).astype(BF16)
    here = pl.ds(pl.multiple_of(at_ref[0] * 96, 32), 96)
    approx_ref[...] = full_ref[here, :].astype(BF16)


def final_of(data, core, inverse, sums, p_mine, p_other, grad):
    return pl.pallas_call(
        final_kernel,
        in_specs=[SMEM, VMEM, VMEM, VMEM, VMEM, VMEM],
        out_specs=[VMEM] * 4,
        out_shape=[
            jax.ShapeDtypeStruct((96, 128), BF16),
            jax.ShapeDtypeStruct((RANK, 128), F32),
            jax.ShapeDtypeStruct((WIDTH, 128), BF16),
            jax.ShapeDtypeStruct((1, USED), F32),
        ],
        scratch_shapes=[pltpu.VMEM((WIDTH, 128), F32)],
        compiler_params=pltpu.CompilerParams(vmem_limit_bytes=LIMIT),
    )(jnp.stack([data, core]), inverse, sums, p_mine, p_other, grad)


def first_kernel(
    q_ref, cols_ref, tokens_ref, routes_ref, logits_ref, score_ref, out_ref, expert_ref
):
    part = folded(
        lax.dot_general(
            three(q_ref[...]), cols_ref[...], (((1,), (1,)), ((), ())), preferred_element_type=F32
        )
    )
    first = 1.0 / (1.0 + jnp.exp(logits_ref[1:2, :] - logits_ref[0:1, :]))
    rows = first * (1.0 - first) * (score_ref[0:1, :] - score_ref[1:2, :])
    rows = jnp.broadcast_to(rows, (8, 128))
    label = lax.broadcasted_iota(jnp.int32, (8, 128), 0)
    spread = jnp.where(routes_ref[0:1, :] == label, rows, 0.0) - jnp.where(
        routes_ref[1:2, :] == label, rows, 0.0
    )
    experts = jnp.dot(spread.astype(BF16), tokens_ref[...], preferred_element_type=F32)
    for t in range(48):
        expert_ref[:, t, :] = experts[:, t * 128 : t * 128 + 128]
    blank = jnp.zeros((15, 128), F32)
    for i in range(8):
        codes, scales = packed(jnp.concatenate([part, expert_ref[i]], axis=0))
        out_ref[i, : RANK + 48, :] = coded(codes)
        out_ref[i, RANK + 48 :, :] = coded(jnp.concatenate([scales, blank], axis=0))


def first_of(power_t, out_cols, tokens, routes_t, logits_t, score_t):
    def whole(*shape):
        return pl.BlockSpec(shape, lambda i: (0,) * len(shape))

    return pl.pallas_call(
        first_kernel,
        grid=(1,),
        in_specs=[
            whole(RANK, 128),
            whole(128, 128),
            whole(128, WIDTH),
            whole(2, 128),
            whole(2, 128),
            whole(2, 128),
        ],
        out_specs=whole(8, RANK + 64, 128),
        out_shape=jax.ShapeDtypeStruct((8, RANK + 64, 128), I16),
        scratch_shapes=[pltpu.VMEM((8, 48, 128), F32)],
        compiler_params=pltpu.CompilerParams(vmem_limit_bytes=MOST),
    )(power_t, out_cols, tokens, routes_t, logits_t, score_t)


def local(attn_out, out_cols, error_in, power_q, tokens, routes, route_logits, pair_score):
    error = error_in[0]
    core = lax.axis_index("c").astype(jnp.int32)
    place = lax.axis_index("l").astype(jnp.int32)
    data = (lax.axis_index("x") * 8 + lax.axis_index("y")) * 2 + lax.axis_index("h")
    power_t = power_q.T

    first = first_of(power_t, out_cols, tokens, routes.T, route_logits.T, pair_score.T)
    cq_all = exchange(first, EXPERT)

    given, attn_first = error_share(power_t, error, 1 - core, attn_out, first)
    came = swap_cores(given)
    kept, attn_here = error_share(power_t, error, core, attn_first, first)
    shifted = [
        lax.ppermute(attn_here, "l", [(i, (i + k) % 4) for i in range(4)]) for k in (1, 2, 3)
    ]
    own = jnp.stack([attn_here, *shifted])
    codes, experts = share_of(place, cq_all, attn_out, kept, came)
    by_y = experts.reshape(4, 8, 2, 96).transpose(1, 0, 2, 3).reshape(8, 8, 96)
    by_y = jnp.pad(by_y, ((0, 0), (0, 0), (0, 32)))
    grad = grad_of(place, core, own, swap_cores(own), out_cols, error)
    piece = summed(exchange(codes.reshape(256, 8, 128), FLAT).reshape(2048, 128), grad, by_y)
    mine = exchange(piece.reshape(256, 8, 128), FLAT).reshape(2048, 128)
    other = swap_cores(mine)
    raw, square, p_mine = mine_of(core, mine, grad)
    send, gram, p_other = other_of(core, other, grad, raw, square, by_y)

    sums = exchange(passed(exchange(send, "y")), ("x", "h"))

    factor = jnp.linalg.cholesky(gram, symmetrize_input=False)
    inverse = lax.linalg.triangular_solve(
        factor, jnp.eye(RANK, dtype=F32), left_side=True, lower=True
    )
    approx, q_t, error_out, expert_grad = final_of(
        data.astype(jnp.int32), core, inverse, sums, p_mine, p_other, grad
    )
    return approx, q_t.T, error_out[None], expert_grad


def solution(mesh):
    fine = Mesh(mesh.devices.reshape(4, 8, 2, 4, 2), DP + EXPERT)
    everyone = P(DP + EXPERT, None)
    return jax.shard_map(
        local,
        mesh=fine,
        in_specs=(
            P(DP, EXPERT),
            P(DP, EXPERT),
            P(DP, None, EXPERT),
            P(EXPERT, None),
            everyone,
            everyone,
            everyone,
            everyone,
        ),
        out_specs=(P(DP, EXPERT), P(EXPERT, None), P(DP, None, EXPERT), P(EXPERT, DP)),
        check_vma=False,
    )
```

```python
import functools

import jax
import jax.numpy as jnp
from jax import lax
from jax.experimental import pallas as pl
from jax.experimental.pallas import tpu as pltpu
from jax.sharding import Mesh, PartitionSpec as P

HIGH = lax.Precision.HIGHEST
F32, BF16, I16 = jnp.float32, jnp.bfloat16, jnp.int16
RANK = 64
WIDTH = 6144
BLOCK = 768
DP = ("x", "y", "h")
EXPERT = ("l", "c")
FLAT = ("x", "y", "h", "l")
LIMIT = 12 * 1024 * 1024
MOST = 60 * 1024 * 1024
TOP = 32000.0
STEP = 64.0
USED = 96

VMEM = pl.BlockSpec(memory_space=pltpu.VMEM)
SMEM = pl.BlockSpec(memory_space=pltpu.SMEM)
ANY = pl.BlockSpec(memory_space=pl.ANY)


def exchange(values, axes):
    return lax.all_to_all(values, axes, split_axis=0, concat_axis=0, tiled=True)


def swap_cores(values):
    return lax.ppermute(values, "c", [(0, 1), (1, 0)])


def three(values):
    high = values.astype(BF16)
    rest = values - high.astype(F32)
    middle = rest.astype(BF16)
    low = (rest - middle.astype(F32)).astype(BF16)
    return jnp.concatenate([high, middle, low], axis=0)


def folded(stacked):
    return stacked[:RANK] + stacked[RANK : 2 * RANK] + stacked[2 * RANK :]


def scale_of(largest):
    exponent = jnp.ceil(STEP * jnp.log2(jnp.maximum(largest, 1e-30))) + 1.0
    return exponent, jnp.exp2(exponent * (-1.0 / STEP)) * TOP


def lanes_of(shape):
    return lax.broadcasted_iota(jnp.int32, shape, 1)


def coded(values):
    return jnp.round(values).astype(jnp.int32).astype(I16)


def decoded(tile):
    wide = tile.astype(jnp.int32).astype(F32)
    return wide * (jnp.exp2(wide[:, 127:128] * (1.0 / STEP)) * (1.0 / TOP))


def eye_of(rows):
    shape = (rows, 128)
    return lax.broadcasted_iota(jnp.int32, shape, 0) == lax.broadcasted_iota(jnp.int32, shape, 1)


def packed(rows):
    exponent, factor = scale_of(jnp.max(jnp.abs(rows), axis=1, keepdims=True))
    eye = eye_of(rows.shape[0])
    return rows * factor, jnp.sum(jnp.where(eye, exponent, 0.0), axis=0, keepdims=True)


def unscaled(codes, row):
    exponent = jnp.sum(jnp.where(eye_of(codes.shape[0]), row, 0.0), axis=1, keepdims=True)
    return codes * (jnp.exp2(exponent * (1.0 / STEP)) * (1.0 / TOP))


def floats(codes):
    return codes.astype(jnp.int32).astype(F32)


def tagged(rows):
    used = lanes_of(rows.shape) < USED
    rows = jnp.where(used, rows, 0.0)
    exponent, factor = scale_of(jnp.max(jnp.abs(rows), axis=1, keepdims=True))
    return jnp.where(used, rows * factor, exponent)


def collected(ref):
    raw = jnp.zeros((RANK, 128), F32)
    rows = jnp.zeros((8, 128), F32)
    for i in range(8):
        rest = floats(ref[i, RANK:, :])
        raw += unscaled(floats(ref[i, :RANK, :]), rest[8:9])
        rows += rest[:8] * (jnp.exp2(rest[:8, 127:128] * (1.0 / STEP)) * (1.0 / TOP))
    return raw, rows


def error_kernel(block_ref, q_ref, error_ref, attn_ref, other_ref, out_ref, pass_ref):
    del block_ref, other_ref
    pass_ref[...] = attn_ref[...]
    out_ref[...] = folded(
        lax.dot_general(
            three(q_ref[...]), error_ref[...], (((1,), (1,)), ((), ())), preferred_element_type=F32
        )
    )


def error_share(power_t, error, core, attn_out, other):
    return pl.pallas_call(
        error_kernel,
        grid_spec=pltpu.PrefetchScalarGridSpec(
            num_scalar_prefetch=1,
            grid=(4,),
            in_specs=[
                pl.BlockSpec((RANK, 128), lambda i, core: (0, 0)),
                pl.BlockSpec((BLOCK, 128), lambda i, core: (2 * i + core[0], 0)),
                pl.BlockSpec((32, BLOCK), lambda i, core: (i, 0)),
                ANY,
            ],
            out_specs=[
                pl.BlockSpec((RANK, BLOCK), lambda i, core: (0, i)),
                pl.BlockSpec((32, BLOCK), lambda i, core: (i, 0)),
            ],
        ),
        out_shape=[
            jax.ShapeDtypeStruct((RANK, 4 * BLOCK), F32),
            jax.ShapeDtypeStruct((128, BLOCK), BF16),
        ],
        compiler_params=pltpu.CompilerParams(vmem_limit_bytes=LIMIT),
        cost_estimate=pl.CostEstimate(
            flops=2 * 192 * 128 * 3072, bytes_accessed=3072 * 512, transcendentals=0
        ),
    )(core.reshape(1), power_t, error, attn_out, other)


def share_kernel(
    place_ref, core_ref, cq_ref, attn_ref, q_ref, error_ref, came_ref,
    out_ref, expert_ref, half_ref,
):
    total = jnp.zeros((RANK + 48, 128), F32)
    for i in range(8):
        total += unscaled(
            floats(cq_ref[i, : RANK + 48, :]), floats(cq_ref[i, RANK + 48 :, :])[:1]
        )
    expert_ref[...] = total[RANK:]
    from_attn = folded(jnp.dot(three(total[:RANK]), attn_ref[...], preferred_element_type=F32))
    parts = three(q_ref[...])
    for i in range(4):
        rows = pl.ds(pl.multiple_of((2 * i + core_ref[0]) * BLOCK, BLOCK), BLOCK)
        kept = lax.dot_general(
            parts, error_ref[rows, :], (((1,), (1,)), ((), ())), preferred_element_type=F32
        )
        lanes = slice(i * BLOCK, i * BLOCK + BLOCK)
        half_ref[:, lanes] = folded(kept) + came_ref[:, lanes]
    here = pl.ds(pl.multiple_of(place_ref[0] * BLOCK, BLOCK), BLOCK)
    half_ref[:, here] += from_attn
    lane = lanes_of((8, 128))
    for band in range(8):
        rows = slice(band * 8, band * 8 + 8)
        tiles = [half_ref[rows, t * 128 : t * 128 + 128] for t in range(24)]
        largest = functools.reduce(jnp.maximum, [jnp.abs(t) for t in tiles])
        exponent, factor = scale_of(jnp.max(largest, axis=1, keepdims=True))
        exponent = jnp.broadcast_to(exponent, (8, 128))
        factor = jnp.broadcast_to(factor, (8, 128))
        for group in range(8):
            a, b, c = (t * factor for t in tiles[group * 3 : group * 3 + 3])
            tail = jnp.where(
                lane < 32,
                pltpu.roll(a, 32, 1),
                jnp.where(lane < 64, pltpu.roll(b, 64, 1), pltpu.roll(c, 96, 1)),
            )
            a, b, c, tail = (jnp.where(lane < USED, t, exponent) for t in (a, b, c, tail))
            at = (band * 32 + group * 4) * 8
            out_ref[at : at + 16, :] = coded(jnp.concatenate([a, b], axis=0))
            out_ref[at + 16 : at + 32, :] = coded(jnp.concatenate([c, tail], axis=0))


def share_of(place, core, cq_all, attn_out, power_t, error, came):
    return pl.pallas_call(
        share_kernel,
        in_specs=[SMEM, SMEM, VMEM, VMEM, VMEM, VMEM, VMEM],
        out_specs=[VMEM, VMEM],
        out_shape=[
            jax.ShapeDtypeStruct((2048, 128), I16),
            jax.ShapeDtypeStruct((48, 128), F32),
        ],
        scratch_shapes=[pltpu.VMEM((RANK, 4 * BLOCK), F32)],
        compiler_params=pltpu.CompilerParams(vmem_limit_bytes=LIMIT),
        cost_estimate=pl.CostEstimate(
            flops=2 * 192 * 128 * 768, bytes_accessed=6000000, transcendentals=0
        ),
    )(place.reshape(1), core.reshape(1), cq_all, attn_out, power_t, error, came)


def sum_kernel(in_ref, grad_ref, expert_ref, out_ref, tiles_ref, sem):
    del grad_ref, expert_ref
    copies = []
    for i in range(4):
        here = pl.ds(512 * i, 512)
        copies.append(pltpu.make_async_copy(in_ref.at[here, :], tiles_ref.at[here, :], sem.at[i]))
        copies[-1].start()

    def step(i, total):
        at = pl.multiple_of(i * 64, 64)
        parts = [decoded(tiles_ref[pl.ds(at + 16 * j, 16), :]) for j in range(4)]
        return total + ((parts[0] + parts[1]) + (parts[2] + parts[3]))

    total = jnp.zeros((16, 128), F32)
    for i in range(4):
        copies[i].wait()
        total = lax.fori_loop(8 * i, 8 * i + 8, step, total, unroll=4)
    total = total[:8] + total[8:]
    used = lanes_of((8, 128)) < USED
    largest = jnp.max(jnp.where(used, jnp.abs(total), 0.0), axis=1, keepdims=True)
    exponent, factor = scale_of(largest)
    tile = jnp.where(used, total * factor, exponent)
    tile = coded(jnp.concatenate([tile, tile], axis=0))
    out_ref[...] = jnp.broadcast_to(tile[None], (128, 16, 128)).reshape(2048, 128)


def summed(received, *others):
    return pl.pallas_call(
        sum_kernel,
        in_specs=[ANY, ANY, ANY],
        out_specs=VMEM,
        out_shape=jax.ShapeDtypeStruct((2048, 128), I16),
        scratch_shapes=[pltpu.VMEM((2048, 128), I16), pltpu.SemaphoreType.DMA((4,))],
        compiler_params=pltpu.CompilerParams(vmem_limit_bytes=LIMIT),
        cost_estimate=pl.CostEstimate(flops=1000000, bytes_accessed=1500000, transcendentals=0),
    )(received, *others)


def grad_kernel(at_ref, own_ref, other_ref, cols_ref, error_ref, out_ref):
    step = pl.program_id(0)
    mine = lax.rem(step, 2) == at_ref[1]
    attn = jnp.where(mine, own_ref[0], other_ref[0])
    grad = lax.dot_general(
        attn, cols_ref[...], (((0,), (0,)), ((), ())), preferred_element_type=F32
    ) + error_ref[...].astype(F32)
    high = grad.astype(BF16)
    out_ref[:, :128] = high
    out_ref[:, 128:] = (grad - high.astype(F32)).astype(BF16)


def grad_of(place, core, own, other, out_cols, error):
    def slot(i, at):
        return (lax.rem(at[0] + 4 - i // 2, 4), 0, 0)

    return pl.pallas_call(
        grad_kernel,
        grid_spec=pltpu.PrefetchScalarGridSpec(
            num_scalar_prefetch=1,
            grid=(8,),
            in_specs=[
                pl.BlockSpec((1, 128, BLOCK), slot),
                pl.BlockSpec((1, 128, BLOCK), slot),
                pl.BlockSpec((128, 128), lambda i, at: (0, 0)),
                pl.BlockSpec((BLOCK, 128), lambda i, at: (i, 0)),
            ],
            out_specs=pl.BlockSpec((BLOCK, 256), lambda i, at: (i, 0)),
        ),
        out_shape=jax.ShapeDtypeStruct((WIDTH, 256), BF16),
        compiler_params=pltpu.CompilerParams(vmem_limit_bytes=LIMIT),
        cost_estimate=pl.CostEstimate(
            flops=2 * 128 * 128 * WIDTH, bytes_accessed=WIDTH * 1024, transcendentals=0
        ),
    )(jnp.stack([place, core]), own, other, out_cols, error)


def unpacked(ref, p_ref):
    lane = lanes_of((16, 128))
    for pair in range(4):
        for group in range(8):
            first, second = [], []
            for band in (2 * pair, 2 * pair + 1):
                at = (band * 32 + group * 4) * 8
                first.append(decoded(ref[at : at + 16, :]))
                second.append(decoded(ref[at + 16 : at + 32, :]))
            a = jnp.concatenate([t[:8] for t in first], axis=0)
            b = jnp.concatenate([t[8:] for t in first], axis=0)
            c = jnp.concatenate([t[:8] for t in second], axis=0)
            tail = jnp.concatenate([t[8:] for t in second], axis=0)
            for j, (tile, shift) in enumerate(((a, 96), (b, 64), (c, 32))):
                tile = jnp.where(lane < USED, tile, pltpu.roll(tail, shift, 1))
                place = group * 3 + j
                lanes = slice(128 * (place % 2), 128 * (place % 2) + 128)
                high = tile.astype(BF16)
                low = (tile - high.astype(F32)).astype(BF16)
                p_ref[place // 2, pair * 16 : pair * 16 + 16, lanes] = high
                p_ref[place // 2, RANK + pair * 16 : RANK + pair * 16 + 16, lanes] = low


def rows_of(i, core):
    return pl.ds(pl.multiple_of((2 * (i // 3) + core) * BLOCK + (i % 3) * 256, 256), 256)


def product(p_ref, grad_ref, core):
    total = jnp.zeros((128, 256), F32)
    for i in range(12):
        total += jnp.dot(p_ref[i], grad_ref[rows_of(i, core), :], preferred_element_type=F32)
    total = total[:RANK] + total[RANK:]
    return total[:, :128] + total[:, 128:]


def squared(p_ref):
    total = jnp.zeros((128, 128), F32)
    for i in range(12):
        total += lax.dot_general(
            p_ref[i], p_ref[i], (((1,), (1,)), ((), ())), preferred_element_type=F32
        )
    total = total[:RANK] + total[RANK:]
    return total[:, :RANK] + total[:, RANK:]


def mine_kernel(core_ref, codes_ref, grad_ref, raw_ref, square_ref, p_ref):
    unpacked(codes_ref, p_ref)
    raw_ref[...] = product(p_ref, grad_ref, core_ref[0])
    square_ref[...] = squared(p_ref)


def other_kernel(
    core_ref, codes_ref, grad_ref, mine_ref, square_ref, expert_ref, out_ref, gram_ref, p_ref
):
    unpacked(codes_ref, p_ref)
    gram_ref[...] = square_ref[...] + squared(p_ref)
    codes, scales = packed(mine_ref[...] + product(p_ref, grad_ref, 1 - core_ref[0]))
    codes = coded(codes)
    blank = jnp.zeros((7, 128), F32)
    for i in range(8):
        rest = jnp.concatenate([tagged(expert_ref[i]), scales, blank], axis=0)
        out_ref[i, :RANK, :] = codes
        out_ref[i, RANK:, :] = coded(rest)


SQUARE = jax.ShapeDtypeStruct((RANK, RANK), F32)
MESSAGE = jax.ShapeDtypeStruct((8, RANK + 16, 128), I16)
HALF = jax.ShapeDtypeStruct((12, 128, 256), BF16)
HALF_COST = pl.CostEstimate(flops=2 * 128 * 256 * 3072, bytes_accessed=3000000, transcendentals=0)


def mine_of(core, codes, grad):
    return pl.pallas_call(
        mine_kernel,
        in_specs=[SMEM, VMEM, VMEM],
        out_specs=[VMEM, VMEM, VMEM],
        out_shape=[jax.ShapeDtypeStruct((RANK, 128), F32), SQUARE, HALF],
        compiler_params=pltpu.CompilerParams(vmem_limit_bytes=LIMIT),
        cost_estimate=HALF_COST,
    )(core.reshape(1), codes, grad)


def other_of(core, codes, grad, raw, square, by_y):
    return pl.pallas_call(
        other_kernel,
        in_specs=[SMEM, VMEM, VMEM, VMEM, VMEM, VMEM],
        out_specs=[VMEM, VMEM, VMEM],
        out_shape=[MESSAGE, SQUARE, HALF],
        compiler_params=pltpu.CompilerParams(vmem_limit_bytes=LIMIT),
        cost_estimate=HALF_COST,
    )(core.reshape(1), codes, grad, raw, square, by_y)


def pass_kernel(in_ref, out_ref):
    raw, rows = collected(in_ref)
    codes, scales = packed(raw)
    codes = coded(codes)
    rows = tagged(rows)
    blank = jnp.zeros((7, 128), F32)
    for i in range(8):
        mine = jnp.broadcast_to(rows[i : i + 1], (8, 128))
        out_ref[i, :RANK, :] = codes
        out_ref[i, RANK:, :] = coded(jnp.concatenate([mine, scales, blank], axis=0))


def passed(received):
    return pl.pallas_call(
        pass_kernel,
        in_specs=[VMEM],
        out_specs=VMEM,
        out_shape=MESSAGE,
        compiler_params=pltpu.CompilerParams(vmem_limit_bytes=LIMIT),
    )(received)


def final_kernel(
    at_ref, inverse_ref, sums_ref, mine_ref, other_ref, grad_ref,
    approx_ref, q_ref, error_ref, expert_ref, full_ref,
):
    raw, rows = collected(sums_ref)
    expert_ref[...] = rows[:1, :USED]
    inverse = inverse_ref[...]
    q_t = jnp.dot(inverse, raw, precision=HIGH) * (1.0 / 64.0)
    q_ref[...] = q_t
    weights = jnp.dot(inverse.T, q_t, precision=HIGH)
    high = weights.astype(BF16)
    low = (weights - high.astype(F32)).astype(BF16)
    both = jnp.concatenate([high, low], axis=1)
    both = jnp.concatenate([both, both], axis=0)
    for ref, core in ((mine_ref, at_ref[1]), (other_ref, 1 - at_ref[1])):
        for i in range(12):
            rows = rows_of(i, core)
            part = lax.dot_general(
                ref[i], both, (((0,), (0,)), ((), ())), preferred_element_type=F32
            )
            part = part[:, :128] + part[:, 128:]
            full_ref[rows, :] = part
            grad = grad_ref[rows, :].astype(F32)
            error_ref[rows, :] = (grad[:, :128] + grad[:, 128:] - part).astype(BF16)
    here = pl.ds(pl.multiple_of(at_ref[0] * 96, 32), 96)
    approx_ref[...] = full_ref[here, :].astype(BF16)


def final_of(data, core, inverse, sums, p_mine, p_other, grad):
    return pl.pallas_call(
        final_kernel,
        in_specs=[SMEM, VMEM, VMEM, VMEM, VMEM, VMEM],
        out_specs=[VMEM] * 4,
        out_shape=[
            jax.ShapeDtypeStruct((96, 128), BF16),
            jax.ShapeDtypeStruct((RANK, 128), F32),
            jax.ShapeDtypeStruct((WIDTH, 128), BF16),
            jax.ShapeDtypeStruct((1, USED), F32),
        ],
        scratch_shapes=[pltpu.VMEM((WIDTH, 128), F32)],
        compiler_params=pltpu.CompilerParams(vmem_limit_bytes=LIMIT),
    )(jnp.stack([data, core]), inverse, sums, p_mine, p_other, grad)


def first_kernel(
    q_ref, cols_ref, tokens_ref, routes_ref, logits_ref, score_ref, out_ref, expert_ref
):
    part = folded(
        lax.dot_general(
            three(q_ref[...]), cols_ref[...], (((1,), (1,)), ((), ())), preferred_element_type=F32
        )
    )
    first = 1.0 / (1.0 + jnp.exp(logits_ref[1:2, :] - logits_ref[0:1, :]))
    rows = first * (1.0 - first) * (score_ref[0:1, :] - score_ref[1:2, :])
    rows = jnp.broadcast_to(rows, (8, 128))
    label = lax.broadcasted_iota(jnp.int32, (8, 128), 0)
    spread = jnp.where(routes_ref[0:1, :] == label, rows, 0.0) - jnp.where(
        routes_ref[1:2, :] == label, rows, 0.0
    )
    experts = jnp.dot(spread.astype(BF16), tokens_ref[...], preferred_element_type=F32)
    for t in range(48):
        expert_ref[:, t, :] = experts[:, t * 128 : t * 128 + 128]
    blank = jnp.zeros((15, 128), F32)
    for i in range(8):
        codes, scales = packed(jnp.concatenate([part, expert_ref[i]], axis=0))
        out_ref[i, : RANK + 48, :] = coded(codes)
        out_ref[i, RANK + 48 :, :] = coded(jnp.concatenate([scales, blank], axis=0))


def first_of(power_t, out_cols, tokens, routes_t, logits_t, score_t):
    def whole(*shape):
        return pl.BlockSpec(shape, lambda i: (0,) * len(shape))

    return pl.pallas_call(
        first_kernel,
        grid=(1,),
        in_specs=[
            whole(RANK, 128),
            whole(128, 128),
            whole(128, WIDTH),
            whole(2, 128),
            whole(2, 128),
            whole(2, 128),
        ],
        out_specs=whole(8, RANK + 64, 128),
        out_shape=jax.ShapeDtypeStruct((8, RANK + 64, 128), I16),
        scratch_shapes=[pltpu.VMEM((8, 48, 128), F32)],
        compiler_params=pltpu.CompilerParams(vmem_limit_bytes=MOST),
    )(power_t, out_cols, tokens, routes_t, logits_t, score_t)


def local(attn_out, out_cols, error_in, power_q, tokens, routes, route_logits, pair_score):
    error = error_in[0]
    core = lax.axis_index("c").astype(jnp.int32)
    place = lax.axis_index("l").astype(jnp.int32)
    data = (lax.axis_index("x") * 8 + lax.axis_index("y")) * 2 + lax.axis_index("h")
    power_t = power_q.T

    first = first_of(power_t, out_cols, tokens, routes.T, route_logits.T, pair_score.T)
    cq_all = exchange(first, EXPERT)

    given, attn_here = error_share(power_t, error, 1 - core, attn_out, first)
    came = swap_cores(given)
    shifted = [
        lax.ppermute(attn_here, "l", [(i, (i + k) % 4) for i in range(4)]) for k in (1, 2, 3)
    ]
    own = jnp.stack([attn_here, *shifted])
    codes, experts = share_of(place, core, cq_all, attn_out, power_t, error, came)
    by_y = experts.reshape(4, 8, 2, 96).transpose(1, 0, 2, 3).reshape(8, 8, 96)
    by_y = jnp.pad(by_y, ((0, 0), (0, 0), (0, 32)))
    grad = grad_of(place, core, own, swap_cores(own), out_cols, error)
    piece = summed(exchange(codes.reshape(256, 8, 128), FLAT).reshape(2048, 128), grad, by_y)
    mine = exchange(piece.reshape(256, 8, 128), FLAT).reshape(2048, 128)
    other = swap_cores(mine)
    raw, square, p_mine = mine_of(core, mine, grad)
    send, gram, p_other = other_of(core, other, grad, raw, square, by_y)

    sums = exchange(passed(exchange(send, "y")), ("x", "h"))

    factor = jnp.linalg.cholesky(gram, symmetrize_input=False)
    inverse = lax.linalg.triangular_solve(
        factor, jnp.eye(RANK, dtype=F32), left_side=True, lower=True
    )
    approx, q_t, error_out, expert_grad = final_of(
        data.astype(jnp.int32), core, inverse, sums, p_mine, p_other, grad
    )
    return approx, q_t.T, error_out[None], expert_grad


def solution(mesh):
    fine = Mesh(mesh.devices.reshape(4, 8, 2, 4, 2), DP + EXPERT)
    everyone = P(DP + EXPERT, None)
    return jax.shard_map(
        local,
        mesh=fine,
        in_specs=(
            P(DP, EXPERT),
            P(DP, EXPERT),
            P(DP, None, EXPERT),
            P(EXPERT, None),
            everyone,
            everyone,
            everyone,
            everyone,
        ),
        out_specs=(P(DP, EXPERT), P(EXPERT, None), P(DP, None, EXPERT), P(EXPERT, DP)),
        check_vma=False,
    )
```

```python
import functools

import jax
import jax.numpy as jnp
from jax import lax
from jax.experimental import pallas as pl
from jax.experimental.pallas import tpu as pltpu
from jax.sharding import Mesh, PartitionSpec as P

HIGH = lax.Precision.HIGHEST
F32, BF16, I16 = jnp.float32, jnp.bfloat16, jnp.int16
RANK = 64
WIDTH = 6144
BLOCK = 768
DP = ("x", "y", "h")
EXPERT = ("l", "c")
FLAT = ("x", "y", "h", "l")
LIMIT = 12 * 1024 * 1024
MOST = 60 * 1024 * 1024
TOP = 32000.0
STEP = 64.0
USED = 96

VMEM = pl.BlockSpec(memory_space=pltpu.VMEM)
SMEM = pl.BlockSpec(memory_space=pltpu.SMEM)
ANY = pl.BlockSpec(memory_space=pl.ANY)


def exchange(values, axes):
    return lax.all_to_all(values, axes, split_axis=0, concat_axis=0, tiled=True)


def swap_cores(values):
    return lax.ppermute(values, "c", [(0, 1), (1, 0)])


def three(values):
    high = values.astype(BF16)
    rest = values - high.astype(F32)
    middle = rest.astype(BF16)
    low = (rest - middle.astype(F32)).astype(BF16)
    return jnp.concatenate([high, middle, low], axis=0)


def folded(stacked):
    return stacked[:RANK] + stacked[RANK : 2 * RANK] + stacked[2 * RANK :]


def scale_of(largest):
    exponent = jnp.ceil(STEP * jnp.log2(jnp.maximum(largest, 1e-30))) + 1.0
    return exponent, jnp.exp2(exponent * (-1.0 / STEP)) * TOP


def lanes_of(shape):
    return lax.broadcasted_iota(jnp.int32, shape, 1)


def coded(values):
    return jnp.round(values).astype(jnp.int32).astype(I16)


def decoded(tile):
    wide = tile.astype(jnp.int32).astype(F32)
    return wide * (jnp.exp2(wide[:, 127:128] * (1.0 / STEP)) * (1.0 / TOP))


def eye_of(rows):
    shape = (rows, 128)
    return lax.broadcasted_iota(jnp.int32, shape, 0) == lax.broadcasted_iota(jnp.int32, shape, 1)


def packed(rows):
    exponent, factor = scale_of(jnp.max(jnp.abs(rows), axis=1, keepdims=True))
    eye = eye_of(rows.shape[0])
    return rows * factor, jnp.sum(jnp.where(eye, exponent, 0.0), axis=0, keepdims=True)


def unscaled(codes, row):
    exponent = jnp.sum(jnp.where(eye_of(codes.shape[0]), row, 0.0), axis=1, keepdims=True)
    return codes * (jnp.exp2(exponent * (1.0 / STEP)) * (1.0 / TOP))


def floats(codes):
    return codes.astype(jnp.int32).astype(F32)


def tagged(rows):
    used = lanes_of(rows.shape) < USED
    rows = jnp.where(used, rows, 0.0)
    exponent, factor = scale_of(jnp.max(jnp.abs(rows), axis=1, keepdims=True))
    return jnp.where(used, rows * factor, exponent)


def collected(ref):
    raw = jnp.zeros((RANK, 128), F32)
    rows = jnp.zeros((8, 128), F32)
    for i in range(8):
        rest = floats(ref[i, RANK:, :])
        raw += unscaled(floats(ref[i, :RANK, :]), rest[8:9])
        rows += rest[:8] * (jnp.exp2(rest[:8, 127:128] * (1.0 / STEP)) * (1.0 / TOP))
    return raw, rows


def error_kernel(block_ref, q_ref, error_ref, attn_ref, other_ref, out_ref, pass_ref):
    del block_ref, other_ref
    pass_ref[...] = attn_ref[...]
    out_ref[...] = folded(
        lax.dot_general(
            three(q_ref[...]), error_ref[...], (((1,), (1,)), ((), ())), preferred_element_type=F32
        )
    )


def error_share(power_t, error, core, attn_out, other):
    return pl.pallas_call(
        error_kernel,
        grid_spec=pltpu.PrefetchScalarGridSpec(
            num_scalar_prefetch=1,
            grid=(4,),
            in_specs=[
                pl.BlockSpec((RANK, 128), lambda i, core: (0, 0)),
                pl.BlockSpec((BLOCK, 128), lambda i, core: (2 * i + core[0], 0)),
                pl.BlockSpec((32, BLOCK), lambda i, core: (i, 0)),
                ANY,
            ],
            out_specs=[
                pl.BlockSpec((RANK, BLOCK), lambda i, core: (0, i)),
                pl.BlockSpec((32, BLOCK), lambda i, core: (i, 0)),
            ],
        ),
        out_shape=[
            jax.ShapeDtypeStruct((RANK, 4 * BLOCK), F32),
            jax.ShapeDtypeStruct((128, BLOCK), BF16),
        ],
        compiler_params=pltpu.CompilerParams(vmem_limit_bytes=LIMIT),
        cost_estimate=pl.CostEstimate(
            flops=2 * 192 * 128 * 3072, bytes_accessed=3072 * 512, transcendentals=0
        ),
    )(core.reshape(1), power_t, error, attn_out, other)


def share_kernel(
    place_ref, core_ref, cq_ref, attn_ref, q_ref, error_ref, came_ref,
    out_ref, expert_ref, half_ref,
):
    total = jnp.zeros((RANK + 48, 128), F32)
    for i in range(8):
        total += unscaled(
            floats(cq_ref[i, : RANK + 48, :]), floats(cq_ref[i, RANK + 48 :, :])[:1]
        )
    expert_ref[...] = total[RANK:]
    from_attn = folded(jnp.dot(three(total[:RANK]), attn_ref[...], preferred_element_type=F32))
    parts = three(q_ref[...])
    for i in range(4):
        rows = pl.ds(pl.multiple_of((2 * i + core_ref[0]) * BLOCK, BLOCK), BLOCK)
        kept = lax.dot_general(
            parts, error_ref[rows, :], (((1,), (1,)), ((), ())), preferred_element_type=F32
        )
        lanes = slice(i * BLOCK, i * BLOCK + BLOCK)
        half_ref[:, lanes] = folded(kept) + came_ref[:, lanes]
    here = pl.ds(pl.multiple_of(place_ref[0] * BLOCK, BLOCK), BLOCK)
    half_ref[:, here] += from_attn
    lane = lanes_of((8, 128))
    for band in range(8):
        rows = slice(band * 8, band * 8 + 8)
        tiles = [half_ref[rows, t * 128 : t * 128 + 128] for t in range(24)]
        largest = functools.reduce(jnp.maximum, [jnp.abs(t) for t in tiles])
        exponent, factor = scale_of(jnp.max(largest, axis=1, keepdims=True))
        exponent = jnp.broadcast_to(exponent, (8, 128))
        factor = jnp.broadcast_to(factor, (8, 128))
        for group in range(8):
            a, b, c = (t * factor for t in tiles[group * 3 : group * 3 + 3])
            tail = jnp.where(
                lane < 32,
                pltpu.roll(a, 32, 1),
                jnp.where(lane < 64, pltpu.roll(b, 64, 1), pltpu.roll(c, 96, 1)),
            )
            a, b, c, tail = (jnp.where(lane < USED, t, exponent) for t in (a, b, c, tail))
            at = (band * 32 + group * 4) * 8
            out_ref[at : at + 16, :] = coded(jnp.concatenate([a, b], axis=0))
            out_ref[at + 16 : at + 32, :] = coded(jnp.concatenate([c, tail], axis=0))


def share_of(place, core, cq_all, attn_out, power_t, error, came):
    return pl.pallas_call(
        share_kernel,
        in_specs=[SMEM, SMEM, VMEM, VMEM, VMEM, VMEM, VMEM],
        out_specs=[VMEM, VMEM],
        out_shape=[
            jax.ShapeDtypeStruct((2048, 128), I16),
            jax.ShapeDtypeStruct((48, 128), F32),
        ],
        scratch_shapes=[pltpu.VMEM((RANK, 4 * BLOCK), F32)],
        compiler_params=pltpu.CompilerParams(vmem_limit_bytes=LIMIT),
        cost_estimate=pl.CostEstimate(
            flops=2 * 192 * 128 * 768, bytes_accessed=6000000, transcendentals=0
        ),
    )(place.reshape(1), core.reshape(1), cq_all, attn_out, power_t, error, came)


def sum_kernel(in_ref, grad_ref, expert_ref, out_ref, tiles_ref, sem):
    del grad_ref, expert_ref
    copies = []
    for i in range(4):
        here = pl.ds(512 * i, 512)
        copies.append(pltpu.make_async_copy(in_ref.at[here, :], tiles_ref.at[here, :], sem.at[i]))
        copies[-1].start()

    def step(i, total):
        at = pl.multiple_of(i * 64, 64)
        parts = [decoded(tiles_ref[pl.ds(at + 16 * j, 16), :]) for j in range(4)]
        return total + ((parts[0] + parts[1]) + (parts[2] + parts[3]))

    total = jnp.zeros((16, 128), F32)
    for i in range(4):
        copies[i].wait()
        total = lax.fori_loop(8 * i, 8 * i + 8, step, total, unroll=4)
    total = total[:8] + total[8:]
    used = lanes_of((8, 128)) < USED
    largest = jnp.max(jnp.where(used, jnp.abs(total), 0.0), axis=1, keepdims=True)
    exponent, factor = scale_of(largest)
    tile = jnp.where(used, total * factor, exponent)
    tile = coded(jnp.concatenate([tile, tile], axis=0))
    out_ref[...] = jnp.broadcast_to(tile[None], (128, 16, 128)).reshape(2048, 128)


def summed(received, *others):
    return pl.pallas_call(
        sum_kernel,
        in_specs=[ANY, ANY, ANY],
        out_specs=VMEM,
        out_shape=jax.ShapeDtypeStruct((2048, 128), I16),
        scratch_shapes=[pltpu.VMEM((2048, 128), I16), pltpu.SemaphoreType.DMA((4,))],
        compiler_params=pltpu.CompilerParams(vmem_limit_bytes=LIMIT),
        cost_estimate=pl.CostEstimate(flops=1000000, bytes_accessed=1500000, transcendentals=0),
    )(received, *others)


def grad_kernel(at_ref, own_ref, other_ref, cols_ref, error_ref, out_ref):
    step = pl.program_id(0)
    mine = lax.rem(step, 2) == at_ref[1]
    attn = jnp.where(mine, own_ref[0], other_ref[0])
    grad = lax.dot_general(
        attn, cols_ref[...], (((0,), (0,)), ((), ())), preferred_element_type=F32
    ) + error_ref[...].astype(F32)
    high = grad.astype(BF16)
    out_ref[:, :128] = high
    out_ref[:, 128:] = (grad - high.astype(F32)).astype(BF16)


def grad_of(place, core, own, other, out_cols, error):
    def slot(i, at):
        apart = lax.bitwise_xor(at[0], i // 2)
        return (lax.rem(apart, 2) * 2 + apart // 2, 0, 0)

    return pl.pallas_call(
        grad_kernel,
        grid_spec=pltpu.PrefetchScalarGridSpec(
            num_scalar_prefetch=1,
            grid=(8,),
            in_specs=[
                pl.BlockSpec((1, 128, BLOCK), slot),
                pl.BlockSpec((1, 128, BLOCK), slot),
                pl.BlockSpec((128, 128), lambda i, at: (0, 0)),
                pl.BlockSpec((BLOCK, 128), lambda i, at: (i, 0)),
            ],
            out_specs=pl.BlockSpec((BLOCK, 256), lambda i, at: (i, 0)),
        ),
        out_shape=jax.ShapeDtypeStruct((WIDTH, 256), BF16),
        compiler_params=pltpu.CompilerParams(vmem_limit_bytes=LIMIT),
        cost_estimate=pl.CostEstimate(
            flops=2 * 128 * 128 * WIDTH, bytes_accessed=WIDTH * 1024, transcendentals=0
        ),
    )(jnp.stack([place, core]), own, other, out_cols, error)


def unpacked(ref, p_ref):
    lane = lanes_of((16, 128))
    for pair in range(4):
        for group in range(8):
            first, second = [], []
            for band in (2 * pair, 2 * pair + 1):
                at = (band * 32 + group * 4) * 8
                first.append(decoded(ref[at : at + 16, :]))
                second.append(decoded(ref[at + 16 : at + 32, :]))
            a = jnp.concatenate([t[:8] for t in first], axis=0)
            b = jnp.concatenate([t[8:] for t in first], axis=0)
            c = jnp.concatenate([t[:8] for t in second], axis=0)
            tail = jnp.concatenate([t[8:] for t in second], axis=0)
            for j, (tile, shift) in enumerate(((a, 96), (b, 64), (c, 32))):
                tile = jnp.where(lane < USED, tile, pltpu.roll(tail, shift, 1))
                place = group * 3 + j
                lanes = slice(128 * (place % 2), 128 * (place % 2) + 128)
                high = tile.astype(BF16)
                low = (tile - high.astype(F32)).astype(BF16)
                p_ref[place // 2, pair * 16 : pair * 16 + 16, lanes] = high
                p_ref[place // 2, RANK + pair * 16 : RANK + pair * 16 + 16, lanes] = low


def rows_of(i, core):
    return pl.ds(pl.multiple_of((2 * (i // 3) + core) * BLOCK + (i % 3) * 256, 256), 256)


def product(p_ref, grad_ref, core):
    total = jnp.zeros((128, 256), F32)
    for i in range(12):
        total += jnp.dot(p_ref[i], grad_ref[rows_of(i, core), :], preferred_element_type=F32)
    total = total[:RANK] + total[RANK:]
    return total[:, :128] + total[:, 128:]


def squared(p_ref):
    total = jnp.zeros((128, 128), F32)
    for i in range(12):
        total += lax.dot_general(
            p_ref[i], p_ref[i], (((1,), (1,)), ((), ())), preferred_element_type=F32
        )
    total = total[:RANK] + total[RANK:]
    return total[:, :RANK] + total[:, RANK:]


def mine_kernel(core_ref, codes_ref, grad_ref, raw_ref, square_ref, p_ref):
    unpacked(codes_ref, p_ref)
    raw_ref[...] = product(p_ref, grad_ref, core_ref[0])
    square_ref[...] = squared(p_ref)


def other_kernel(
    core_ref, codes_ref, grad_ref, mine_ref, square_ref, expert_ref, out_ref, gram_ref, p_ref
):
    unpacked(codes_ref, p_ref)
    gram_ref[...] = square_ref[...] + squared(p_ref)
    codes, scales = packed(mine_ref[...] + product(p_ref, grad_ref, 1 - core_ref[0]))
    codes = coded(codes)
    blank = jnp.zeros((7, 128), F32)
    for i in range(8):
        rest = jnp.concatenate([tagged(expert_ref[i]), scales, blank], axis=0)
        out_ref[i, :RANK, :] = codes
        out_ref[i, RANK:, :] = coded(rest)


SQUARE = jax.ShapeDtypeStruct((RANK, RANK), F32)
MESSAGE = jax.ShapeDtypeStruct((8, RANK + 16, 128), I16)
HALF = jax.ShapeDtypeStruct((12, 128, 256), BF16)
HALF_COST = pl.CostEstimate(flops=2 * 128 * 256 * 3072, bytes_accessed=3000000, transcendentals=0)


def mine_of(core, codes, grad):
    return pl.pallas_call(
        mine_kernel,
        in_specs=[SMEM, VMEM, VMEM],
        out_specs=[VMEM, VMEM, VMEM],
        out_shape=[jax.ShapeDtypeStruct((RANK, 128), F32), SQUARE, HALF],
        compiler_params=pltpu.CompilerParams(vmem_limit_bytes=LIMIT),
        cost_estimate=HALF_COST,
    )(core.reshape(1), codes, grad)


def other_of(core, codes, grad, raw, square, by_y):
    return pl.pallas_call(
        other_kernel,
        in_specs=[SMEM, VMEM, VMEM, VMEM, VMEM, VMEM],
        out_specs=[VMEM, VMEM, VMEM],
        out_shape=[MESSAGE, SQUARE, HALF],
        compiler_params=pltpu.CompilerParams(vmem_limit_bytes=LIMIT),
        cost_estimate=HALF_COST,
    )(core.reshape(1), codes, grad, raw, square, by_y)


def pass_kernel(in_ref, out_ref):
    raw, rows = collected(in_ref)
    codes, scales = packed(raw)
    codes = coded(codes)
    rows = tagged(rows)
    blank = jnp.zeros((7, 128), F32)
    for i in range(8):
        mine = jnp.broadcast_to(rows[i : i + 1], (8, 128))
        out_ref[i, :RANK, :] = codes
        out_ref[i, RANK:, :] = coded(jnp.concatenate([mine, scales, blank], axis=0))


def passed(received):
    return pl.pallas_call(
        pass_kernel,
        in_specs=[VMEM],
        out_specs=VMEM,
        out_shape=MESSAGE,
        compiler_params=pltpu.CompilerParams(vmem_limit_bytes=LIMIT),
    )(received)


def final_kernel(
    at_ref, inverse_ref, sums_ref, mine_ref, other_ref, grad_ref,
    approx_ref, q_ref, error_ref, expert_ref, full_ref,
):
    raw, rows = collected(sums_ref)
    expert_ref[...] = rows[:1, :USED]
    inverse = inverse_ref[...]
    q_t = jnp.dot(inverse, raw, precision=HIGH) * (1.0 / 64.0)
    q_ref[...] = q_t
    weights = jnp.dot(inverse.T, q_t, precision=HIGH)
    high = weights.astype(BF16)
    low = (weights - high.astype(F32)).astype(BF16)
    both = jnp.concatenate([high, low], axis=1)
    both = jnp.concatenate([both, both], axis=0)
    for ref, core in ((mine_ref, at_ref[1]), (other_ref, 1 - at_ref[1])):
        for i in range(12):
            rows = rows_of(i, core)
            part = lax.dot_general(
                ref[i], both, (((0,), (0,)), ((), ())), preferred_element_type=F32
            )
            part = part[:, :128] + part[:, 128:]
            full_ref[rows, :] = part
            grad = grad_ref[rows, :].astype(F32)
            error_ref[rows, :] = (grad[:, :128] + grad[:, 128:] - part).astype(BF16)
    here = pl.ds(pl.multiple_of(at_ref[0] * 96, 32), 96)
    approx_ref[...] = full_ref[here, :].astype(BF16)


def final_of(data, core, inverse, sums, p_mine, p_other, grad):
    return pl.pallas_call(
        final_kernel,
        in_specs=[SMEM, VMEM, VMEM, VMEM, VMEM, VMEM],
        out_specs=[VMEM] * 4,
        out_shape=[
            jax.ShapeDtypeStruct((96, 128), BF16),
            jax.ShapeDtypeStruct((RANK, 128), F32),
            jax.ShapeDtypeStruct((WIDTH, 128), BF16),
            jax.ShapeDtypeStruct((1, USED), F32),
        ],
        scratch_shapes=[pltpu.VMEM((WIDTH, 128), F32)],
        compiler_params=pltpu.CompilerParams(vmem_limit_bytes=LIMIT),
    )(jnp.stack([data, core]), inverse, sums, p_mine, p_other, grad)


def first_kernel(
    q_ref, cols_ref, tokens_ref, routes_ref, logits_ref, score_ref, out_ref, expert_ref
):
    part = folded(
        lax.dot_general(
            three(q_ref[...]), cols_ref[...], (((1,), (1,)), ((), ())), preferred_element_type=F32
        )
    )
    first = 1.0 / (1.0 + jnp.exp(logits_ref[1:2, :] - logits_ref[0:1, :]))
    rows = first * (1.0 - first) * (score_ref[0:1, :] - score_ref[1:2, :])
    rows = jnp.broadcast_to(rows, (8, 128))
    label = lax.broadcasted_iota(jnp.int32, (8, 128), 0)
    spread = jnp.where(routes_ref[0:1, :] == label, rows, 0.0) - jnp.where(
        routes_ref[1:2, :] == label, rows, 0.0
    )
    experts = jnp.dot(spread.astype(BF16), tokens_ref[...], preferred_element_type=F32)
    for t in range(48):
        expert_ref[:, t, :] = experts[:, t * 128 : t * 128 + 128]
    blank = jnp.zeros((15, 128), F32)
    for i in range(8):
        codes, scales = packed(jnp.concatenate([part, expert_ref[i]], axis=0))
        out_ref[i, : RANK + 48, :] = coded(codes)
        out_ref[i, RANK + 48 :, :] = coded(jnp.concatenate([scales, blank], axis=0))


def first_of(power_t, out_cols, tokens, routes_t, logits_t, score_t):
    def whole(*shape):
        return pl.BlockSpec(shape, lambda i: (0,) * len(shape))

    return pl.pallas_call(
        first_kernel,
        grid=(1,),
        in_specs=[
            whole(RANK, 128),
            whole(128, 128),
            whole(128, WIDTH),
            whole(2, 128),
            whole(2, 128),
            whole(2, 128),
        ],
        out_specs=whole(8, RANK + 64, 128),
        out_shape=jax.ShapeDtypeStruct((8, RANK + 64, 128), I16),
        scratch_shapes=[pltpu.VMEM((8, 48, 128), F32)],
        compiler_params=pltpu.CompilerParams(vmem_limit_bytes=MOST),
    )(power_t, out_cols, tokens, routes_t, logits_t, score_t)


def local(attn_out, out_cols, error_in, power_q, tokens, routes, route_logits, pair_score):
    error = error_in[0]
    core = lax.axis_index("c").astype(jnp.int32)
    place = lax.axis_index("l").astype(jnp.int32)
    data = (lax.axis_index("x") * 8 + lax.axis_index("y")) * 2 + lax.axis_index("h")
    power_t = power_q.T

    first = first_of(power_t, out_cols, tokens, routes.T, route_logits.T, pair_score.T)
    cq_all = exchange(first, EXPERT)

    given, attn_here = error_share(power_t, error, 1 - core, attn_out, first)
    came = swap_cores(given)
    across = lax.ppermute(attn_here, "l", [(i, i ^ 2) for i in range(4)])
    pair = jnp.stack([attn_here, across])
    beside = lax.ppermute(pair, "l", [(i, i ^ 1) for i in range(4)])
    own = jnp.concatenate([pair, beside])
    codes, experts = share_of(place, core, cq_all, attn_out, power_t, error, came)
    by_y = experts.reshape(4, 8, 2, 96).transpose(1, 0, 2, 3).reshape(8, 8, 96)
    by_y = jnp.pad(by_y, ((0, 0), (0, 0), (0, 32)))
    grad = grad_of(place, core, own, swap_cores(own), out_cols, error)
    piece = summed(exchange(codes.reshape(256, 8, 128), FLAT).reshape(2048, 128), grad, by_y)
    mine = exchange(piece.reshape(256, 8, 128), FLAT).reshape(2048, 128)
    other = swap_cores(mine)
    raw, square, p_mine = mine_of(core, mine, grad)
    send, gram, p_other = other_of(core, other, grad, raw, square, by_y)

    sums = exchange(passed(exchange(send, "y")), ("x", "h"))

    factor = jnp.linalg.cholesky(gram, symmetrize_input=False)
    inverse = lax.linalg.triangular_solve(
        factor, jnp.eye(RANK, dtype=F32), left_side=True, lower=True
    )
    approx, q_t, error_out, expert_grad = final_of(
        data.astype(jnp.int32), core, inverse, sums, p_mine, p_other, grad
    )
    return approx, q_t.T, error_out[None], expert_grad


def solution(mesh):
    fine = Mesh(mesh.devices.reshape(4, 8, 2, 4, 2), DP + EXPERT)
    everyone = P(DP + EXPERT, None)
    return jax.shard_map(
        local,
        mesh=fine,
        in_specs=(
            P(DP, EXPERT),
            P(DP, EXPERT),
            P(DP, None, EXPERT),
            P(EXPERT, None),
            everyone,
            everyone,
            everyone,
            everyone,
        ),
        out_specs=(P(DP, EXPERT), P(EXPERT, None), P(DP, None, EXPERT), P(EXPERT, DP)),
        check_vma=False,
    )
```

```python
import functools

import jax
import jax.numpy as jnp
from jax import lax
from jax.experimental import pallas as pl
from jax.experimental.pallas import tpu as pltpu
from jax.sharding import Mesh, PartitionSpec as P

HIGH = lax.Precision.HIGHEST
F32, BF16, I16 = jnp.float32, jnp.bfloat16, jnp.int16
RANK = 64
WIDTH = 6144
BLOCK = 768
DP = ("x", "y", "h")
EXPERT = ("l", "c")
FLAT = ("x", "y", "h", "l")
LIMIT = 12 * 1024 * 1024
MOST = 60 * 1024 * 1024
TOP = 32000.0
STEP = 64.0
USED = 96

VMEM = pl.BlockSpec(memory_space=pltpu.VMEM)
SMEM = pl.BlockSpec(memory_space=pltpu.SMEM)
ANY = pl.BlockSpec(memory_space=pl.ANY)


def exchange(values, axes):
    return lax.all_to_all(values, axes, split_axis=0, concat_axis=0, tiled=True)


def swap_cores(values):
    return lax.ppermute(values, "c", [(0, 1), (1, 0)])


def three(values):
    high = values.astype(BF16)
    rest = values - high.astype(F32)
    middle = rest.astype(BF16)
    low = (rest - middle.astype(F32)).astype(BF16)
    return jnp.concatenate([high, middle, low], axis=0)


def folded(stacked):
    return stacked[:RANK] + stacked[RANK : 2 * RANK] + stacked[2 * RANK :]


def scale_of(largest):
    exponent = jnp.ceil(STEP * jnp.log2(jnp.maximum(largest, 1e-30))) + 1.0
    return exponent, jnp.exp2(exponent * (-1.0 / STEP)) * TOP


def lanes_of(shape):
    return lax.broadcasted_iota(jnp.int32, shape, 1)


def coded(values):
    return jnp.round(values).astype(jnp.int32).astype(I16)


def decoded(tile):
    wide = tile.astype(jnp.int32).astype(F32)
    return wide * (jnp.exp2(wide[:, 127:128] * (1.0 / STEP)) * (1.0 / TOP))


def eye_of(rows):
    shape = (rows, 128)
    return lax.broadcasted_iota(jnp.int32, shape, 0) == lax.broadcasted_iota(jnp.int32, shape, 1)


def packed(rows):
    exponent, factor = scale_of(jnp.max(jnp.abs(rows), axis=1, keepdims=True))
    eye = eye_of(rows.shape[0])
    return rows * factor, jnp.sum(jnp.where(eye, exponent, 0.0), axis=0, keepdims=True)


def unscaled(codes, row):
    exponent = jnp.sum(jnp.where(eye_of(codes.shape[0]), row, 0.0), axis=1, keepdims=True)
    return codes * (jnp.exp2(exponent * (1.0 / STEP)) * (1.0 / TOP))


def floats(codes):
    return codes.astype(jnp.int32).astype(F32)


def tagged(rows):
    used = lanes_of(rows.shape) < USED
    rows = jnp.where(used, rows, 0.0)
    exponent, factor = scale_of(jnp.max(jnp.abs(rows), axis=1, keepdims=True))
    return jnp.where(used, rows * factor, exponent)


def collected(ref):
    raw = jnp.zeros((RANK, 128), F32)
    rows = jnp.zeros((8, 128), F32)
    for i in range(8):
        rest = floats(ref[i, RANK:, :])
        raw += unscaled(floats(ref[i, :RANK, :]), rest[8:9])
        rows += rest[:8] * (jnp.exp2(rest[:8, 127:128] * (1.0 / STEP)) * (1.0 / TOP))
    return raw, rows


def error_kernel(block_ref, q_ref, error_ref, attn_ref, other_ref, out_ref, pass_ref):
    del block_ref, other_ref
    pass_ref[...] = attn_ref[...]
    out_ref[...] = folded(
        lax.dot_general(
            three(q_ref[...]), error_ref[...], (((1,), (1,)), ((), ())), preferred_element_type=F32
        )
    )


def error_share(power_t, error, core, attn_out, other):
    return pl.pallas_call(
        error_kernel,
        grid_spec=pltpu.PrefetchScalarGridSpec(
            num_scalar_prefetch=1,
            grid=(4,),
            in_specs=[
                pl.BlockSpec((RANK, 128), lambda i, core: (0, 0)),
                pl.BlockSpec((BLOCK, 128), lambda i, core: (2 * i + core[0], 0)),
                pl.BlockSpec((32, BLOCK), lambda i, core: (i, 0)),
                ANY,
            ],
            out_specs=[
                pl.BlockSpec((RANK, BLOCK), lambda i, core: (0, i)),
                pl.BlockSpec((32, BLOCK), lambda i, core: (i, 0)),
            ],
        ),
        out_shape=[
            jax.ShapeDtypeStruct((RANK, 4 * BLOCK), F32),
            jax.ShapeDtypeStruct((128, BLOCK), BF16),
        ],
        compiler_params=pltpu.CompilerParams(vmem_limit_bytes=LIMIT),
        cost_estimate=pl.CostEstimate(
            flops=2 * 192 * 128 * 3072, bytes_accessed=3072 * 512, transcendentals=0
        ),
    )(core.reshape(1), power_t, error, attn_out, other)


def share_kernel(place_ref, cq_ref, attn_ref, kept_ref, came_ref, out_ref, expert_ref, half_ref):
    total = jnp.zeros((RANK + 48, 128), F32)
    for i in range(8):
        total += unscaled(
            floats(cq_ref[i, : RANK + 48, :]), floats(cq_ref[i, RANK + 48 :, :])[:1]
        )
    expert_ref[...] = total[RANK:]
    from_attn = folded(jnp.dot(three(total[:RANK]), attn_ref[...], preferred_element_type=F32))
    half_ref[...] = kept_ref[...] + came_ref[...]
    here = pl.ds(pl.multiple_of(place_ref[0] * BLOCK, BLOCK), BLOCK)
    half_ref[:, here] += from_attn
    lane = lanes_of((8, 128))
    for band in range(8):
        rows = slice(band * 8, band * 8 + 8)
        tiles = [half_ref[rows, t * 128 : t * 128 + 128] for t in range(24)]
        largest = functools.reduce(jnp.maximum, [jnp.abs(t) for t in tiles])
        exponent, factor = scale_of(jnp.max(largest, axis=1, keepdims=True))
        exponent = jnp.broadcast_to(exponent, (8, 128))
        factor = jnp.broadcast_to(factor, (8, 128))
        for group in range(8):
            a, b, c = (t * factor for t in tiles[group * 3 : group * 3 + 3])
            tail = jnp.where(
                lane < 32,
                pltpu.roll(a, 32, 1),
                jnp.where(lane < 64, pltpu.roll(b, 64, 1), pltpu.roll(c, 96, 1)),
            )
            a, b, c, tail = (jnp.where(lane < USED, t, exponent) for t in (a, b, c, tail))
            at = (band * 32 + group * 4) * 8
            out_ref[at : at + 16, :] = coded(jnp.concatenate([a, b], axis=0))
            out_ref[at + 16 : at + 32, :] = coded(jnp.concatenate([c, tail], axis=0))


def share_of(place, cq_all, attn_out, kept, came):
    return pl.pallas_call(
        share_kernel,
        in_specs=[SMEM, VMEM, VMEM, VMEM, VMEM],
        out_specs=[VMEM, VMEM],
        out_shape=[
            jax.ShapeDtypeStruct((2048, 128), I16),
            jax.ShapeDtypeStruct((48, 128), F32),
        ],
        scratch_shapes=[pltpu.VMEM((RANK, 4 * BLOCK), F32)],
        compiler_params=pltpu.CompilerParams(vmem_limit_bytes=LIMIT),
        cost_estimate=pl.CostEstimate(
            flops=2 * 192 * 128 * 768, bytes_accessed=6000000, transcendentals=0
        ),
    )(place.reshape(1), cq_all, attn_out, kept, came)


def sum_kernel(in_ref, grad_ref, expert_ref, out_ref, tiles_ref, sem):
    del grad_ref, expert_ref
    copies = []
    for i in range(4):
        here = pl.ds(512 * i, 512)
        copies.append(pltpu.make_async_copy(in_ref.at[here, :], tiles_ref.at[here, :], sem.at[i]))
        copies[-1].start()

    def step(i, total):
        at = pl.multiple_of(i * 64, 64)
        parts = [decoded(tiles_ref[pl.ds(at + 16 * j, 16), :]) for j in range(4)]
        return total + ((parts[0] + parts[1]) + (parts[2] + parts[3]))

    total = jnp.zeros((16, 128), F32)
    for i in range(4):
        copies[i].wait()
        total = lax.fori_loop(8 * i, 8 * i + 8, step, total, unroll=4)
    total = total[:8] + total[8:]
    used = lanes_of((8, 128)) < USED
    largest = jnp.max(jnp.where(used, jnp.abs(total), 0.0), axis=1, keepdims=True)
    exponent, factor = scale_of(largest)
    tile = jnp.where(used, total * factor, exponent)
    tile = coded(jnp.concatenate([tile, tile], axis=0))
    out_ref[...] = jnp.broadcast_to(tile[None], (128, 16, 128)).reshape(2048, 128)


def summed(received, *others):
    return pl.pallas_call(
        sum_kernel,
        in_specs=[ANY, ANY, ANY],
        out_specs=VMEM,
        out_shape=jax.ShapeDtypeStruct((2048, 128), I16),
        scratch_shapes=[pltpu.VMEM((2048, 128), I16), pltpu.SemaphoreType.DMA((4,))],
        compiler_params=pltpu.CompilerParams(vmem_limit_bytes=LIMIT),
        cost_estimate=pl.CostEstimate(flops=1000000, bytes_accessed=1500000, transcendentals=0),
    )(received, *others)


def grad_kernel(at_ref, own_ref, other_ref, cols_ref, error_ref, out_ref):
    step = pl.program_id(0)
    mine = lax.rem(step, 2) == at_ref[1]
    attn = jnp.where(mine, own_ref[0], other_ref[0])
    grad = lax.dot_general(
        attn, cols_ref[...], (((0,), (0,)), ((), ())), preferred_element_type=F32
    ) + error_ref[...].astype(F32)
    high = grad.astype(BF16)
    out_ref[:, :128] = high
    out_ref[:, 128:] = (grad - high.astype(F32)).astype(BF16)


def grad_of(place, core, own, other, out_cols, error):
    def slot(i, at):
        return (lax.rem(at[0] + 4 - i // 2, 4), 0, 0)

    return pl.pallas_call(
        grad_kernel,
        grid_spec=pltpu.PrefetchScalarGridSpec(
            num_scalar_prefetch=1,
            grid=(8,),
            in_specs=[
                pl.BlockSpec((1, 128, BLOCK), slot),
                pl.BlockSpec((1, 128, BLOCK), slot),
                pl.BlockSpec((128, 128), lambda i, at: (0, 0)),
                pl.BlockSpec((BLOCK, 128), lambda i, at: (i, 0)),
            ],
            out_specs=pl.BlockSpec((BLOCK, 256), lambda i, at: (i, 0)),
        ),
        out_shape=jax.ShapeDtypeStruct((WIDTH, 256), BF16),
        compiler_params=pltpu.CompilerParams(vmem_limit_bytes=LIMIT),
        cost_estimate=pl.CostEstimate(
            flops=2 * 128 * 128 * WIDTH, bytes_accessed=WIDTH * 1024, transcendentals=0
        ),
    )(jnp.stack([place, core]), own, other, out_cols, error)


def unpacked(ref, p_ref):
    lane = lanes_of((16, 128))
    for pair in range(4):
        for group in range(8):
            first, second = [], []
            for band in (2 * pair, 2 * pair + 1):
                at = (band * 32 + group * 4) * 8
                first.append(decoded(ref[at : at + 16, :]))
                second.append(decoded(ref[at + 16 : at + 32, :]))
            a = jnp.concatenate([t[:8] for t in first], axis=0)
            b = jnp.concatenate([t[8:] for t in first], axis=0)
            c = jnp.concatenate([t[:8] for t in second], axis=0)
            tail = jnp.concatenate([t[8:] for t in second], axis=0)
            for j, (tile, shift) in enumerate(((a, 96), (b, 64), (c, 32))):
                tile = jnp.where(lane < USED, tile, pltpu.roll(tail, shift, 1))
                place = group * 3 + j
                lanes = slice(128 * (place % 2), 128 * (place % 2) + 128)
                high = tile.astype(BF16)
                low = (tile - high.astype(F32)).astype(BF16)
                p_ref[place // 2, pair * 16 : pair * 16 + 16, lanes] = high
                p_ref[place // 2, RANK + pair * 16 : RANK + pair * 16 + 16, lanes] = low


def rows_of(i, core):
    return pl.ds(pl.multiple_of((2 * (i // 3) + core) * BLOCK + (i % 3) * 256, 256), 256)


def product(p_ref, grad_ref, core):
    total = jnp.zeros((128, 256), F32)
    for i in range(12):
        total += jnp.dot(p_ref[i], grad_ref[rows_of(i, core), :], preferred_element_type=F32)
    total = total[:RANK] + total[RANK:]
    return total[:, :128] + total[:, 128:]


def squared(p_ref):
    total = jnp.zeros((128, 128), F32)
    for i in range(12):
        total += lax.dot_general(
            p_ref[i], p_ref[i], (((1,), (1,)), ((), ())), preferred_element_type=F32
        )
    total = total[:RANK] + total[RANK:]
    return total[:, :RANK] + total[:, RANK:]


def mine_kernel(core_ref, codes_ref, grad_ref, raw_ref, square_ref, p_ref):
    unpacked(codes_ref, p_ref)
    raw_ref[...] = product(p_ref, grad_ref, core_ref[0])
    square_ref[...] = squared(p_ref)


def other_kernel(
    core_ref, codes_ref, grad_ref, mine_ref, square_ref, expert_ref, out_ref, gram_ref, p_ref
):
    unpacked(codes_ref, p_ref)
    gram_ref[...] = square_ref[...] + squared(p_ref)
    codes, scales = packed(mine_ref[...] + product(p_ref, grad_ref, 1 - core_ref[0]))
    codes = coded(codes)
    blank = jnp.zeros((7, 128), F32)
    for i in range(8):
        rest = jnp.concatenate([tagged(expert_ref[i]), scales, blank], axis=0)
        out_ref[i, :RANK, :] = codes
        out_ref[i, RANK:, :] = coded(rest)


SQUARE = jax.ShapeDtypeStruct((RANK, RANK), F32)
MESSAGE = jax.ShapeDtypeStruct((8, RANK + 16, 128), I16)
HALF = jax.ShapeDtypeStruct((12, 128, 256), BF16)
HALF_COST = pl.CostEstimate(flops=2 * 128 * 256 * 3072, bytes_accessed=3000000, transcendentals=0)


def mine_of(core, codes, grad):
    return pl.pallas_call(
        mine_kernel,
        in_specs=[SMEM, VMEM, VMEM],
        out_specs=[VMEM, VMEM, VMEM],
        out_shape=[jax.ShapeDtypeStruct((RANK, 128), F32), SQUARE, HALF],
        compiler_params=pltpu.CompilerParams(vmem_limit_bytes=LIMIT),
        cost_estimate=HALF_COST,
    )(core.reshape(1), codes, grad)


def other_of(core, codes, grad, raw, square, by_y):
    return pl.pallas_call(
        other_kernel,
        in_specs=[SMEM, VMEM, VMEM, VMEM, VMEM, VMEM],
        out_specs=[VMEM, VMEM, VMEM],
        out_shape=[MESSAGE, SQUARE, HALF],
        compiler_params=pltpu.CompilerParams(vmem_limit_bytes=LIMIT),
        cost_estimate=HALF_COST,
    )(core.reshape(1), codes, grad, raw, square, by_y)


def after_kernel(in_ref, other_ref, out_ref):
    del in_ref, other_ref, out_ref


def after(values, other):
    return pl.pallas_call(
        after_kernel,
        in_specs=[ANY, ANY],
        out_specs=ANY,
        out_shape=jax.ShapeDtypeStruct(values.shape, values.dtype),
        input_output_aliases={0: 0},
        compiler_params=pltpu.CompilerParams(vmem_limit_bytes=1024 * 1024),
    )(values, other)


def pass_kernel(in_ref, out_ref):
    raw, rows = collected(in_ref)
    codes, scales = packed(raw)
    codes = coded(codes)
    rows = tagged(rows)
    blank = jnp.zeros((7, 128), F32)
    for i in range(8):
        mine = jnp.broadcast_to(rows[i : i + 1], (8, 128))
        out_ref[i, :RANK, :] = codes
        out_ref[i, RANK:, :] = coded(jnp.concatenate([mine, scales, blank], axis=0))


def passed(received):
    return pl.pallas_call(
        pass_kernel,
        in_specs=[VMEM],
        out_specs=VMEM,
        out_shape=MESSAGE,
        compiler_params=pltpu.CompilerParams(vmem_limit_bytes=LIMIT),
    )(received)


def final_kernel(
    at_ref, inverse_ref, sums_ref, mine_ref, other_ref, grad_ref,
    approx_ref, q_ref, error_ref, expert_ref, full_ref,
):
    raw, rows = collected(sums_ref)
    expert_ref[...] = rows[:1, :USED]
    inverse = inverse_ref[...]
    q_t = jnp.dot(inverse, raw, precision=HIGH) * (1.0 / 64.0)
    q_ref[...] = q_t
    weights = jnp.dot(inverse.T, q_t, precision=HIGH)
    high = weights.astype(BF16)
    low = (weights - high.astype(F32)).astype(BF16)
    both = jnp.concatenate([high, low], axis=1)
    both = jnp.concatenate([both, both], axis=0)
    for ref, core in ((mine_ref, at_ref[1]), (other_ref, 1 - at_ref[1])):
        for i in range(12):
            rows = rows_of(i, core)
            part = lax.dot_general(
                ref[i], both, (((0,), (0,)), ((), ())), preferred_element_type=F32
            )
            part = part[:, :128] + part[:, 128:]
            full_ref[rows, :] = part
            grad = grad_ref[rows, :].astype(F32)
            error_ref[rows, :] = (grad[:, :128] + grad[:, 128:] - part).astype(BF16)
    here = pl.ds(pl.multiple_of(at_ref[0] * 96, 32), 96)
    approx_ref[...] = full_ref[here, :].astype(BF16)


def final_of(data, core, inverse, sums, p_mine, p_other, grad):
    return pl.pallas_call(
        final_kernel,
        in_specs=[SMEM, VMEM, VMEM, VMEM, VMEM, VMEM],
        out_specs=[VMEM] * 4,
        out_shape=[
            jax.ShapeDtypeStruct((96, 128), BF16),
            jax.ShapeDtypeStruct((RANK, 128), F32),
            jax.ShapeDtypeStruct((WIDTH, 128), BF16),
            jax.ShapeDtypeStruct((1, USED), F32),
        ],
        scratch_shapes=[pltpu.VMEM((WIDTH, 128), F32)],
        compiler_params=pltpu.CompilerParams(vmem_limit_bytes=LIMIT),
    )(jnp.stack([data, core]), inverse, sums, p_mine, p_other, grad)


def first_kernel(
    q_ref, cols_ref, tokens_ref, routes_ref, logits_ref, score_ref, out_ref, expert_ref
):
    part = folded(
        lax.dot_general(
            three(q_ref[...]), cols_ref[...], (((1,), (1,)), ((), ())), preferred_element_type=F32
        )
    )
    first = 1.0 / (1.0 + jnp.exp(logits_ref[1:2, :] - logits_ref[0:1, :]))
    rows = first * (1.0 - first) * (score_ref[0:1, :] - score_ref[1:2, :])
    rows = jnp.broadcast_to(rows, (8, 128))
    label = lax.broadcasted_iota(jnp.int32, (8, 128), 0)
    spread = jnp.where(routes_ref[0:1, :] == label, rows, 0.0) - jnp.where(
        routes_ref[1:2, :] == label, rows, 0.0
    )
    experts = jnp.dot(spread.astype(BF16), tokens_ref[...], preferred_element_type=F32)
    for t in range(48):
        expert_ref[:, t, :] = experts[:, t * 128 : t * 128 + 128]
    blank = jnp.zeros((15, 128), F32)
    for i in range(8):
        codes, scales = packed(jnp.concatenate([part, expert_ref[i]], axis=0))
        out_ref[i, : RANK + 48, :] = coded(codes)
        out_ref[i, RANK + 48 :, :] = coded(jnp.concatenate([scales, blank], axis=0))


def first_of(power_t, out_cols, tokens, routes_t, logits_t, score_t):
    def whole(*shape):
        return pl.BlockSpec(shape, lambda i: (0,) * len(shape))

    return pl.pallas_call(
        first_kernel,
        grid=(1,),
        in_specs=[
            whole(RANK, 128),
            whole(128, 128),
            whole(128, WIDTH),
            whole(2, 128),
            whole(2, 128),
            whole(2, 128),
        ],
        out_specs=whole(8, RANK + 64, 128),
        out_shape=jax.ShapeDtypeStruct((8, RANK + 64, 128), I16),
        scratch_shapes=[pltpu.VMEM((8, 48, 128), F32)],
        compiler_params=pltpu.CompilerParams(vmem_limit_bytes=MOST),
    )(power_t, out_cols, tokens, routes_t, logits_t, score_t)


def local(attn_out, out_cols, error_in, power_q, tokens, routes, route_logits, pair_score):
    error = error_in[0]
    core = lax.axis_index("c").astype(jnp.int32)
    place = lax.axis_index("l").astype(jnp.int32)
    data = (lax.axis_index("x") * 8 + lax.axis_index("y")) * 2 + lax.axis_index("h")
    power_t = power_q.T

    first = first_of(power_t, out_cols, tokens, routes.T, route_logits.T, pair_score.T)
    cq_all = exchange(first, EXPERT)

    given, attn_first = error_share(power_t, error, 1 - core, attn_out, first)
    came = swap_cores(given)
    kept, attn_here = error_share(power_t, error, core, attn_first, first)
    shifted = [
        lax.ppermute(attn_here, "l", [(i, (i + k) % 4) for i in range(4)]) for k in (1, 2, 3)
    ]
    own = jnp.stack([attn_here, *shifted])
    codes, experts = share_of(place, cq_all, attn_out, kept, came)
    by_y = experts.reshape(4, 8, 2, 96).transpose(1, 0, 2, 3).reshape(8, 8, 96)
    by_y = jnp.pad(by_y, ((0, 0), (0, 0), (0, 32)))
    beside = swap_cores(own)
    piece = summed(exchange(codes.reshape(256, 8, 128), FLAT).reshape(2048, 128), beside, by_y)
    grad = grad_of(place, core, own, beside, out_cols, error)
    mine = exchange(piece.reshape(256, 8, 128), FLAT).reshape(2048, 128)
    mine = after(mine, grad)
    other = swap_cores(mine)
    raw, square, p_mine = mine_of(core, mine, grad)
    send, gram, p_other = other_of(core, other, grad, raw, square, by_y)

    sums = exchange(passed(exchange(send, "y")), ("x", "h"))

    factor = jnp.linalg.cholesky(gram, symmetrize_input=False)
    inverse = lax.linalg.triangular_solve(
        factor, jnp.eye(RANK, dtype=F32), left_side=True, lower=True
    )
    approx, q_t, error_out, expert_grad = final_of(
        data.astype(jnp.int32), core, inverse, sums, p_mine, p_other, grad
    )
    return approx, q_t.T, error_out[None], expert_grad


def solution(mesh):
    fine = Mesh(mesh.devices.reshape(4, 8, 2, 4, 2), DP + EXPERT)
    everyone = P(DP + EXPERT, None)
    return jax.shard_map(
        local,
        mesh=fine,
        in_specs=(
            P(DP, EXPERT),
            P(DP, EXPERT),
            P(DP, None, EXPERT),
            P(EXPERT, None),
            everyone,
            everyone,
            everyone,
            everyone,
        ),
        out_specs=(P(DP, EXPERT), P(EXPERT, None), P(DP, None, EXPERT), P(EXPERT, DP)),
        check_vma=False,
    )
```
